32 devices in a mesh: dp: 4 (over x, core), expert: 8 (over z, y).
Axes of the slice: x: 2, y: 2, z: 4, core: 2. Of those that a mesh axis runs over, the one named last changes fastest.
Arguments:
- tokens: bfloat16 [1024, 2048], P('expert', 'dp'), may hold values from -6 to 6
- cotangent: bfloat16 [1024, 2048], P('expert', 'dp'), may hold values from -3 to 3
- expert_ids: int32 [1024, 1], P('expert'), may hold values from 0 to 7; in each aligned block of 128 rows (0 to 127, 128 to 255, ...) at most 16 rows name the same one
- route_weights: float32 [1024, 1], P('expert'), may hold values from 0.2 to 1
- gate_weight: bfloat16 [8, 2048, 1408], P('expert', 'dp'), may hold values from -0.125 to 0.125
- up_weight: bfloat16 [8, 2048, 1408], P('expert', 'dp'), may hold values from -0.125 to 0.125
- down_weight: bfloat16 [8, 1408, 2048], P('expert', None, 'dp'), may hold values from -0.15625 to 0.15625
Outputs:
- token_grad: bfloat16 [1024, 2048], P('expert', 'dp')
- gate_grad: float32 [8, 2048, 1408], P('expert', 'dp')
- up_grad: float32 [8, 2048, 1408], P('expert', 'dp')
- down_grad: float32 [8, 1408, 2048], P('expert', None, 'dp')
The draws below stay inside these ranges and needn't reach their ends.
Inputs may be any that keep to these rules, and one draw needn't show every extreme that they name: `expert_ids`: each row names 1 different experts. Among the rows of one device no expert is named more than 16 times, a bound that some block reaches in some devices' rows.
All inputs are finite; a program needn't handle non-finite values.
Results may differ from the reference program's by a relative error of at most 0.0057.
Values may be sent and summed in bfloat16 or wider, within the bound.
No kernel may reach another device: no remote copies, remote signals or barrier semaphores. Data moves between devices by JAX's collectives and lax.ppermute only.
A program may use at most 64 MiB of HBM per device.

```python
import math
import jax
import jax.numpy as jnp
import numpy as np
from jax import lax

D = 2048
FF = 1408
TOP = 1
TOK_DEV = 128
EXPERTS = 8
CAP = 16
SLOTS = 128
TOKENS = 1024
N_EXPERT = 8


def levels(rng, extent, cuts, least, largest):
    gain = 1.0
    for axis_at, blocks in cuts:
        heights = jax.random.uniform(jax.random.fold_in(jax.random.fold_in(rng, 6), axis_at), (blocks,), jnp.float32, least / len(cuts), largest / len(cuts))
        gain = gain * jnp.repeat(jnp.exp(heights), extent[axis_at] // blocks).reshape((-1,) + (1,) * (len(extent) - 1 - axis_at))
    return gain


def deal_out(rng, own, number, rows, number_of, top, reach, slope):
    order = jax.random.permutation(rng, number_of)
    heavy_load, common = shares(number_of, rows * top, reach, slope, True), shares(number_of, rows * top, reach, slope, False)
    places = jnp.arange(number_of)

    def named(tallies, rotation):
        used = int((tallies > 0).sum())
        fixed = max(1, used // 4)
        passed = fixed + (places - fixed + rotation * (used - fixed)) % max(1, number_of - fixed)
        return jnp.zeros((number_of,), jnp.int32).at[order[jnp.where(places < fixed, places, passed)]].set(jnp.asarray(tallies, jnp.int32))

    tallies = jnp.where(number % 4 == 0, named(heavy_load, number // 4), named(common, number - number // 4 - 1))
    mixed = jax.random.permutation(jax.random.fold_in(own, 3), number_of)
    source_of, sink = mixed[0:number_of // 2 * 2:2], mixed[1:number_of // 2 * 2:2]
    slack = jnp.minimum(tallies[source_of] - 1, reach - tallies[sink]) // 2
    slack = jnp.where((source_of == order[0]) | (sink == order[0]) | (tallies[sink] == 0), 0, jnp.maximum(slack, 0))
    passed = jax.random.randint(jax.random.fold_in(own, 4), (number_of // 2,), 0, 1 << 20) % (slack + 1)
    tallies = tallies.at[source_of].add(-passed).at[sink].add(passed)
    labels = jnp.searchsorted(jnp.cumsum(tallies), jnp.arange(rows * top), side="right").astype(jnp.int32)
    grid = labels.reshape(top, rows).T
    grid = grid[jax.random.permutation(jax.random.fold_in(own, 1), rows)]
    rotation = jax.random.randint(jax.random.fold_in(own, 2), (rows, 1), 0, top)
    return jnp.take_along_axis(grid, (jnp.arange(top)[None, :] + rotation) % top, axis=1)


def shares(count, total, bound, skew, full):
    weights = [(1 << 20) // math.isqrt(standing ** skew) + 1 for standing in range(1, count + 1)]
    largest = bound if full else min(bound, max(-(-total // count), total * weights[0] // sum(weights)))
    least = 1 if total - largest >= count - 1 else 0
    counts, rest = [largest] + [least] * (count - 1), total - largest - least * (count - 1)
    while rest > 0:
        free = [i for i in range(1, count) if counts[i] < largest] or [i for i in range(1, count) if counts[i] < bound]
        pool, budget = sum([weights[i] for i in free]), rest
        for i in free:
            addition = min(bound - counts[i], max(1, budget * weights[i] // pool), rest)
            counts[i] = counts[i] + addition
            rest = rest - addition
    return np.array(counts)


def centred(own_key, dims, scale, most, split=(), kind=jnp.bfloat16):
    values = scale * jax.random.normal(own_key, dims, jnp.float32)
    if split:
        values = values * levels(own_key, dims, split, -0.22, 0.18)
    return jnp.clip(values, -most, most).astype(kind)


def setup_inputs(seed: int = 0) -> dict:
    seeds = jax.random.split(jax.random.key(seed), 8)
    tokens = centred(seeds[0], (TOKENS, D), 1.0, 6.0, ((0, 8), (1, 4)))
    cotangent = centred(seeds[1], (TOKENS, D), 0.5, 3.0, ((0, 8), (1, 4)))
    expert_ids_keys = jax.random.split(jax.random.fold_in(seeds[2], 1), TOKENS // TOK_DEV)
    expert_ids_turns = jax.random.permutation(jax.random.fold_in(seeds[2], 3), TOKENS // TOK_DEV)
    expert_ids = jax.vmap(lambda own, number: deal_out(jax.random.fold_in(seeds[2], 2), own, number, TOK_DEV, EXPERTS, TOP, CAP, 2))(expert_ids_keys, expert_ids_turns).reshape((TOKENS, TOP))
    route_weights = jnp.clip(0.2 + 0.8 * jax.random.uniform(seeds[3], (TOKENS, TOP), jnp.float32) ** levels(seeds[3], (TOKENS, TOP), ((0, 8),), -0.2, 0.2), 0.2, 1.0)
    gate_weight = centred(seeds[4], (EXPERTS, D, FF), D ** -0.5, 0.125, ((0, 8), (1, 4)))
    up_weight = centred(seeds[5], (EXPERTS, D, FF), D ** -0.5, 0.125, ((0, 8), (1, 4)))
    down_weight = centred(seeds[6], (EXPERTS, FF, D), FF ** -0.5, 0.15625, ((0, 8), (2, 4)))
    return dict(tokens=tokens, cotangent=cotangent, expert_ids=expert_ids, route_weights=route_weights, gate_weight=gate_weight, up_weight=up_weight, down_weight=down_weight)


def slot_index(expert_ids):
    pairs = expert_ids.reshape(N_EXPERT, TOK_DEV * TOP)
    position = jnp.arange(TOK_DEV * TOP, dtype=jnp.int32)
    earlier = (pairs[:, :, None] == pairs[:, None, :]) & (position[None, None, :] < position[None, :, None])
    rank_pos = jnp.sum(earlier.astype(jnp.int32), axis=2)
    source = jnp.arange(N_EXPERT, dtype=jnp.int32)[:, None]
    destination = pairs * SLOTS + source * CAP + rank_pos
    return destination.reshape(-1).astype(jnp.int32)


def expert_step(operands):
    slot_tokens, slot_cot, w_gate, w_up, w_down = operands
    gate_pre = jnp.dot(slot_tokens, w_gate, preferred_element_type=jnp.float32)
    up_pre = jnp.dot(slot_tokens, w_up, preferred_element_type=jnp.float32)
    hidden_grad = jnp.dot(slot_cot, w_down.T, preferred_element_type=jnp.float32)
    sigma = jax.nn.sigmoid(gate_pre)
    activated = gate_pre * sigma
    hidden = (activated * up_pre).astype(jnp.bfloat16)
    gate_delta = (hidden_grad * up_pre * sigma * (1.0 + gate_pre * (1.0 - sigma))).astype(jnp.bfloat16)
    up_delta = (hidden_grad * activated).astype(jnp.bfloat16)
    gate_part = jnp.dot(slot_tokens.T, gate_delta, preferred_element_type=jnp.float32)
    up_part = jnp.dot(slot_tokens.T, up_delta, preferred_element_type=jnp.float32)
    down_part = jnp.dot(hidden.T, slot_cot, preferred_element_type=jnp.float32)
    slot_grad = (jnp.dot(gate_delta, w_gate.T, preferred_element_type=jnp.float32)
                 + jnp.dot(up_delta, w_up.T, preferred_element_type=jnp.float32)).astype(jnp.bfloat16)
    return gate_part, up_part, down_part, slot_grad


def reference(tokens, cotangent, expert_ids, route_weights, gate_weight, up_weight, down_weight):
    destination = slot_index(expert_ids)
    pair_rows = jnp.repeat(tokens, TOP, axis=0)
    scaled = (jnp.repeat(cotangent.astype(jnp.float32), TOP, axis=0) * route_weights.reshape(-1, 1)).astype(jnp.bfloat16)
    slot_tokens = jnp.zeros((EXPERTS * SLOTS, D), tokens.dtype).at[destination].set(pair_rows).reshape(EXPERTS, SLOTS, D)
    slot_cot = jnp.zeros((EXPERTS * SLOTS, D), scaled.dtype).at[destination].set(scaled).reshape(EXPERTS, SLOTS, D)
    gate_grad, up_grad, down_grad, slot_grad = lax.map(expert_step, (slot_tokens, slot_cot, gate_weight, up_weight, down_weight))
    per_pair = slot_grad.reshape(EXPERTS * SLOTS, D)[destination].astype(jnp.float32).reshape(TOKENS, TOP, D)
    token_grad = jnp.sum(per_pair, axis=1).astype(jnp.bfloat16)
    return token_grad, gate_grad, up_grad, down_grad
```

```python
import jax
import jax.numpy as jnp
from jax import lax
from jax.sharding import PartitionSpec as P


def contract_rows(left, right):
    return lax.dot_general(
        left, right, (((0,), (0,)), ((), ())), preferred_element_type=jnp.float32
    )


def contract_cols(left, right):
    return lax.dot_general(
        left, right, (((1,), (1,)), ((), ())), preferred_element_type=jnp.float32
    )


def local_deltas(gate_pre, up_pre, hidden_grad):
    sigma = jax.nn.sigmoid(gate_pre)
    activated = gate_pre * sigma
    hidden = (activated * up_pre).astype(jnp.bfloat16)
    gate_delta = (hidden_grad * up_pre * sigma * (1.0 + gate_pre * (1.0 - sigma))).astype(
        jnp.bfloat16
    )
    up_delta = (hidden_grad * activated).astype(jnp.bfloat16)
    return (hidden, gate_delta, up_delta)


def swap(value, bit):
    size = lax.axis_size("dp")
    return lax.ppermute(value, "dp", [(i, i ^ bit) for i in range(size)])


def body(tokens, cotangent, expert_ids, route_weights, gate_weight, up_weight, down_weight):
    owners = lax.axis_size("expert")
    width_parts = lax.axis_size("dp")
    tok_rows, top_count = expert_ids.shape
    width = tokens.shape[1]
    capacity = min(tok_rows, max(2, (tok_rows * top_count + owners - 1) // owners))
    slot_count = owners * capacity
    flat_ids = expert_ids.reshape(-1)
    position = jnp.arange(flat_ids.shape[0], dtype=jnp.int32)
    earlier = (flat_ids[:, None] == flat_ids[None, :]) & (position[None, :] < position[:, None])
    rank_pos = jnp.sum(earlier.astype(jnp.int32), axis=1)
    slot_pos = flat_ids * capacity + rank_pos
    pair_select = (slot_pos[:, None] == jnp.arange(slot_count, dtype=jnp.int32)[None, :]).astype(
        jnp.bfloat16
    )
    chosen = jnp.sum(
        pair_select.reshape(tok_rows, top_count, slot_count).astype(jnp.float32), axis=1
    ).astype(jnp.bfloat16)
    pair_tokens = jnp.repeat(tokens, top_count, axis=0)
    pair_scaled = (
        jnp.repeat(cotangent.astype(jnp.float32), top_count, axis=0) * route_weights
    ).astype(jnp.bfloat16)
    payload = jnp.concatenate([pair_tokens, pair_scaled], axis=1)
    send = contract_rows(pair_select, payload).astype(jnp.bfloat16)
    slots = lax.all_to_all(send, "expert", split_axis=0, concat_axis=0, tiled=True)

    core = lax.axis_index("dp") % 2
    half = slot_count // 2
    mine_slots = lax.dynamic_slice_in_dim(slots, core * half, half, 0)
    other_slots = lax.dynamic_slice_in_dim(slots, (1 - core) * half, half, 0)
    w_gate = gate_weight[0]
    w_up = up_weight[0]
    w_down = down_weight[0]

    def partial_sums(rows):
        feats, cots = rows[:, :width], rows[:, width:]
        return (
            jnp.dot(feats, w_gate, preferred_element_type=jnp.float32),
            jnp.dot(feats, w_up, preferred_element_type=jnp.float32),
            contract_cols(cots, w_down),
        )

    def pack(parts):
        return jnp.stack([part.astype(jnp.bfloat16) for part in parts])

    received = swap(pack(partial_sums(other_slots)), 1)
    sums = jnp.stack(partial_sums(mine_slots)) + received.astype(jnp.float32)
    bit = 2
    while bit < width_parts:
        sums = sums + swap(sums.astype(jnp.bfloat16), bit).astype(jnp.float32)
        bit *= 2
    mine = jnp.stack(local_deltas(sums[0], sums[1], sums[2]))
    other = swap(mine, 1)
    hidden, gate_delta, up_delta = jnp.concatenate([mine, other], axis=1)
    both = jnp.concatenate([mine_slots, other_slots], axis=0)
    slot_grad = (contract_cols(gate_delta, w_gate) + contract_cols(up_delta, w_up)).astype(
        jnp.bfloat16
    )
    slot_grad = jnp.where(
        core == 0, slot_grad, jnp.concatenate([slot_grad[half:], slot_grad[:half]], axis=0)
    )
    returned = lax.all_to_all(slot_grad, "expert", split_axis=0, concat_axis=0, tiled=True)
    feats, cots = both[:, :width], both[:, width:]
    gate_grad = contract_rows(feats, gate_delta)
    up_grad = contract_rows(feats, up_delta)
    down_grad = contract_rows(hidden, cots)
    token_grad = jnp.dot(chosen, returned, preferred_element_type=jnp.float32).astype(jnp.bfloat16)
    return (token_grad, gate_grad[None], up_grad[None], down_grad[None])


def solution(mesh):
    return jax.shard_map(
        body,
        mesh=mesh,
        in_specs=(
            P("expert", "dp"),
            P("expert", "dp"),
            P("expert", None),
            P("expert", None),
            P("expert", "dp", None),
            P("expert", "dp", None),
            P("expert", None, "dp"),
        ),
        out_specs=(
            P("expert", "dp"),
            P("expert", "dp", None),
            P("expert", "dp", None),
            P("expert", None, "dp"),
        ),
        check_vma=False,
    )
```

```python
import functools

import jax
import jax.numpy as jnp
from jax import lax
from jax.experimental import pallas as pl
from jax.experimental.pallas import tpu as pltpu
from jax.sharding import PartitionSpec as P


def contract_rows(left, right):
    return lax.dot_general(
        left, right, (((0,), (0,)), ((), ())), preferred_element_type=jnp.float32
    )


def contract_cols(left, right):
    return lax.dot_general(
        left, right, (((1,), (1,)), ((), ())), preferred_element_type=jnp.float32
    )


def local_deltas(gate_pre, up_pre, hidden_grad):
    sigma = jax.nn.sigmoid(gate_pre)
    activated = gate_pre * sigma
    hidden = (activated * up_pre).astype(jnp.bfloat16)
    gate_delta = (hidden_grad * up_pre * sigma * (1.0 + gate_pre * (1.0 - sigma))).astype(
        jnp.bfloat16
    )
    up_delta = (hidden_grad * activated).astype(jnp.bfloat16)
    return (hidden, gate_delta, up_delta)


def swap(value, bit, axis="dp"):
    size = lax.axis_size(axis)
    return lax.ppermute(value, axis, [(i, i ^ bit) for i in range(size)])


COST = dict(
    load=10**7,
    products=(1, 1),
    sums=(1, 1),
    deltas=(1, 1),
    grad=(1, 1),
    wgrad=10**7,
)
TIE = 1


def after(values, marker):
    return lax.optimization_barrier((values, marker))[0]


def call(kernel, outs, *args, cost=1, far=(), scratch=()):
    spaces = [pltpu.HBM if place in far else pltpu.VMEM for place in range(len(args))]
    args = [
        pltpu.with_memory_space_constraint(arg, pltpu.HBM) if place in far else arg
        for place, arg in enumerate(args)
    ]
    args = [
        pltpu.with_memory_space_constraint(arg, pltpu.HBM) if place in far else arg
        for place, arg in enumerate(args)
    ]
    return pl.pallas_call(
        kernel,
        out_shape=outs,
        in_specs=[pl.BlockSpec(memory_space=space) for space in spaces],
        scratch_shapes=scratch,
        compiler_params=pltpu.CompilerParams(vmem_limit_bytes=24 * 1024 * 1024),
        cost_estimate=pl.CostEstimate(flops=cost, bytes_accessed=cost, transcendentals=0),
    )(*args)


def shape(rows, cols, dtype=jnp.bfloat16):
    return jax.ShapeDtypeStruct((rows, cols), dtype)


def dispatch_kernel(owners, capacity, ids_hbm, weights_hbm, tokens_hbm, cotangent_hbm, *refs):
    chosen_ref, *out_refs, ids_ref, weights_ref, tokens_ref, cotangent_ref, sems = refs
    copies = [
        pltpu.make_async_copy(source, target, sems.at[place])
        for place, (source, target) in enumerate(
            (
                (ids_hbm, ids_ref),
                (weights_hbm, weights_ref),
                (tokens_hbm, tokens_ref),
                (cotangent_hbm, cotangent_ref),
            )
        )
    ]
    for copy in copies:
        copy.start()
    copies[0].wait()
    pairs = ids_ref.shape[1]
    width = tokens_ref.shape[1]
    slot_count = owners * capacity
    me = lax.axis_index("expert")
    ids = ids_ref[...]
    named = ids == lax.broadcasted_iota(jnp.int32, (owners, pairs), 0)
    before = lax.broadcasted_iota(jnp.int32, (pairs, pairs), 0) < lax.broadcasted_iota(
        jnp.int32, (pairs, pairs), 1
    )
    named = named.astype(jnp.float32)
    counts = jnp.dot(
        named.astype(jnp.bfloat16),
        before.astype(jnp.float32).astype(jnp.bfloat16),
        preferred_element_type=jnp.float32,
    )
    rank = jnp.sum(named * counts, axis=0, keepdims=True).astype(jnp.int32)
    slots = lax.broadcasted_iota(jnp.int32, (slot_count, pairs), 0)
    chosen_ref[...] = (slots == ids * capacity + rank).astype(jnp.float32).astype(jnp.bfloat16)
    chosen = (slots == (ids ^ me) * capacity + rank).astype(jnp.float32)
    select = chosen.astype(jnp.bfloat16)
    for copy in copies[1:]:
        copy.wait()
    scale = jnp.sum(chosen * weights_ref[...], axis=1, keepdims=True)
    feats = jnp.dot(select, tokens_ref[...], preferred_element_type=jnp.float32)
    cots = jnp.dot(select, cotangent_ref[...], preferred_element_type=jnp.float32) * scale
    at = 0
    for out_ref in out_refs:
        rows = slice(at, at + out_ref.shape[0])
        out_ref[:, :width] = feats[rows].astype(jnp.bfloat16)
        out_ref[:, width:] = cots[rows].astype(jnp.bfloat16)
        at += out_ref.shape[0]


def load_kernel(gate_hbm, up_hbm, down_hbm, marker_hbm, gate_ref, up_ref, down_ref, sems):
    copies = [
        pltpu.make_async_copy(source, target, sems.at[place])
        for place, (source, target) in enumerate(
            ((gate_hbm, gate_ref), (up_hbm, up_ref), (down_hbm, down_ref))
        )
    ]
    for copy in copies:
        copy.start()
    for copy in copies:
        copy.wait()


def straight_rows(refs):
    return [ref[:ref.shape[0] // 2] for ref in refs]


def pair_rows(refs):
    return [ref[...] for ref in refs]


def products_kernel(take_rows, *refs):
    *row_refs, gate_ref, up_ref, down_ref, mine_ref, other_ref = refs
    rows = jnp.concatenate(take_rows(row_refs), axis=0)
    half = rows.shape[0] // 2
    width = rows.shape[1] // 2
    hidden_units = gate_ref.shape[1]
    core = lax.axis_index("dp") % 2
    feats, cots = rows[:, :width], rows[:, width:]
    for place, weight_ref in enumerate((gate_ref, up_ref, down_ref)):
        cols = slice(place * hidden_units, (place + 1) * hidden_units)
        if place < 2:
            out = jnp.dot(feats, weight_ref[...], preferred_element_type=jnp.float32)
        else:
            out = contract_cols(cots, weight_ref[...])
        low, high = out[:half], out[half:]
        mine_ref[:, cols] = jnp.where(core == 0, low, high)
        other_ref[:, cols] = jnp.where(core == 0, high, low).astype(jnp.bfloat16)


def sums_kernel(mine_ref, received_ref, sums_ref, packed_ref):
    sums = mine_ref[...] + received_ref[...].astype(jnp.float32)
    sums_ref[...] = sums
    packed_ref[...] = sums.astype(jnp.bfloat16)


def deltas_kernel(sums_ref, received_ref, out_ref):
    hidden_units = sums_ref.shape[1] // 3
    cols = [slice(i * hidden_units, (i + 1) * hidden_units) for i in range(3)]
    parts = [sums_ref[:, c] + received_ref[:, c].astype(jnp.float32) for c in cols]
    for c, part in zip(cols, local_deltas(*parts)):
        out_ref[:, c] = part


def in_order(core, mine, other):
    return jnp.concatenate(
        [jnp.where(core == 0, mine, other), jnp.where(core == 0, other, mine)], axis=0
    )


def slot_grad_kernel(owners, mine_ref, other_ref, gate_ref, up_ref, *refs):
    *earlier_ref, out_ref = refs
    hidden_units = gate_ref.shape[1]
    rows = in_order(lax.axis_index("dp") % 2, mine_ref[...], other_ref[...])
    out = (
        contract_cols(rows[:, hidden_units:2 * hidden_units], gate_ref[...])
        + contract_cols(rows[:, 2 * hidden_units:], up_ref[...])
    ).astype(jnp.bfloat16)
    if not earlier_ref:
        out_ref[...] = out
        return
    me = lax.axis_index("expert")
    block = out_ref.shape[0] // owners
    earlier = earlier_ref[0][...]
    for k in range(owners):
        source = (earlier, out)[k % 2]
        at = k // 2 * block
        out_ref[pl.ds(pl.multiple_of((me ^ k) * block, block), block)] = source[at:at + block]


def weight_grads_kernel(*refs):
    *in_refs, gate_ref, up_ref, down_ref, rows_ref, deltas_ref = refs
    row_refs, delta_refs = in_refs[:-4], in_refs[-4:]
    step = pl.program_id(0)
    tile = gate_ref.shape[0]
    down_tile = down_ref.shape[0]
    width = rows_ref.shape[1] // 2
    hidden_units = gate_ref.shape[1]

    @pl.when(step == 0)
    def _():
        at = 0
        for value in straight_rows(row_refs[:-1]) + pair_rows(row_refs[-1:]):
            rows_ref[at:at + value.shape[0]] = value
            at += value.shape[0]
        core = lax.axis_index("dp") % 2
        half = deltas_ref.shape[0] // 2
        for place in range(2):
            both = in_order(core, delta_refs[2 * place][...], delta_refs[2 * place + 1][...])
            deltas_ref[place * half:(place + 1) * half] = both

    feats = rows_ref[:, pl.ds(pl.multiple_of(step * tile, tile), tile)]
    gate_ref[...] = contract_rows(feats, deltas_ref[:, hidden_units:2 * hidden_units])
    up_ref[...] = contract_rows(feats, deltas_ref[:, 2 * hidden_units:])
    hidden = deltas_ref[:, pl.ds(pl.multiple_of(step * down_tile, down_tile), down_tile)]
    down_ref[...] = contract_rows(hidden, rows_ref[:, width:])


def token_grad_kernel(chosen_ref, returned_ref, out_ref):
    out_ref[...] = contract_rows(chosen_ref[...], returned_ref[...]).astype(jnp.bfloat16)


def body_by_all_to_all(tokens, cotangent, expert_ids, route_weights, gate_weight, up_weight, down_weight):
    owners = lax.axis_size("expert")
    width_parts = lax.axis_size("dp")
    tok_rows, top_count = expert_ids.shape
    width = tokens.shape[1]
    capacity = min(tok_rows, max(2, (tok_rows * top_count + owners - 1) // owners))
    slot_count = owners * capacity
    flat_ids = expert_ids.reshape(-1)
    position = jnp.arange(flat_ids.shape[0], dtype=jnp.int32)
    earlier = (flat_ids[:, None] == flat_ids[None, :]) & (position[None, :] < position[:, None])
    rank_pos = jnp.sum(earlier.astype(jnp.int32), axis=1)
    slot_pos = flat_ids * capacity + rank_pos
    pair_select = (slot_pos[:, None] == jnp.arange(slot_count, dtype=jnp.int32)[None, :]).astype(
        jnp.bfloat16
    )
    chosen = jnp.sum(
        pair_select.reshape(tok_rows, top_count, slot_count).astype(jnp.float32), axis=1
    ).astype(jnp.bfloat16)
    pair_tokens = jnp.repeat(tokens, top_count, axis=0)
    pair_scaled = (
        jnp.repeat(cotangent.astype(jnp.float32), top_count, axis=0) * route_weights
    ).astype(jnp.bfloat16)
    payload = jnp.concatenate([pair_tokens, pair_scaled], axis=1)
    send = contract_rows(pair_select, payload).astype(jnp.bfloat16)
    slots = lax.all_to_all(send, "expert", split_axis=0, concat_axis=0, tiled=True)

    core = lax.axis_index("dp") % 2
    half = slot_count // 2
    mine_slots = lax.dynamic_slice_in_dim(slots, core * half, half, 0)
    other_slots = lax.dynamic_slice_in_dim(slots, (1 - core) * half, half, 0)
    w_gate = gate_weight[0]
    w_up = up_weight[0]
    w_down = down_weight[0]

    def partial_sums(rows):
        feats, cots = rows[:, :width], rows[:, width:]
        return (
            jnp.dot(feats, w_gate, preferred_element_type=jnp.float32),
            jnp.dot(feats, w_up, preferred_element_type=jnp.float32),
            contract_cols(cots, w_down),
        )

    def pack(parts):
        return jnp.stack([part.astype(jnp.bfloat16) for part in parts])

    received = swap(pack(partial_sums(other_slots)), 1)
    sums = jnp.stack(partial_sums(mine_slots)) + received.astype(jnp.float32)
    bit = 2
    while bit < width_parts:
        sums = sums + swap(sums.astype(jnp.bfloat16), bit).astype(jnp.float32)
        bit *= 2
    mine = jnp.stack(local_deltas(sums[0], sums[1], sums[2]))
    other = swap(mine, 1)
    hidden, gate_delta, up_delta = jnp.concatenate([mine, other], axis=1)
    both = jnp.concatenate([mine_slots, other_slots], axis=0)
    slot_grad = (contract_cols(gate_delta, w_gate) + contract_cols(up_delta, w_up)).astype(
        jnp.bfloat16
    )
    slot_grad = jnp.where(
        core == 0, slot_grad, jnp.concatenate([slot_grad[half:], slot_grad[:half]], axis=0)
    )
    returned = lax.all_to_all(slot_grad, "expert", split_axis=0, concat_axis=0, tiled=True)
    feats, cots = both[:, :width], both[:, width:]
    gate_grad = contract_rows(feats, gate_delta)
    up_grad = contract_rows(feats, up_delta)
    down_grad = contract_rows(hidden, cots)
    token_grad = jnp.dot(chosen, returned, preferred_element_type=jnp.float32).astype(jnp.bfloat16)
    return (token_grad, gate_grad[None], up_grad[None], down_grad[None])


def body_by_pairs(tokens, cotangent, expert_ids, route_weights, gate_weight, up_weight, down_weight):
    owners = lax.axis_size("expert")
    width_parts = lax.axis_size("dp")
    tok_rows, _ = expert_ids.shape
    width = tokens.shape[1]
    hidden_units = gate_weight.shape[2]
    capacity = min(tok_rows, max(2, (tok_rows + owners - 1) // owners))
    slot_count = owners * capacity
    half = owners // 2

    chosen, *groups = call(
        functools.partial(dispatch_kernel, owners, capacity),
        (shape(slot_count, tok_rows),) + (shape(2 * capacity, 2 * width),) * half,
        expert_ids.reshape(1, tok_rows),
        route_weights.reshape(1, tok_rows),
        tokens,
        cotangent,
        far=range(4),
        scratch=[
            pltpu.VMEM((1, tok_rows), jnp.int32),
            pltpu.VMEM((1, tok_rows), jnp.float32),
            pltpu.VMEM((tok_rows, width), jnp.bfloat16),
            pltpu.VMEM((tok_rows, width), jnp.bfloat16),
            pltpu.SemaphoreType.DMA((4,)),
        ],
    )
    weights = call(
        load_kernel,
        (shape(width, hidden_units), shape(width, hidden_units), shape(hidden_units, width)),
        gate_weight[0],
        up_weight[0],
        down_weight[0],
        chosen,
        far=range(3),
        scratch=[pltpu.SemaphoreType.DMA((3,))],
        cost=COST["load"],
    )
    moved = {j: swap(groups[j], 2 * j, "expert") for j in reversed(range(1, half))}
    groups = [groups[0]] + [moved[j] for j in range(1, half)]
    forward = jnp.concatenate([group[capacity:] for group in groups], axis=0)
    forward = after(forward, weights[2])
    by_pair = swap(forward, 1, "expert")
    order = list(range(0, owners, 2)) + list(range(1, owners, 2))

    part = slot_count // 4
    packed = shape(part, 3 * hidden_units)
    wide = shape(part, 3 * hidden_units, jnp.float32)
    held = []
    for place, (take, rows) in enumerate(((straight_rows, groups), (pair_rows, [by_pair]))):
        mine, other = call(
            functools.partial(products_kernel, take),
            (wide, packed),
            *rows,
            *weights,
            cost=COST["products"][place],
        )
        sums, marker = call(
            sums_kernel, (wide, packed), mine, swap(other, 1), cost=COST["sums"][place]
        )
        bit = 2
        while 2 * bit < width_parts:
            sums, marker = call(sums_kernel, (wide, packed), sums, swap(marker, bit))
            bit *= 2
        held.append((sums, swap(marker, bit)))
    deltas, grads = [], []
    for place, (sums, received) in enumerate(held):
        if place and TIE == 1:
            sums = after(sums, grads)
        mine = call(deltas_kernel, packed, sums, received, cost=COST["deltas"][place])
        if place and TIE == 3:
            mine = after(mine, grads)
        pair = [mine, swap(mine, 1)]
        deltas += pair
        grads = [
            call(
                functools.partial(slot_grad_kernel, owners),
                shape((place + 1) * half * capacity, width),
                *pair,
                *weights[:2],
                *grads,
                cost=COST["grad"][place],
            )
        ]
    returned = lax.all_to_all(grads[0], "expert", split_axis=0, concat_axis=0, tiled=True)
    steps = 4 if width % 512 == 0 else 1
    down_tile = -(-hidden_units // (128 * steps)) * 128
    gate_grad, up_grad, down_grad = pl.pallas_call(
        weight_grads_kernel,
        out_shape=(
            shape(width, hidden_units, jnp.float32),
            shape(width, hidden_units, jnp.float32),
            shape(hidden_units, width, jnp.float32),
        ),
        grid=(steps,),
        in_specs=[pl.BlockSpec(memory_space=pltpu.VMEM)] * (half + 1 + 4),
        out_specs=(
            pl.BlockSpec((width // steps, hidden_units), lambda i: (i, 0)),
            pl.BlockSpec((width // steps, hidden_units), lambda i: (i, 0)),
            pl.BlockSpec((down_tile, width), lambda i: (i, 0)),
        ),
        scratch_shapes=[
            pltpu.VMEM((slot_count, 2 * width), jnp.bfloat16),
            pltpu.VMEM((slot_count, 3 * hidden_units), jnp.bfloat16),
        ],
        compiler_params=pltpu.CompilerParams(vmem_limit_bytes=24 * 1024 * 1024),
        cost_estimate=pl.CostEstimate(
            flops=COST["wgrad"], bytes_accessed=COST["wgrad"], transcendentals=0
        ),
    )(*groups, by_pair, *deltas)
    token_grad = call(token_grad_kernel, shape(tok_rows, width), chosen, returned)
    return (token_grad, gate_grad[None], up_grad[None], down_grad[None])


def body(tokens, cotangent, expert_ids, *rest):
    owners = lax.axis_size("expert")
    width_parts = lax.axis_size("dp")
    tok_rows, top_count = expert_ids.shape
    by_pairs = (
        top_count == 1
        and owners >= 8
        and owners & (owners - 1) == 0
        and width_parts >= 4
        and tok_rows % (16 * owners) == 0
    )
    chosen = body_by_pairs if by_pairs else body_by_all_to_all
    return chosen(tokens, cotangent, expert_ids, *rest)


def solution(mesh):
    return jax.shard_map(
        body,
        mesh=mesh,
        in_specs=(
            P("expert", "dp"),
            P("expert", "dp"),
            P("expert", None),
            P("expert", None),
            P("expert", "dp", None),
            P("expert", "dp", None),
            P("expert", None, "dp"),
        ),
        out_specs=(
            P("expert", "dp"),
            P("expert", "dp", None),
            P("expert", "dp", None),
            P("expert", None, "dp"),
        ),
        check_vma=False,
    )
```

```python
import functools

import jax
import jax.numpy as jnp
from jax import lax
from jax.experimental import pallas as pl
from jax.experimental.pallas import tpu as pltpu
from jax.sharding import PartitionSpec as P


def contract_rows(left, right):
    return lax.dot_general(
        left, right, (((0,), (0,)), ((), ())), preferred_element_type=jnp.float32
    )


def contract_cols(left, right):
    return lax.dot_general(
        left, right, (((1,), (1,)), ((), ())), preferred_element_type=jnp.float32
    )


def local_deltas(gate_pre, up_pre, hidden_grad):
    sigma = jax.nn.sigmoid(gate_pre)
    activated = gate_pre * sigma
    hidden = (activated * up_pre).astype(jnp.bfloat16)
    gate_delta = (hidden_grad * up_pre * sigma * (1.0 + gate_pre * (1.0 - sigma))).astype(
        jnp.bfloat16
    )
    up_delta = (hidden_grad * activated).astype(jnp.bfloat16)
    return (hidden, gate_delta, up_delta)


def swap(value, bit, axis="dp"):
    size = lax.axis_size(axis)
    return lax.ppermute(value, axis, [(i, i ^ bit) for i in range(size)])


def after(values, marker):
    return lax.optimization_barrier((values, marker))[0]


def call(kernel, outs, *args, cost=1, far=(), scratch=()):
    spaces = [pltpu.HBM if place in far else pltpu.VMEM for place in range(len(args))]
    args = [
        pltpu.with_memory_space_constraint(arg, pltpu.HBM) if place in far else arg
        for place, arg in enumerate(args)
    ]
    return pl.pallas_call(
        kernel,
        out_shape=outs,
        in_specs=[pl.BlockSpec(memory_space=space) for space in spaces],
        scratch_shapes=scratch,
        compiler_params=pltpu.CompilerParams(vmem_limit_bytes=24 * 1024 * 1024),
        cost_estimate=pl.CostEstimate(flops=cost, bytes_accessed=cost, transcendentals=0),
    )(*args)


def shape(rows, cols, dtype=jnp.bfloat16):
    return jax.ShapeDtypeStruct((rows, cols), dtype)


def dispatch_kernel(owners, capacity, ids_hbm, weights_hbm, tokens_hbm, cotangent_hbm, *refs):
    chosen_ref, *out_refs, ids_ref, weights_ref, tokens_ref, cotangent_ref, sems = refs
    copies = [
        pltpu.make_async_copy(source, target, sems.at[place])
        for place, (source, target) in enumerate(
            (
                (ids_hbm, ids_ref),
                (weights_hbm, weights_ref),
                (tokens_hbm, tokens_ref),
                (cotangent_hbm, cotangent_ref),
            )
        )
    ]
    for copy in copies:
        copy.start()
    copies[0].wait()
    pairs = ids_ref.shape[1]
    width = tokens_ref.shape[1]
    slot_count = owners * capacity
    me = lax.axis_index("expert")
    ids = ids_ref[...]
    named = ids == lax.broadcasted_iota(jnp.int32, (owners, pairs), 0)
    before = lax.broadcasted_iota(jnp.int32, (pairs, pairs), 0) < lax.broadcasted_iota(
        jnp.int32, (pairs, pairs), 1
    )
    named = named.astype(jnp.float32)
    counts = jnp.dot(
        named.astype(jnp.bfloat16),
        before.astype(jnp.float32).astype(jnp.bfloat16),
        preferred_element_type=jnp.float32,
    )
    rank = jnp.sum(named * counts, axis=0, keepdims=True).astype(jnp.int32)
    slots = lax.broadcasted_iota(jnp.int32, (slot_count, pairs), 0)
    chosen_ref[...] = (slots == ids * capacity + rank).astype(jnp.float32).astype(jnp.bfloat16)
    chosen = (slots == (ids ^ me) * capacity + rank).astype(jnp.float32)
    select = chosen.astype(jnp.bfloat16)
    for copy in copies[1:]:
        copy.wait()
    scale = jnp.sum(chosen * weights_ref[...], axis=1, keepdims=True)
    feats = jnp.dot(select, tokens_ref[...], preferred_element_type=jnp.float32)
    cots = jnp.dot(select, cotangent_ref[...], preferred_element_type=jnp.float32) * scale
    at = 0
    for out_ref in out_refs:
        rows = slice(at, at + out_ref.shape[0])
        out_ref[:, :width] = feats[rows].astype(jnp.bfloat16)
        out_ref[:, width:] = cots[rows].astype(jnp.bfloat16)
        at += out_ref.shape[0]


def load_kernel(gate_hbm, up_hbm, down_hbm, marker_hbm, gate_ref, up_ref, down_ref, sems):
    copies = [
        pltpu.make_async_copy(source, target, sems.at[place])
        for place, (source, target) in enumerate(
            ((gate_hbm, gate_ref), (up_hbm, up_ref), (down_hbm, down_ref))
        )
    ]
    for copy in copies:
        copy.start()
    for copy in copies:
        copy.wait()


def straight_rows(refs):
    return jnp.concatenate([ref[:ref.shape[0] // 2] for ref in refs], axis=0)


def products_kernel(*refs):
    *row_refs, gate_ref, up_ref, down_ref, mine_ref, other_ref = refs
    rows = straight_rows(row_refs) if len(row_refs) > 1 else row_refs[0][...]
    half = rows.shape[0] // 2
    width = rows.shape[1] // 2
    hidden_units = gate_ref.shape[1]
    core = lax.axis_index("dp") % 2
    feats, cots = rows[:, :width], rows[:, width:]
    for place, weight_ref in enumerate((gate_ref, up_ref, down_ref)):
        cols = slice(place * hidden_units, (place + 1) * hidden_units)
        if place < 2:
            out = jnp.dot(feats, weight_ref[...], preferred_element_type=jnp.float32)
        else:
            out = contract_cols(cots, weight_ref[...])
        low, high = out[:half], out[half:]
        mine_ref[:, cols] = jnp.where(core == 0, low, high)
        other_ref[:, cols] = jnp.where(core == 0, high, low).astype(jnp.bfloat16)


def sums_kernel(mine_ref, received_ref, sums_ref, packed_ref):
    cols = mine_ref.shape[1]
    sums = mine_ref[...] + received_ref[:, :cols].astype(jnp.float32)
    sums_ref[...] = sums
    packed_ref[:, :cols] = sums.astype(jnp.bfloat16)
    packed_ref[:, cols:] = jnp.zeros((sums.shape[0], packed_ref.shape[1] - cols), jnp.bfloat16)


def deltas_kernel(sums_ref, received_ref, out_ref):
    hidden_units = sums_ref.shape[1] // 3
    cols = [slice(i * hidden_units, (i + 1) * hidden_units) for i in range(3)]
    parts = [sums_ref[:, c] + received_ref[:, c].astype(jnp.float32) for c in cols]
    for c, part in zip(cols, local_deltas(*parts)):
        out_ref[:, c] = part


def in_order(core, mine, other):
    return jnp.concatenate(
        [jnp.where(core == 0, mine, other), jnp.where(core == 0, other, mine)], axis=0
    )


def slot_grad_kernel(groups, mine_ref, other_ref, gate_ref, up_ref, *refs):
    *earlier_ref, out_ref = refs
    hidden_units = gate_ref.shape[1]
    rows = in_order(lax.axis_index("dp") % 2, mine_ref[...], other_ref[...])
    out = (
        contract_cols(rows[:, hidden_units:2 * hidden_units], gate_ref[...])
        + contract_cols(rows[:, 2 * hidden_units:], up_ref[...])
    ).astype(jnp.bfloat16)
    if not earlier_ref:
        out_ref[...] = out
        return
    me = lax.axis_index("expert")
    block = out_ref.shape[0] // (2 * len(groups))
    for side, rows in enumerate((earlier_ref[0][...], out)):
        for place, group in enumerate(groups):
            start = pl.multiple_of((me ^ (2 * group + side)) * block, block)
            out_ref[pl.ds(start, block)] = rows[place * block:(place + 1) * block]


def weight_grads_kernel(*refs):
    *in_refs, gate_ref, up_ref, down_ref, rows_ref, deltas_ref = refs
    row_refs, delta_refs = in_refs[:-4], in_refs[-4:]
    step = pl.program_id(0)
    tile = gate_ref.shape[0]
    down_tile = down_ref.shape[0]
    width = rows_ref.shape[1] // 2
    hidden_units = gate_ref.shape[1]

    @pl.when(step == 0)
    def _():
        core = lax.axis_index("dp") % 2
        half = deltas_ref.shape[0] // 2
        rows_ref[:half] = straight_rows(row_refs[:-1])
        rows_ref[half:] = row_refs[-1][...]
        for place in range(2):
            both = in_order(core, delta_refs[2 * place][...], delta_refs[2 * place + 1][...])
            deltas_ref[place * half:(place + 1) * half] = both

    feats = rows_ref[:, pl.ds(pl.multiple_of(step * tile, tile), tile)]
    gate_ref[...] = contract_rows(feats, deltas_ref[:, hidden_units:2 * hidden_units])
    up_ref[...] = contract_rows(feats, deltas_ref[:, 2 * hidden_units:])
    hidden = deltas_ref[:, pl.ds(pl.multiple_of(step * down_tile, down_tile), down_tile)]
    down_ref[...] = contract_rows(hidden, rows_ref[:, width:])


def token_grad_kernel(chosen_ref, returned_ref, out_ref):
    out_ref[...] = contract_rows(chosen_ref[...], returned_ref[...]).astype(jnp.bfloat16)


def body_by_all_to_all(tokens, cotangent, expert_ids, route_weights, gate_weight, up_weight, down_weight):
    owners = lax.axis_size("expert")
    width_parts = lax.axis_size("dp")
    tok_rows, top_count = expert_ids.shape
    width = tokens.shape[1]
    capacity = min(tok_rows, max(2, (tok_rows * top_count + owners - 1) // owners))
    slot_count = owners * capacity
    flat_ids = expert_ids.reshape(-1)
    position = jnp.arange(flat_ids.shape[0], dtype=jnp.int32)
    earlier = (flat_ids[:, None] == flat_ids[None, :]) & (position[None, :] < position[:, None])
    rank_pos = jnp.sum(earlier.astype(jnp.int32), axis=1)
    slot_pos = flat_ids * capacity + rank_pos
    pair_select = (slot_pos[:, None] == jnp.arange(slot_count, dtype=jnp.int32)[None, :]).astype(
        jnp.bfloat16
    )
    chosen = jnp.sum(
        pair_select.reshape(tok_rows, top_count, slot_count).astype(jnp.float32), axis=1
    ).astype(jnp.bfloat16)
    pair_tokens = jnp.repeat(tokens, top_count, axis=0)
    pair_scaled = (
        jnp.repeat(cotangent.astype(jnp.float32), top_count, axis=0) * route_weights
    ).astype(jnp.bfloat16)
    payload = jnp.concatenate([pair_tokens, pair_scaled], axis=1)
    send = contract_rows(pair_select, payload).astype(jnp.bfloat16)
    slots = lax.all_to_all(send, "expert", split_axis=0, concat_axis=0, tiled=True)

    core = lax.axis_index("dp") % 2
    half = slot_count // 2
    mine_slots = lax.dynamic_slice_in_dim(slots, core * half, half, 0)
    other_slots = lax.dynamic_slice_in_dim(slots, (1 - core) * half, half, 0)
    w_gate = gate_weight[0]
    w_up = up_weight[0]
    w_down = down_weight[0]

    def partial_sums(rows):
        feats, cots = rows[:, :width], rows[:, width:]
        return (
            jnp.dot(feats, w_gate, preferred_element_type=jnp.float32),
            jnp.dot(feats, w_up, preferred_element_type=jnp.float32),
            contract_cols(cots, w_down),
        )

    def pack(parts):
        return jnp.stack([part.astype(jnp.bfloat16) for part in parts])

    received = swap(pack(partial_sums(other_slots)), 1)
    sums = jnp.stack(partial_sums(mine_slots)) + received.astype(jnp.float32)
    bit = 2
    while bit < width_parts:
        sums = sums + swap(sums.astype(jnp.bfloat16), bit).astype(jnp.float32)
        bit *= 2
    mine = jnp.stack(local_deltas(sums[0], sums[1], sums[2]))
    other = swap(mine, 1)
    hidden, gate_delta, up_delta = jnp.concatenate([mine, other], axis=1)
    both = jnp.concatenate([mine_slots, other_slots], axis=0)
    slot_grad = (contract_cols(gate_delta, w_gate) + contract_cols(up_delta, w_up)).astype(
        jnp.bfloat16
    )
    slot_grad = jnp.where(
        core == 0, slot_grad, jnp.concatenate([slot_grad[half:], slot_grad[:half]], axis=0)
    )
    returned = lax.all_to_all(slot_grad, "expert", split_axis=0, concat_axis=0, tiled=True)
    feats, cots = both[:, :width], both[:, width:]
    gate_grad = contract_rows(feats, gate_delta)
    up_grad = contract_rows(feats, up_delta)
    down_grad = contract_rows(hidden, cots)
    token_grad = jnp.dot(chosen, returned, preferred_element_type=jnp.float32).astype(jnp.bfloat16)
    return (token_grad, gate_grad[None], up_grad[None], down_grad[None])


def body_by_pairs(tokens, cotangent, expert_ids, route_weights, gate_weight, up_weight, down_weight):
    owners = lax.axis_size("expert")
    width_parts = lax.axis_size("dp")
    tok_rows, _ = expert_ids.shape
    width = tokens.shape[1]
    hidden_units = gate_weight.shape[2]
    capacity = min(tok_rows, max(2, (tok_rows + owners - 1) // owners))
    slot_count = owners * capacity
    half = owners // 2

    far_first = [0] + list(reversed(range(1, half)))
    chosen, *groups = call(
        functools.partial(dispatch_kernel, owners, capacity),
        (shape(slot_count, tok_rows),) + (shape(2 * capacity, 2 * width),) * half,
        expert_ids.reshape(1, tok_rows),
        route_weights.reshape(1, tok_rows),
        tokens,
        cotangent,
        far=range(4),
        scratch=[
            pltpu.VMEM((1, tok_rows), jnp.int32),
            pltpu.VMEM((1, tok_rows), jnp.float32),
            pltpu.VMEM((tok_rows, width), jnp.bfloat16),
            pltpu.VMEM((tok_rows, width), jnp.bfloat16),
            pltpu.SemaphoreType.DMA((4,)),
        ],
    )
    weights = call(
        load_kernel,
        (shape(width, hidden_units), shape(width, hidden_units), shape(hidden_units, width)),
        gate_weight[0],
        up_weight[0],
        down_weight[0],
        chosen,
        far=range(3),
        scratch=[pltpu.SemaphoreType.DMA((3,))],
        cost=10**7,
    )
    groups = [groups[0]] + [swap(groups[j], 2 * j, "expert") for j in far_first[1:]]
    seconds = jnp.concatenate([group[capacity:] for group in groups], axis=0)
    by_pair = swap(after(seconds, weights[2]), 1, "expert")

    part = slot_count // 4
    packed = shape(part, 3 * hidden_units)
    wide = shape(part, 3 * hidden_units, jnp.float32)
    padded = shape(part, 3 * hidden_units + 128)
    held = []
    for rows, cost in ((groups, 1), ([by_pair], 10**9)):
        mine, other = call(products_kernel, (wide, packed), *rows, *weights, cost=cost)
        sums, marker = call(sums_kernel, (wide, padded), mine, swap(other, 1))
        bit = 2
        while 2 * bit < width_parts:
            sums, marker = call(sums_kernel, (wide, padded), sums, swap(marker, bit))
            bit *= 2
        held.append((sums, swap(marker, bit)))
    deltas, grads = [], []
    for place, (sums, received) in enumerate(held):
        mine = call(deltas_kernel, packed, after(sums, grads) if grads else sums, received)
        pair = [mine, swap(mine, 1)]
        deltas += pair
        grads = [
            call(
                functools.partial(slot_grad_kernel, far_first),
                shape((place + 1) * half * capacity, width),
                *pair,
                *weights[:2],
                *grads,
            )
        ]
    returned = lax.all_to_all(grads[0], "expert", split_axis=0, concat_axis=0, tiled=True)
    steps = 4 if width % 512 == 0 else 1
    down_tile = -(-hidden_units // (128 * steps)) * 128
    gate_grad, up_grad, down_grad = pl.pallas_call(
        weight_grads_kernel,
        out_shape=(
            shape(width, hidden_units, jnp.float32),
            shape(width, hidden_units, jnp.float32),
            shape(hidden_units, width, jnp.float32),
        ),
        grid=(steps,),
        in_specs=[pl.BlockSpec(memory_space=pltpu.VMEM)] * (half + 1 + 4),
        out_specs=(
            pl.BlockSpec((width // steps, hidden_units), lambda i: (i, 0)),
            pl.BlockSpec((width // steps, hidden_units), lambda i: (i, 0)),
            pl.BlockSpec((down_tile, width), lambda i: (i, 0)),
        ),
        scratch_shapes=[
            pltpu.VMEM((slot_count, 2 * width), jnp.bfloat16),
            pltpu.VMEM((slot_count, 3 * hidden_units), jnp.bfloat16),
        ],
        compiler_params=pltpu.CompilerParams(vmem_limit_bytes=24 * 1024 * 1024),
        cost_estimate=pl.CostEstimate(flops=10**7, bytes_accessed=10**7, transcendentals=0),
    )(*groups, by_pair, *deltas)
    token_grad = call(token_grad_kernel, shape(tok_rows, width), chosen, returned)
    return (token_grad, gate_grad[None], up_grad[None], down_grad[None])


def body(tokens, cotangent, expert_ids, *rest):
    owners = lax.axis_size("expert")
    width_parts = lax.axis_size("dp")
    tok_rows, top_count = expert_ids.shape
    by_pairs = (
        top_count == 1
        and owners >= 8
        and owners & (owners - 1) == 0
        and width_parts >= 4
        and tok_rows % (16 * owners) == 0
    )
    chosen = body_by_pairs if by_pairs else body_by_all_to_all
    return chosen(tokens, cotangent, expert_ids, *rest)


def solution(mesh):
    return jax.shard_map(
        body,
        mesh=mesh,
        in_specs=(
            P("expert", "dp"),
            P("expert", "dp"),
            P("expert", None),
            P("expert", None),
            P("expert", "dp", None),
            P("expert", "dp", None),
            P("expert", None, "dp"),
        ),
        out_specs=(
            P("expert", "dp"),
            P("expert", "dp", None),
            P("expert", "dp", None),
            P("expert", None, "dp"),
        ),
        check_vma=False,
    )
```

```python
import functools

import jax
import jax.numpy as jnp
from jax import lax
from jax.experimental import pallas as pl
from jax.experimental.pallas import tpu as pltpu
from jax.sharding import PartitionSpec as P


def contract_rows(left, right):
    return lax.dot_general(
        left, right, (((0,), (0,)), ((), ())), preferred_element_type=jnp.float32
    )


def contract_cols(left, right):
    return lax.dot_general(
        left, right, (((1,), (1,)), ((), ())), preferred_element_type=jnp.float32
    )


def local_deltas(gate_pre, up_pre, hidden_grad):
    sigma = jax.nn.sigmoid(gate_pre)
    activated = gate_pre * sigma
    hidden = (activated * up_pre).astype(jnp.bfloat16)
    gate_delta = (hidden_grad * up_pre * sigma * (1.0 + gate_pre * (1.0 - sigma))).astype(
        jnp.bfloat16
    )
    up_delta = (hidden_grad * activated).astype(jnp.bfloat16)
    return (hidden, gate_delta, up_delta)


def swap(value, bit, axis="dp"):
    size = lax.axis_size(axis)
    return lax.ppermute(value, axis, [(i, i ^ bit) for i in range(size)])


FAR_PRODUCTS_COST = 10**9
FAR_DELTAS_COST = 2 * 10**9


def after(values, marker):
    return lax.optimization_barrier((values, marker))[0]


def call(kernel, outs, *args, cost=1, far=(), scratch=()):
    spaces = [pltpu.HBM if place in far else pltpu.VMEM for place in range(len(args))]
    args = [
        pltpu.with_memory_space_constraint(arg, pltpu.HBM) if place in far else arg
        for place, arg in enumerate(args)
    ]
    return pl.pallas_call(
        kernel,
        out_shape=outs,
        in_specs=[pl.BlockSpec(memory_space=space) for space in spaces],
        scratch_shapes=scratch,
        compiler_params=pltpu.CompilerParams(vmem_limit_bytes=24 * 1024 * 1024),
        cost_estimate=pl.CostEstimate(flops=cost, bytes_accessed=cost, transcendentals=0),
    )(*args)


def shape(rows, cols, dtype=jnp.bfloat16):
    return jax.ShapeDtypeStruct((rows, cols), dtype)


def dispatch_kernel(owners, capacity, ids_hbm, weights_hbm, tokens_hbm, cotangent_hbm, *refs):
    chosen_ref, *out_refs, ids_ref, weights_ref, tokens_ref, cotangent_ref, sems = refs
    copies = [
        pltpu.make_async_copy(source, target, sems.at[place])
        for place, (source, target) in enumerate(
            (
                (ids_hbm, ids_ref),
                (weights_hbm, weights_ref),
                (tokens_hbm, tokens_ref),
                (cotangent_hbm, cotangent_ref),
            )
        )
    ]
    for copy in copies:
        copy.start()
    copies[0].wait()
    pairs = ids_ref.shape[1]
    width = tokens_ref.shape[1]
    slot_count = owners * capacity
    me = lax.axis_index("expert")
    ids = ids_ref[...]
    named = ids == lax.broadcasted_iota(jnp.int32, (owners, pairs), 0)
    before = lax.broadcasted_iota(jnp.int32, (pairs, pairs), 0) < lax.broadcasted_iota(
        jnp.int32, (pairs, pairs), 1
    )
    named = named.astype(jnp.float32)
    counts = jnp.dot(
        named.astype(jnp.bfloat16),
        before.astype(jnp.float32).astype(jnp.bfloat16),
        preferred_element_type=jnp.float32,
    )
    rank = jnp.sum(named * counts, axis=0, keepdims=True).astype(jnp.int32)
    slots = lax.broadcasted_iota(jnp.int32, (slot_count, pairs), 0)
    chosen_ref[...] = (slots == ids * capacity + rank).astype(jnp.float32).astype(jnp.bfloat16)
    chosen = (slots == (ids ^ me) * capacity + rank).astype(jnp.float32)
    select = chosen.astype(jnp.bfloat16)
    for copy in copies[1:]:
        copy.wait()
    scale = jnp.sum(chosen * weights_ref[...], axis=1, keepdims=True)
    feats = jnp.dot(select, tokens_ref[...], preferred_element_type=jnp.float32)
    cots = jnp.dot(select, cotangent_ref[...], preferred_element_type=jnp.float32) * scale
    at = 0
    for out_ref in out_refs:
        rows = slice(at, at + out_ref.shape[0])
        out_ref[:, :width] = feats[rows].astype(jnp.bfloat16)
        out_ref[:, width:] = cots[rows].astype(jnp.bfloat16)
        at += out_ref.shape[0]


def load_kernel(gate_hbm, up_hbm, down_hbm, marker_hbm, gate_ref, up_ref, down_ref, sems):
    copies = [
        pltpu.make_async_copy(source, target, sems.at[place])
        for place, (source, target) in enumerate(
            ((gate_hbm, gate_ref), (up_hbm, up_ref), (down_hbm, down_ref))
        )
    ]
    for copy in copies:
        copy.start()
    for copy in copies:
        copy.wait()


def near_rows(own_ref, from_pair_ref, *group_refs):
    halves = [ref[:ref.shape[0] // 2] for ref in group_refs]
    return jnp.concatenate([own_ref[...]] + halves + [from_pair_ref[...]], axis=0)


def products_kernel(*refs):
    *row_refs, gate_ref, up_ref, down_ref, mine_ref, other_ref = refs
    rows = near_rows(*row_refs) if len(row_refs) > 1 else row_refs[0][...]
    half = rows.shape[0] // 2
    width = rows.shape[1] // 2
    hidden_units = gate_ref.shape[1]
    core = lax.axis_index("dp") % 2
    feats, cots = rows[:, :width], rows[:, width:]
    for place, weight_ref in enumerate((gate_ref, up_ref, down_ref)):
        cols = slice(place * hidden_units, (place + 1) * hidden_units)
        if place < 2:
            out = jnp.dot(feats, weight_ref[...], preferred_element_type=jnp.float32)
        else:
            out = contract_cols(cots, weight_ref[...])
        low, high = out[:half], out[half:]
        mine_ref[:, cols] = jnp.where(core == 0, low, high)
        other_ref[:, cols] = jnp.where(core == 0, high, low).astype(jnp.bfloat16)


def sums_kernel(mine_ref, received_ref, sums_ref, packed_ref):
    sums = mine_ref[...] + received_ref[...].astype(jnp.float32)
    sums_ref[...] = sums
    packed_ref[...] = sums.astype(jnp.bfloat16)


def deltas_kernel(sums_ref, received_ref, out_ref):
    hidden_units = sums_ref.shape[1] // 3
    cols = [slice(i * hidden_units, (i + 1) * hidden_units) for i in range(3)]
    parts = [sums_ref[:, c] + received_ref[:, c].astype(jnp.float32) for c in cols]
    for c, part in zip(cols, local_deltas(*parts)):
        out_ref[:, c] = part


def in_order(core, mine, other):
    return jnp.concatenate(
        [jnp.where(core == 0, mine, other), jnp.where(core == 0, other, mine)], axis=0
    )


def slot_grad_kernel(order, mine_ref, other_ref, gate_ref, up_ref, *refs):
    *earlier_ref, out_ref = refs
    hidden_units = gate_ref.shape[1]
    rows = in_order(lax.axis_index("dp") % 2, mine_ref[...], other_ref[...])
    out = (
        contract_cols(rows[:, hidden_units:2 * hidden_units], gate_ref[...])
        + contract_cols(rows[:, 2 * hidden_units:], up_ref[...])
    ).astype(jnp.bfloat16)
    if not earlier_ref:
        out_ref[...] = out
        return
    me = lax.axis_index("expert")
    block = out_ref.shape[0] // len(order)
    rows = jnp.concatenate([earlier_ref[0][...], out], axis=0)
    for place, k in enumerate(order):
        start = pl.multiple_of((me ^ k) * block, block)
        out_ref[pl.ds(start, block)] = rows[place * block:(place + 1) * block]


def weight_grads_kernel(*refs):
    *in_refs, gate_ref, up_ref, down_ref, rows_ref, deltas_ref = refs
    row_refs, delta_refs = in_refs[:-4], in_refs[-4:]
    step = pl.program_id(0)
    tile = gate_ref.shape[0]
    down_tile = down_ref.shape[0]
    width = rows_ref.shape[1] // 2
    hidden_units = gate_ref.shape[1]

    @pl.when(step == 0)
    def _():
        core = lax.axis_index("dp") % 2
        near = 2 * delta_refs[0].shape[0]
        rows_ref[:near] = near_rows(*row_refs[:-1])
        rows_ref[near:] = row_refs[-1][...]
        deltas_ref[:near] = in_order(core, delta_refs[0][...], delta_refs[1][...])
        deltas_ref[near:] = in_order(core, delta_refs[2][...], delta_refs[3][...])

    feats = rows_ref[:, pl.ds(pl.multiple_of(step * tile, tile), tile)]
    gate_ref[...] = contract_rows(feats, deltas_ref[:, hidden_units:2 * hidden_units])
    up_ref[...] = contract_rows(feats, deltas_ref[:, 2 * hidden_units:])
    hidden = deltas_ref[:, pl.ds(pl.multiple_of(step * down_tile, down_tile), down_tile)]
    down_ref[...] = contract_rows(hidden, rows_ref[:, width:])


def token_grad_kernel(chosen_ref, returned_ref, out_ref):
    out_ref[...] = contract_rows(chosen_ref[...], returned_ref[...]).astype(jnp.bfloat16)


def body_by_all_to_all(tokens, cotangent, expert_ids, route_weights, gate_weight, up_weight, down_weight):
    owners = lax.axis_size("expert")
    width_parts = lax.axis_size("dp")
    tok_rows, top_count = expert_ids.shape
    width = tokens.shape[1]
    capacity = min(tok_rows, max(2, (tok_rows * top_count + owners - 1) // owners))
    slot_count = owners * capacity
    flat_ids = expert_ids.reshape(-1)
    position = jnp.arange(flat_ids.shape[0], dtype=jnp.int32)
    earlier = (flat_ids[:, None] == flat_ids[None, :]) & (position[None, :] < position[:, None])
    rank_pos = jnp.sum(earlier.astype(jnp.int32), axis=1)
    slot_pos = flat_ids * capacity + rank_pos
    pair_select = (slot_pos[:, None] == jnp.arange(slot_count, dtype=jnp.int32)[None, :]).astype(
        jnp.bfloat16
    )
    chosen = jnp.sum(
        pair_select.reshape(tok_rows, top_count, slot_count).astype(jnp.float32), axis=1
    ).astype(jnp.bfloat16)
    pair_tokens = jnp.repeat(tokens, top_count, axis=0)
    pair_scaled = (
        jnp.repeat(cotangent.astype(jnp.float32), top_count, axis=0) * route_weights
    ).astype(jnp.bfloat16)
    payload = jnp.concatenate([pair_tokens, pair_scaled], axis=1)
    send = contract_rows(pair_select, payload).astype(jnp.bfloat16)
    slots = lax.all_to_all(send, "expert", split_axis=0, concat_axis=0, tiled=True)

    core = lax.axis_index("dp") % 2
    half = slot_count // 2
    mine_slots = lax.dynamic_slice_in_dim(slots, core * half, half, 0)
    other_slots = lax.dynamic_slice_in_dim(slots, (1 - core) * half, half, 0)
    w_gate = gate_weight[0]
    w_up = up_weight[0]
    w_down = down_weight[0]

    def partial_sums(rows):
        feats, cots = rows[:, :width], rows[:, width:]
        return (
            jnp.dot(feats, w_gate, preferred_element_type=jnp.float32),
            jnp.dot(feats, w_up, preferred_element_type=jnp.float32),
            contract_cols(cots, w_down),
        )

    def pack(parts):
        return jnp.stack([part.astype(jnp.bfloat16) for part in parts])

    received = swap(pack(partial_sums(other_slots)), 1)
    sums = jnp.stack(partial_sums(mine_slots)) + received.astype(jnp.float32)
    bit = 2
    while bit < width_parts:
        sums = sums + swap(sums.astype(jnp.bfloat16), bit).astype(jnp.float32)
        bit *= 2
    mine = jnp.stack(local_deltas(sums[0], sums[1], sums[2]))
    other = swap(mine, 1)
    hidden, gate_delta, up_delta = jnp.concatenate([mine, other], axis=1)
    both = jnp.concatenate([mine_slots, other_slots], axis=0)
    slot_grad = (contract_cols(gate_delta, w_gate) + contract_cols(up_delta, w_up)).astype(
        jnp.bfloat16
    )
    slot_grad = jnp.where(
        core == 0, slot_grad, jnp.concatenate([slot_grad[half:], slot_grad[:half]], axis=0)
    )
    returned = lax.all_to_all(slot_grad, "expert", split_axis=0, concat_axis=0, tiled=True)
    feats, cots = both[:, :width], both[:, width:]
    gate_grad = contract_rows(feats, gate_delta)
    up_grad = contract_rows(feats, up_delta)
    down_grad = contract_rows(hidden, cots)
    token_grad = jnp.dot(chosen, returned, preferred_element_type=jnp.float32).astype(jnp.bfloat16)
    return (token_grad, gate_grad[None], up_grad[None], down_grad[None])


def body_by_pairs(tokens, cotangent, expert_ids, route_weights, gate_weight, up_weight, down_weight):
    owners = lax.axis_size("expert")
    width_parts = lax.axis_size("dp")
    tok_rows, _ = expert_ids.shape
    width = tokens.shape[1]
    hidden_units = gate_weight.shape[2]
    capacity = min(tok_rows, max(2, (tok_rows + owners - 1) // owners))
    slot_count = owners * capacity
    half = owners // 2

    far_first = [0] + list(reversed(range(1, half)))
    chosen, own, pair_block, *groups = call(
        functools.partial(dispatch_kernel, owners, capacity),
        (shape(slot_count, tok_rows),)
        + (shape(capacity, 2 * width),) * 2
        + (shape(2 * capacity, 2 * width),) * (half - 1),
        expert_ids.reshape(1, tok_rows),
        route_weights.reshape(1, tok_rows),
        tokens,
        cotangent,
        far=range(4),
        scratch=[
            pltpu.VMEM((1, tok_rows), jnp.int32),
            pltpu.VMEM((1, tok_rows), jnp.float32),
            pltpu.VMEM((tok_rows, width), jnp.bfloat16),
            pltpu.VMEM((tok_rows, width), jnp.bfloat16),
            pltpu.SemaphoreType.DMA((4,)),
        ],
    )
    weights = call(
        load_kernel,
        (shape(width, hidden_units), shape(width, hidden_units), shape(hidden_units, width)),
        gate_weight[0],
        up_weight[0],
        down_weight[0],
        chosen,
        far=range(3),
        scratch=[pltpu.SemaphoreType.DMA((3,))],
        cost=10**7,
    )
    groups = [swap(groups[j - 1], 2 * j, "expert") for j in far_first[1:]]
    from_pair = swap(pair_block, 1, "expert")
    groups = after(groups, from_pair)
    seconds = jnp.concatenate([group[capacity:] for group in groups], axis=0)
    by_pair = swap(after(seconds, weights[2]), 1, "expert")

    order = [0] + [2 * j for j in far_first[1:]] + [1] + [2 * j + 1 for j in far_first[1:]]

    near = [own, from_pair] + groups
    held = []
    for rows, count, cost in ((near, half + 1, 1), ([by_pair], half - 1, FAR_PRODUCTS_COST)):
        part = count * capacity // 2
        packed = shape(part, 3 * hidden_units)
        wide = shape(part, 3 * hidden_units, jnp.float32)
        mine, other = call(products_kernel, (wide, packed), *rows, *weights, cost=cost)
        sums, marker = call(sums_kernel, (wide, packed), mine, swap(other, 1))
        bit = 2
        while 2 * bit < width_parts:
            sums, marker = call(sums_kernel, (wide, packed), sums, swap(marker, bit))
            bit *= 2
        held.append((sums, swap(marker, bit), packed))
    deltas, grads = [], []
    for sums, received, packed in held:
        mine = call(deltas_kernel, packed, sums, received, cost=FAR_DELTAS_COST if deltas else 1)
        if deltas:
            mine = after(mine, deltas[1])
        pair = [mine, swap(mine, 1)]
        deltas += pair
        grads = [
            call(
                functools.partial(slot_grad_kernel, order),
                shape(slot_count if grads else 2 * packed.shape[0], width),
                *pair,
                *weights[:2],
                *grads,
            )
        ]
    returned = lax.all_to_all(grads[0], "expert", split_axis=0, concat_axis=0, tiled=True)
    steps = 4 if width % 512 == 0 else 1
    down_tile = -(-hidden_units // (128 * steps)) * 128
    gate_grad, up_grad, down_grad = pl.pallas_call(
        weight_grads_kernel,
        out_shape=(
            shape(width, hidden_units, jnp.float32),
            shape(width, hidden_units, jnp.float32),
            shape(hidden_units, width, jnp.float32),
        ),
        grid=(steps,),
        in_specs=[pl.BlockSpec(memory_space=pltpu.VMEM)] * (len(near) + 1 + 4),
        out_specs=(
            pl.BlockSpec((width // steps, hidden_units), lambda i: (i, 0)),
            pl.BlockSpec((width // steps, hidden_units), lambda i: (i, 0)),
            pl.BlockSpec((down_tile, width), lambda i: (i, 0)),
        ),
        scratch_shapes=[
            pltpu.VMEM((slot_count, 2 * width), jnp.bfloat16),
            pltpu.VMEM((slot_count, 3 * hidden_units), jnp.bfloat16),
        ],
        compiler_params=pltpu.CompilerParams(vmem_limit_bytes=24 * 1024 * 1024),
        cost_estimate=pl.CostEstimate(flops=10**7, bytes_accessed=10**7, transcendentals=0),
    )(*near, by_pair, *deltas)
    token_grad = call(token_grad_kernel, shape(tok_rows, width), chosen, returned)
    return (token_grad, gate_grad[None], up_grad[None], down_grad[None])


def body(tokens, cotangent, expert_ids, *rest):
    owners = lax.axis_size("expert")
    width_parts = lax.axis_size("dp")
    tok_rows, top_count = expert_ids.shape
    by_pairs = (
        top_count == 1
        and owners >= 8
        and owners & (owners - 1) == 0
        and width_parts >= 4
        and tok_rows % (16 * owners) == 0
    )
    chosen = body_by_pairs if by_pairs else body_by_all_to_all
    return chosen(tokens, cotangent, expert_ids, *rest)


def solution(mesh):
    return jax.shard_map(
        body,
        mesh=mesh,
        in_specs=(
            P("expert", "dp"),
            P("expert", "dp"),
            P("expert", None),
            P("expert", None),
            P("expert", "dp", None),
            P("expert", "dp", None),
            P("expert", None, "dp"),
        ),
        out_specs=(
            P("expert", "dp"),
            P("expert", "dp", None),
            P("expert", "dp", None),
            P("expert", None, "dp"),
        ),
        check_vma=False,
    )
```

```python
import functools

import jax
import jax.numpy as jnp
from jax import lax
from jax.experimental import pallas as pl
from jax.experimental.pallas import tpu as pltpu
from jax.sharding import PartitionSpec as P


def contract_rows(left, right):
    return lax.dot_general(
        left, right, (((0,), (0,)), ((), ())), preferred_element_type=jnp.float32
    )


def contract_cols(left, right):
    return lax.dot_general(
        left, right, (((1,), (1,)), ((), ())), preferred_element_type=jnp.float32
    )


def local_deltas(gate_pre, up_pre, hidden_grad):
    sigma = jax.nn.sigmoid(gate_pre)
    activated = gate_pre * sigma
    hidden = (activated * up_pre).astype(jnp.bfloat16)
    gate_delta = (hidden_grad * up_pre * sigma * (1.0 + gate_pre * (1.0 - sigma))).astype(
        jnp.bfloat16
    )
    up_delta = (hidden_grad * activated).astype(jnp.bfloat16)
    return (hidden, gate_delta, up_delta)


def swap(value, bit, axis="dp"):
    size = lax.axis_size(axis)
    return lax.ppermute(value, axis, [(i, i ^ bit) for i in range(size)])


FAR_PRODUCTS_COST = 10**9
FAR_DELTAS_COST = 16 * 10**8


def after(values, marker):
    return lax.optimization_barrier((values, marker))[0]


def call(kernel, outs, *args, cost=1, far=(), scratch=()):
    spaces = [pltpu.HBM if place in far else pltpu.VMEM for place in range(len(args))]
    args = [
        pltpu.with_memory_space_constraint(arg, pltpu.HBM) if place in far else arg
        for place, arg in enumerate(args)
    ]
    return pl.pallas_call(
        kernel,
        out_shape=outs,
        in_specs=[pl.BlockSpec(memory_space=space) for space in spaces],
        scratch_shapes=scratch,
        compiler_params=pltpu.CompilerParams(vmem_limit_bytes=24 * 1024 * 1024),
        cost_estimate=pl.CostEstimate(flops=cost, bytes_accessed=cost, transcendentals=0),
    )(*args)


def shape(rows, cols, dtype=jnp.bfloat16):
    return jax.ShapeDtypeStruct((rows, cols), dtype)


def dispatch_kernel(owners, capacity, ids_hbm, weights_hbm, tokens_hbm, cotangent_hbm, *refs):
    chosen_ref, *out_refs, ids_ref, weights_ref, tokens_ref, cotangent_ref, sems = refs
    copies = [
        pltpu.make_async_copy(source, target, sems.at[place])
        for place, (source, target) in enumerate(
            (
                (ids_hbm, ids_ref),
                (weights_hbm, weights_ref),
                (tokens_hbm, tokens_ref),
                (cotangent_hbm, cotangent_ref),
            )
        )
    ]
    for copy in copies:
        copy.start()
    copies[0].wait()
    pairs = ids_ref.shape[1]
    width = tokens_ref.shape[1]
    slot_count = owners * capacity
    me = lax.axis_index("expert")
    ids = ids_ref[...]
    named = ids == lax.broadcasted_iota(jnp.int32, (owners, pairs), 0)
    before = lax.broadcasted_iota(jnp.int32, (pairs, pairs), 0) < lax.broadcasted_iota(
        jnp.int32, (pairs, pairs), 1
    )
    named = named.astype(jnp.float32)
    counts = jnp.dot(
        named.astype(jnp.bfloat16),
        before.astype(jnp.float32).astype(jnp.bfloat16),
        preferred_element_type=jnp.float32,
    )
    rank = jnp.sum(named * counts, axis=0, keepdims=True).astype(jnp.int32)
    slots = lax.broadcasted_iota(jnp.int32, (slot_count, pairs), 0)
    chosen_ref[...] = (slots == ids * capacity + rank).astype(jnp.float32).astype(jnp.bfloat16)
    chosen = (slots == (ids ^ me) * capacity + rank).astype(jnp.float32)
    select = chosen.astype(jnp.bfloat16)
    for copy in copies[1:]:
        copy.wait()
    scale = jnp.sum(chosen * weights_ref[...], axis=1, keepdims=True)
    feats = jnp.dot(select, tokens_ref[...], preferred_element_type=jnp.float32)
    cots = jnp.dot(select, cotangent_ref[...], preferred_element_type=jnp.float32) * scale
    at = 0
    for out_ref in out_refs:
        rows = slice(at, at + out_ref.shape[0])
        out_ref[:, :width] = feats[rows].astype(jnp.bfloat16)
        out_ref[:, width:] = cots[rows].astype(jnp.bfloat16)
        at += out_ref.shape[0]


def load_kernel(gate_hbm, up_hbm, down_hbm, marker_hbm, gate_ref, up_ref, down_ref, sems):
    copies = [
        pltpu.make_async_copy(source, target, sems.at[place])
        for place, (source, target) in enumerate(
            ((gate_hbm, gate_ref), (up_hbm, up_ref), (down_hbm, down_ref))
        )
    ]
    for copy in copies:
        copy.start()
    for copy in copies:
        copy.wait()


def turn_kernel(*refs):
    for source, target in zip(refs[:3], refs[3:]):
        target[...] = source[...].T


def near_rows(own_ref, from_pair_ref, *group_refs):
    halves = [ref[:ref.shape[0] // 2] for ref in group_refs]
    return jnp.concatenate([own_ref[...]] + halves + [from_pair_ref[...]], axis=0)


def products_kernel(turned, *refs):
    *row_refs, gate_ref, up_ref, down_ref, mine_ref, other_ref = refs
    rows = near_rows(*row_refs) if len(row_refs) > 1 else row_refs[0][...]
    half = rows.shape[0] // 2
    width = rows.shape[1] // 2
    hidden_units = gate_ref.shape[1]
    core = lax.axis_index("dp") % 2
    feats, cots = rows[:, :width], rows[:, width:]
    for place, weight_ref in enumerate((gate_ref, up_ref, down_ref)):
        cols = slice(place * hidden_units, (place + 1) * hidden_units)
        rows = feats if place < 2 else cots
        if place < 2 or turned:
            out = jnp.dot(rows, weight_ref[...], preferred_element_type=jnp.float32)
        else:
            out = contract_cols(rows, weight_ref[...])
        low, high = out[:half], out[half:]
        mine_ref[:, cols] = jnp.where(core == 0, low, high)
        other_ref[:, cols] = jnp.where(core == 0, high, low).astype(jnp.bfloat16)


def sums_kernel(mine_ref, received_ref, sums_ref, packed_ref):
    sums = mine_ref[...] + received_ref[...].astype(jnp.float32)
    sums_ref[...] = sums
    packed_ref[...] = sums.astype(jnp.bfloat16)


def deltas_kernel(sums_ref, received_ref, out_ref):
    hidden_units = sums_ref.shape[1] // 3
    cols = [slice(i * hidden_units, (i + 1) * hidden_units) for i in range(3)]
    parts = [sums_ref[:, c] + received_ref[:, c].astype(jnp.float32) for c in cols]
    for c, part in zip(cols, local_deltas(*parts)):
        out_ref[:, c] = part


def in_order(core, mine, other):
    return jnp.concatenate(
        [jnp.where(core == 0, mine, other), jnp.where(core == 0, other, mine)], axis=0
    )


def slot_grad_kernel(order, mine_ref, other_ref, gate_ref, up_ref, *refs):
    *earlier_ref, out_ref = refs
    hidden_units = gate_ref.shape[0]
    rows = in_order(lax.axis_index("dp") % 2, mine_ref[...], other_ref[...])
    by_gate, by_up = rows[:, hidden_units:2 * hidden_units], rows[:, 2 * hidden_units:]
    out = (
        jnp.dot(by_gate, gate_ref[...], preferred_element_type=jnp.float32)
        + jnp.dot(by_up, up_ref[...], preferred_element_type=jnp.float32)
    ).astype(jnp.bfloat16)
    if not earlier_ref:
        out_ref[...] = out
        return
    me = lax.axis_index("expert")
    block = out_ref.shape[0] // len(order)
    rows = jnp.concatenate([earlier_ref[0][...], out], axis=0)
    for place, k in enumerate(order):
        start = pl.multiple_of((me ^ k) * block, block)
        out_ref[pl.ds(start, block)] = rows[place * block:(place + 1) * block]


def weight_grads_kernel(*refs):
    *in_refs, gate_ref, up_ref, down_ref, rows_ref, deltas_ref = refs
    row_refs, delta_refs = in_refs[:-4], in_refs[-4:]
    step = pl.program_id(0)
    tile = gate_ref.shape[0]
    down_tile = down_ref.shape[0]
    width = rows_ref.shape[1] // 2
    hidden_units = gate_ref.shape[1]

    @pl.when(step == 0)
    def _():
        core = lax.axis_index("dp") % 2
        near = 2 * delta_refs[0].shape[0]
        rows_ref[:near] = near_rows(*row_refs[:-1])
        rows_ref[near:] = row_refs[-1][...]
        deltas_ref[:near] = in_order(core, delta_refs[0][...], delta_refs[1][...])
        deltas_ref[near:] = in_order(core, delta_refs[2][...], delta_refs[3][...])

    feats = rows_ref[:, pl.ds(pl.multiple_of(step * tile, tile), tile)]
    gate_ref[...] = contract_rows(feats, deltas_ref[:, hidden_units:2 * hidden_units])
    up_ref[...] = contract_rows(feats, deltas_ref[:, 2 * hidden_units:])
    hidden = deltas_ref[:, pl.ds(pl.multiple_of(step * down_tile, down_tile), down_tile)]
    down_ref[...] = contract_rows(hidden, rows_ref[:, width:])


def token_grad_kernel(chosen_ref, returned_ref, out_ref):
    out_ref[...] = contract_rows(chosen_ref[...], returned_ref[...]).astype(jnp.bfloat16)


def body_by_all_to_all(tokens, cotangent, expert_ids, route_weights, gate_weight, up_weight, down_weight):
    owners = lax.axis_size("expert")
    width_parts = lax.axis_size("dp")
    tok_rows, top_count = expert_ids.shape
    width = tokens.shape[1]
    capacity = min(tok_rows, max(2, (tok_rows * top_count + owners - 1) // owners))
    slot_count = owners * capacity
    flat_ids = expert_ids.reshape(-1)
    position = jnp.arange(flat_ids.shape[0], dtype=jnp.int32)
    earlier = (flat_ids[:, None] == flat_ids[None, :]) & (position[None, :] < position[:, None])
    rank_pos = jnp.sum(earlier.astype(jnp.int32), axis=1)
    slot_pos = flat_ids * capacity + rank_pos
    pair_select = (slot_pos[:, None] == jnp.arange(slot_count, dtype=jnp.int32)[None, :]).astype(
        jnp.bfloat16
    )
    chosen = jnp.sum(
        pair_select.reshape(tok_rows, top_count, slot_count).astype(jnp.float32), axis=1
    ).astype(jnp.bfloat16)
    pair_tokens = jnp.repeat(tokens, top_count, axis=0)
    pair_scaled = (
        jnp.repeat(cotangent.astype(jnp.float32), top_count, axis=0) * route_weights
    ).astype(jnp.bfloat16)
    payload = jnp.concatenate([pair_tokens, pair_scaled], axis=1)
    send = contract_rows(pair_select, payload).astype(jnp.bfloat16)
    slots = lax.all_to_all(send, "expert", split_axis=0, concat_axis=0, tiled=True)

    core = lax.axis_index("dp") % 2
    half = slot_count // 2
    mine_slots = lax.dynamic_slice_in_dim(slots, core * half, half, 0)
    other_slots = lax.dynamic_slice_in_dim(slots, (1 - core) * half, half, 0)
    w_gate = gate_weight[0]
    w_up = up_weight[0]
    w_down = down_weight[0]

    def partial_sums(rows):
        feats, cots = rows[:, :width], rows[:, width:]
        return (
            jnp.dot(feats, w_gate, preferred_element_type=jnp.float32),
            jnp.dot(feats, w_up, preferred_element_type=jnp.float32),
            contract_cols(cots, w_down),
        )

    def pack(parts):
        return jnp.stack([part.astype(jnp.bfloat16) for part in parts])

    received = swap(pack(partial_sums(other_slots)), 1)
    sums = jnp.stack(partial_sums(mine_slots)) + received.astype(jnp.float32)
    bit = 2
    while bit < width_parts:
        sums = sums + swap(sums.astype(jnp.bfloat16), bit).astype(jnp.float32)
        bit *= 2
    mine = jnp.stack(local_deltas(sums[0], sums[1], sums[2]))
    other = swap(mine, 1)
    hidden, gate_delta, up_delta = jnp.concatenate([mine, other], axis=1)
    both = jnp.concatenate([mine_slots, other_slots], axis=0)
    slot_grad = (contract_cols(gate_delta, w_gate) + contract_cols(up_delta, w_up)).astype(
        jnp.bfloat16
    )
    slot_grad = jnp.where(
        core == 0, slot_grad, jnp.concatenate([slot_grad[half:], slot_grad[:half]], axis=0)
    )
    returned = lax.all_to_all(slot_grad, "expert", split_axis=0, concat_axis=0, tiled=True)
    feats, cots = both[:, :width], both[:, width:]
    gate_grad = contract_rows(feats, gate_delta)
    up_grad = contract_rows(feats, up_delta)
    down_grad = contract_rows(hidden, cots)
    token_grad = jnp.dot(chosen, returned, preferred_element_type=jnp.float32).astype(jnp.bfloat16)
    return (token_grad, gate_grad[None], up_grad[None], down_grad[None])


def body_by_pairs(tokens, cotangent, expert_ids, route_weights, gate_weight, up_weight, down_weight):
    owners = lax.axis_size("expert")
    width_parts = lax.axis_size("dp")
    tok_rows, _ = expert_ids.shape
    width = tokens.shape[1]
    hidden_units = gate_weight.shape[2]
    capacity = min(tok_rows, max(2, (tok_rows + owners - 1) // owners))
    slot_count = owners * capacity
    half = owners // 2

    far_first = [0] + list(reversed(range(1, half)))
    chosen, own, pair_block, *groups = call(
        functools.partial(dispatch_kernel, owners, capacity),
        (shape(slot_count, tok_rows),)
        + (shape(capacity, 2 * width),) * 2
        + (shape(2 * capacity, 2 * width),) * (half - 1),
        expert_ids.reshape(1, tok_rows),
        route_weights.reshape(1, tok_rows),
        tokens,
        cotangent,
        far=range(4),
        scratch=[
            pltpu.VMEM((1, tok_rows), jnp.int32),
            pltpu.VMEM((1, tok_rows), jnp.float32),
            pltpu.VMEM((tok_rows, width), jnp.bfloat16),
            pltpu.VMEM((tok_rows, width), jnp.bfloat16),
            pltpu.SemaphoreType.DMA((4,)),
        ],
    )
    weights = call(
        load_kernel,
        (shape(width, hidden_units), shape(width, hidden_units), shape(hidden_units, width)),
        gate_weight[0],
        up_weight[0],
        down_weight[0],
        chosen,
        far=range(3),
        scratch=[pltpu.SemaphoreType.DMA((3,))],
        cost=10**7,
    )
    groups = [swap(groups[j - 1], 2 * j, "expert") for j in far_first[1:]]
    from_pair = swap(pair_block, 1, "expert")
    groups = after(groups, from_pair)
    seconds = jnp.concatenate([group[capacity:] for group in groups], axis=0)
    by_pair = swap(after(seconds, weights[2]), 1, "expert")

    order = [0] + [2 * j for j in far_first[1:]] + [1] + [2 * j + 1 for j in far_first[1:]]

    turned = call(
        turn_kernel,
        (shape(hidden_units, width), shape(hidden_units, width), shape(width, hidden_units)),
        *after(weights, groups[0]),
    )
    far = after(by_pair, turned[0])
    near = [own, from_pair] + groups
    held = []
    for rows, count, down, cost in (
        (near, half + 1, weights[2], 1),
        ([far], half - 1, turned[2], FAR_PRODUCTS_COST),
    ):
        part = count * capacity // 2
        packed = shape(part, 3 * hidden_units)
        wide = shape(part, 3 * hidden_units, jnp.float32)
        mine, other = call(
            functools.partial(products_kernel, down is turned[2]),
            (wide, packed),
            *rows,
            *weights[:2],
            down,
            cost=cost,
        )
        sums, marker = call(sums_kernel, (wide, packed), mine, swap(other, 1))
        bit = 2
        while 2 * bit < width_parts:
            sums, marker = call(sums_kernel, (wide, packed), sums, swap(marker, bit))
            bit *= 2
        held.append((sums, swap(marker, bit), packed))
    deltas, grads = [], []
    for sums, received, packed in held:
        mine = call(deltas_kernel, packed, sums, received, cost=FAR_DELTAS_COST if deltas else 1)
        if deltas:
            mine = after(mine, deltas[1])
        pair = [mine, swap(mine, 1)]
        deltas += pair
        grads = [
            call(
                functools.partial(slot_grad_kernel, order),
                shape(slot_count if grads else 2 * packed.shape[0], width),
                *pair,
                *turned[:2],
                *grads,
            )
        ]
    returned = lax.all_to_all(grads[0], "expert", split_axis=0, concat_axis=0, tiled=True)
    steps = 4 if width % 512 == 0 else 1
    down_tile = -(-hidden_units // (128 * steps)) * 128
    gate_grad, up_grad, down_grad = pl.pallas_call(
        weight_grads_kernel,
        out_shape=(
            shape(width, hidden_units, jnp.float32),
            shape(width, hidden_units, jnp.float32),
            shape(hidden_units, width, jnp.float32),
        ),
        grid=(steps,),
        in_specs=[pl.BlockSpec(memory_space=pltpu.VMEM)] * (len(near) + 1 + 4),
        out_specs=(
            pl.BlockSpec((width // steps, hidden_units), lambda i: (i, 0)),
            pl.BlockSpec((width // steps, hidden_units), lambda i: (i, 0)),
            pl.BlockSpec((down_tile, width), lambda i: (i, 0)),
        ),
        scratch_shapes=[
            pltpu.VMEM((slot_count, 2 * width), jnp.bfloat16),
            pltpu.VMEM((slot_count, 3 * hidden_units), jnp.bfloat16),
        ],
        compiler_params=pltpu.CompilerParams(vmem_limit_bytes=24 * 1024 * 1024),
        cost_estimate=pl.CostEstimate(flops=10**7, bytes_accessed=10**7, transcendentals=0),
    )(*near, far, *deltas)
    token_grad = call(token_grad_kernel, shape(tok_rows, width), chosen, returned)
    return (token_grad, gate_grad[None], up_grad[None], down_grad[None])


def body(tokens, cotangent, expert_ids, *rest):
    owners = lax.axis_size("expert")
    width_parts = lax.axis_size("dp")
    tok_rows, top_count = expert_ids.shape
    by_pairs = (
        top_count == 1
        and owners >= 8
        and owners & (owners - 1) == 0
        and width_parts >= 4
        and tok_rows % (16 * owners) == 0
    )
    chosen = body_by_pairs if by_pairs else body_by_all_to_all
    return chosen(tokens, cotangent, expert_ids, *rest)


def solution(mesh):
    return jax.shard_map(
        body,
        mesh=mesh,
        in_specs=(
            P("expert", "dp"),
            P("expert", "dp"),
            P("expert", None),
            P("expert", None),
            P("expert", "dp", None),
            P("expert", "dp", None),
            P("expert", None, "dp"),
        ),
        out_specs=(
            P("expert", "dp"),
            P("expert", "dp", None),
            P("expert", "dp", None),
            P("expert", None, "dp"),
        ),
        check_vma=False,
    )
```

```python
import functools

import jax
import jax.numpy as jnp
from jax import lax
from jax.experimental import pallas as pl
from jax.experimental.pallas import tpu as pltpu
from jax.sharding import PartitionSpec as P


def contract_rows(left, right):
    return lax.dot_general(
        left, right, (((0,), (0,)), ((), ())), preferred_element_type=jnp.float32
    )


def contract_cols(left, right):
    return lax.dot_general(
        left, right, (((1,), (1,)), ((), ())), preferred_element_type=jnp.float32
    )


def local_deltas(gate_pre, up_pre, hidden_grad):
    sigma = jax.nn.sigmoid(gate_pre)
    activated = gate_pre * sigma
    hidden = (activated * up_pre).astype(jnp.bfloat16)
    gate_delta = (hidden_grad * up_pre * sigma * (1.0 + gate_pre * (1.0 - sigma))).astype(
        jnp.bfloat16
    )
    up_delta = (hidden_grad * activated).astype(jnp.bfloat16)
    return (hidden, gate_delta, up_delta)


def swap(value, bit, axis="dp"):
    size = lax.axis_size(axis)
    return lax.ppermute(value, axis, [(i, i ^ bit) for i in range(size)])


FAR_PRODUCTS_COST = 10**9
FAR_DELTAS_COST = 16 * 10**8


def after(values, marker):
    return lax.optimization_barrier((values, marker))[0]


def call(kernel, outs, *args, cost=1, far=(), scratch=()):
    spaces = [pltpu.HBM if place in far else pltpu.VMEM for place in range(len(args))]
    args = [
        pltpu.with_memory_space_constraint(arg, pltpu.HBM) if place in far else arg
        for place, arg in enumerate(args)
    ]
    return pl.pallas_call(
        kernel,
        out_shape=outs,
        in_specs=[pl.BlockSpec(memory_space=space) for space in spaces],
        scratch_shapes=scratch,
        compiler_params=pltpu.CompilerParams(vmem_limit_bytes=24 * 1024 * 1024),
        cost_estimate=pl.CostEstimate(flops=cost, bytes_accessed=cost, transcendentals=0),
    )(*args)


def shape(rows, cols, dtype=jnp.bfloat16):
    return jax.ShapeDtypeStruct((rows, cols), dtype)


def dispatch_kernel(owners, capacity, ids_hbm, weights_hbm, tokens_hbm, cotangent_hbm, *refs):
    chosen_ref, *out_refs, ids_ref, weights_ref, tokens_ref, cotangent_ref, sems = refs
    copies = [
        pltpu.make_async_copy(source, target, sems.at[place])
        for place, (source, target) in enumerate(
            (
                (ids_hbm, ids_ref),
                (weights_hbm, weights_ref),
                (tokens_hbm, tokens_ref),
                (cotangent_hbm, cotangent_ref),
            )
        )
    ]
    for copy in copies:
        copy.start()
    copies[0].wait()
    pairs = ids_ref.shape[1]
    width = tokens_ref.shape[1]
    slot_count = owners * capacity
    me = lax.axis_index("expert")
    ids = ids_ref[...]
    named = ids == lax.broadcasted_iota(jnp.int32, (owners, pairs), 0)
    before = lax.broadcasted_iota(jnp.int32, (pairs, pairs), 0) < lax.broadcasted_iota(
        jnp.int32, (pairs, pairs), 1
    )
    named = named.astype(jnp.float32)
    counts = jnp.dot(
        named.astype(jnp.bfloat16),
        before.astype(jnp.float32).astype(jnp.bfloat16),
        preferred_element_type=jnp.float32,
    )
    rank = jnp.sum(named * counts, axis=0, keepdims=True).astype(jnp.int32)
    slots = lax.broadcasted_iota(jnp.int32, (slot_count, pairs), 0)
    chosen = (slots == (ids ^ me) * capacity + rank).astype(jnp.float32)
    select = chosen.astype(jnp.bfloat16)
    chosen_ref[...] = select
    for copy in copies[1:]:
        copy.wait()
    scale = jnp.sum(chosen * weights_ref[...], axis=1, keepdims=True)
    feats = jnp.dot(select, tokens_ref[...], preferred_element_type=jnp.float32)
    cots = jnp.dot(select, cotangent_ref[...], preferred_element_type=jnp.float32) * scale
    at = 0
    for out_ref in out_refs:
        rows = slice(at, at + out_ref.shape[0])
        out_ref[:, :width] = feats[rows].astype(jnp.bfloat16)
        out_ref[:, width:] = cots[rows].astype(jnp.bfloat16)
        at += out_ref.shape[0]


def load_kernel(gate_hbm, up_hbm, down_hbm, marker_hbm, gate_ref, up_ref, down_ref, sems):
    copies = [
        pltpu.make_async_copy(source, target, sems.at[place])
        for place, (source, target) in enumerate(
            ((gate_hbm, gate_ref), (up_hbm, up_ref), (down_hbm, down_ref))
        )
    ]
    for copy in copies:
        copy.start()
    for copy in copies:
        copy.wait()


def turn_kernel(*refs):
    for source, target in zip(refs[:3], refs[3:]):
        target[...] = source[...].T


def near_rows(own_ref, from_pair_ref, *group_refs):
    halves = [ref[:ref.shape[0] // 2] for ref in group_refs]
    return jnp.concatenate([own_ref[...]] + halves + [from_pair_ref[...]], axis=0)


def products_kernel(turned, *refs):
    *row_refs, gate_ref, up_ref, down_ref, mine_ref, other_ref = refs
    rows = near_rows(*row_refs) if len(row_refs) > 1 else row_refs[0][...]
    half = rows.shape[0] // 2
    width = rows.shape[1] // 2
    hidden_units = gate_ref.shape[1]
    core = lax.axis_index("dp") % 2
    feats, cots = rows[:, :width], rows[:, width:]
    for place, weight_ref in enumerate((gate_ref, up_ref, down_ref)):
        cols = slice(place * hidden_units, (place + 1) * hidden_units)
        rows = feats if place < 2 else cots
        if place < 2 or turned:
            out = jnp.dot(rows, weight_ref[...], preferred_element_type=jnp.float32)
        else:
            out = contract_cols(rows, weight_ref[...])
        low, high = out[:half], out[half:]
        mine_ref[:, cols] = jnp.where(core == 0, low, high)
        other_ref[:, cols] = jnp.where(core == 0, high, low).astype(jnp.bfloat16)


def sums_kernel(mine_ref, received_ref, sums_ref, packed_ref):
    sums = mine_ref[...] + received_ref[...].astype(jnp.float32)
    sums_ref[...] = sums
    packed_ref[...] = sums.astype(jnp.bfloat16)


def deltas_kernel(sums_ref, received_ref, out_ref):
    hidden_units = sums_ref.shape[1] // 3
    cols = [slice(i * hidden_units, (i + 1) * hidden_units) for i in range(3)]
    parts = [sums_ref[:, c] + received_ref[:, c].astype(jnp.float32) for c in cols]
    for c, part in zip(cols, local_deltas(*parts)):
        out_ref[:, c] = part


def in_order(core, mine, other):
    return jnp.concatenate(
        [jnp.where(core == 0, mine, other), jnp.where(core == 0, other, mine)], axis=0
    )


def slot_grad_rows(mine_ref, other_ref, gate_ref, up_ref):
    hidden_units = gate_ref.shape[0]
    rows = in_order(lax.axis_index("dp") % 2, mine_ref[...], other_ref[...])
    by_gate, by_up = rows[:, hidden_units:2 * hidden_units], rows[:, 2 * hidden_units:]
    return (
        jnp.dot(by_gate, gate_ref[...], preferred_element_type=jnp.float32)
        + jnp.dot(by_up, up_ref[...], preferred_element_type=jnp.float32)
    ).astype(jnp.bfloat16)


def near_grad_kernel(mine_ref, other_ref, gate_ref, up_ref, *block_refs):
    out = slot_grad_rows(mine_ref, other_ref, gate_ref, up_ref)
    block = block_refs[0].shape[0]
    for place, ref in enumerate(block_refs):
        ref[...] = out[place * block:(place + 1) * block]


def far_grad_kernel(mine_ref, other_ref, gate_ref, up_ref, pair_ref, out_ref):
    block = pair_ref.shape[0]
    out_ref[:block] = pair_ref[...]
    out_ref[block:] = slot_grad_rows(mine_ref, other_ref, gate_ref, up_ref)


def weight_grads_kernel(names, tiles, *refs):
    outs = len(names)
    *in_refs, rows_ref, deltas_ref, sems = refs
    in_refs, out_refs, tile_refs = in_refs[:-2 * outs], in_refs[-2 * outs:-outs], in_refs[-outs:]
    row_refs, delta_refs = in_refs[:-4], in_refs[-4:]
    width = rows_ref.shape[1] // 2
    hidden_units = deltas_ref.shape[1] // 3
    core = lax.axis_index("dp") % 2
    near = 2 * delta_refs[0].shape[0]
    rows_ref[:near] = near_rows(*row_refs[:-1])
    rows_ref[near:] = row_refs[-1][...]
    deltas_ref[:near] = in_order(core, delta_refs[0][...], delta_refs[1][...])
    deltas_ref[near:] = in_order(core, delta_refs[2][...], delta_refs[3][...])

    copies = []
    for name, tile, out_ref, tile_ref in zip(names, tiles, out_refs, tile_refs):
        for at in range(0, out_ref.shape[0], tile):
            rows = min(tile, out_ref.shape[0] - at)
            if name == "down":
                out = contract_rows(deltas_ref[:, at:at + rows], rows_ref[:, width:])
            else:
                start = hidden_units * (1 if name == "gate" else 2)
                out = contract_rows(
                    rows_ref[:, at:at + rows], deltas_ref[:, start:start + hidden_units]
                )
            tile_ref[at:at + rows] = out
            span = pl.ds(at, rows)
            copies.append(
                pltpu.make_async_copy(tile_ref.at[span], out_ref.at[span], sems.at[len(copies)])
            )
            copies[-1].start()
    for copy in copies:
        copy.wait()


def weight_grads(names, width, hidden_units, slot_count, inputs):
    sizes = {"gate": (width, hidden_units), "up": (width, hidden_units), "down": (hidden_units, width)}
    outs = [shape(*sizes[name], jnp.float32) for name in names]
    tiles = [384 if name == "down" else 128 for name in names]
    copies = sum(-(-out.shape[0] // tile) for out, tile in zip(outs, tiles))
    return pl.pallas_call(
        functools.partial(weight_grads_kernel, names, tiles),
        out_shape=outs,
        in_specs=[pl.BlockSpec(memory_space=pltpu.VMEM)] * len(inputs),
        out_specs=[pl.BlockSpec(memory_space=pltpu.HBM)] * len(outs),
        scratch_shapes=[pltpu.VMEM(out.shape, out.dtype) for out in outs]
        + [
            pltpu.VMEM((slot_count, 2 * width), jnp.bfloat16),
            pltpu.VMEM((slot_count, 3 * hidden_units), jnp.bfloat16),
            pltpu.SemaphoreType.DMA((copies,)),
        ],
        compiler_params=pltpu.CompilerParams(vmem_limit_bytes=24 * 1024 * 1024),
        cost_estimate=pl.CostEstimate(flops=10**7, bytes_accessed=10**7, transcendentals=0),
    )(*inputs)


def token_grad_kernel(chosen_ref, own_ref, from_pair_ref, *refs):
    *group_refs, out_ref = refs
    block = own_ref.shape[0]
    rows = [own_ref[...], from_pair_ref[:block]] + [ref[...] for ref in reversed(group_refs)]
    returned = jnp.concatenate(rows, axis=0)
    out_ref[...] = contract_rows(chosen_ref[...], returned).astype(jnp.bfloat16)


def body_by_all_to_all(tokens, cotangent, expert_ids, route_weights, gate_weight, up_weight, down_weight):
    owners = lax.axis_size("expert")
    width_parts = lax.axis_size("dp")
    tok_rows, top_count = expert_ids.shape
    width = tokens.shape[1]
    capacity = min(tok_rows, max(2, (tok_rows * top_count + owners - 1) // owners))
    slot_count = owners * capacity
    flat_ids = expert_ids.reshape(-1)
    position = jnp.arange(flat_ids.shape[0], dtype=jnp.int32)
    earlier = (flat_ids[:, None] == flat_ids[None, :]) & (position[None, :] < position[:, None])
    rank_pos = jnp.sum(earlier.astype(jnp.int32), axis=1)
    slot_pos = flat_ids * capacity + rank_pos
    pair_select = (slot_pos[:, None] == jnp.arange(slot_count, dtype=jnp.int32)[None, :]).astype(
        jnp.bfloat16
    )
    chosen = jnp.sum(
        pair_select.reshape(tok_rows, top_count, slot_count).astype(jnp.float32), axis=1
    ).astype(jnp.bfloat16)
    pair_tokens = jnp.repeat(tokens, top_count, axis=0)
    pair_scaled = (
        jnp.repeat(cotangent.astype(jnp.float32), top_count, axis=0) * route_weights
    ).astype(jnp.bfloat16)
    payload = jnp.concatenate([pair_tokens, pair_scaled], axis=1)
    send = contract_rows(pair_select, payload).astype(jnp.bfloat16)
    slots = lax.all_to_all(send, "expert", split_axis=0, concat_axis=0, tiled=True)

    core = lax.axis_index("dp") % 2
    half = slot_count // 2
    mine_slots = lax.dynamic_slice_in_dim(slots, core * half, half, 0)
    other_slots = lax.dynamic_slice_in_dim(slots, (1 - core) * half, half, 0)
    w_gate = gate_weight[0]
    w_up = up_weight[0]
    w_down = down_weight[0]

    def partial_sums(rows):
        feats, cots = rows[:, :width], rows[:, width:]
        return (
            jnp.dot(feats, w_gate, preferred_element_type=jnp.float32),
            jnp.dot(feats, w_up, preferred_element_type=jnp.float32),
            contract_cols(cots, w_down),
        )

    def pack(parts):
        return jnp.stack([part.astype(jnp.bfloat16) for part in parts])

    received = swap(pack(partial_sums(other_slots)), 1)
    sums = jnp.stack(partial_sums(mine_slots)) + received.astype(jnp.float32)
    bit = 2
    while bit < width_parts:
        sums = sums + swap(sums.astype(jnp.bfloat16), bit).astype(jnp.float32)
        bit *= 2
    mine = jnp.stack(local_deltas(sums[0], sums[1], sums[2]))
    other = swap(mine, 1)
    hidden, gate_delta, up_delta = jnp.concatenate([mine, other], axis=1)
    both = jnp.concatenate([mine_slots, other_slots], axis=0)
    slot_grad = (contract_cols(gate_delta, w_gate) + contract_cols(up_delta, w_up)).astype(
        jnp.bfloat16
    )
    slot_grad = jnp.where(
        core == 0, slot_grad, jnp.concatenate([slot_grad[half:], slot_grad[:half]], axis=0)
    )
    returned = lax.all_to_all(slot_grad, "expert", split_axis=0, concat_axis=0, tiled=True)
    feats, cots = both[:, :width], both[:, width:]
    gate_grad = contract_rows(feats, gate_delta)
    up_grad = contract_rows(feats, up_delta)
    down_grad = contract_rows(hidden, cots)
    token_grad = jnp.dot(chosen, returned, preferred_element_type=jnp.float32).astype(jnp.bfloat16)
    return (token_grad, gate_grad[None], up_grad[None], down_grad[None])


def body_by_pairs(tokens, cotangent, expert_ids, route_weights, gate_weight, up_weight, down_weight):
    owners = lax.axis_size("expert")
    width_parts = lax.axis_size("dp")
    tok_rows, _ = expert_ids.shape
    width = tokens.shape[1]
    hidden_units = gate_weight.shape[2]
    capacity = min(tok_rows, max(2, (tok_rows + owners - 1) // owners))
    slot_count = owners * capacity
    half = owners // 2

    far_first = [0] + list(reversed(range(1, half)))
    chosen, own, pair_block, *groups = call(
        functools.partial(dispatch_kernel, owners, capacity),
        (shape(slot_count, tok_rows),)
        + (shape(capacity, 2 * width),) * 2
        + (shape(2 * capacity, 2 * width),) * (half - 1),
        expert_ids.reshape(1, tok_rows),
        route_weights.reshape(1, tok_rows),
        tokens,
        cotangent,
        far=range(4),
        scratch=[
            pltpu.VMEM((1, tok_rows), jnp.int32),
            pltpu.VMEM((1, tok_rows), jnp.float32),
            pltpu.VMEM((tok_rows, width), jnp.bfloat16),
            pltpu.VMEM((tok_rows, width), jnp.bfloat16),
            pltpu.SemaphoreType.DMA((4,)),
        ],
    )
    weights = call(
        load_kernel,
        (shape(width, hidden_units), shape(width, hidden_units), shape(hidden_units, width)),
        gate_weight[0],
        up_weight[0],
        down_weight[0],
        chosen,
        far=range(3),
        scratch=[pltpu.SemaphoreType.DMA((3,))],
        cost=10**7,
    )
    groups = [swap(groups[j - 1], 2 * j, "expert") for j in far_first[1:]]
    from_pair = swap(pair_block, 1, "expert")
    groups = after(groups, from_pair)
    seconds = jnp.concatenate([group[capacity:] for group in groups], axis=0)
    by_pair = swap(after(seconds, weights[2]), 1, "expert")

    turned = call(
        turn_kernel,
        (shape(hidden_units, width), shape(hidden_units, width), shape(width, hidden_units)),
        *after(weights, groups[0]),
    )
    far = after(by_pair, turned[0])
    near = [own, from_pair] + groups
    held = []
    for rows, count, down, cost in (
        (near, half + 1, weights[2], 1),
        ([far], half - 1, turned[2], FAR_PRODUCTS_COST),
    ):
        part = count * capacity // 2
        packed = shape(part, 3 * hidden_units)
        wide = shape(part, 3 * hidden_units, jnp.float32)
        mine, other = call(
            functools.partial(products_kernel, down is turned[2]),
            (wide, packed),
            *rows,
            *weights[:2],
            down,
            cost=cost,
        )
        sums, marker = call(sums_kernel, (wide, packed), mine, swap(other, 1))
        bit = 2
        while 2 * bit < width_parts:
            sums, marker = call(sums_kernel, (wide, packed), sums, swap(marker, bit))
            bit *= 2
        held.append((sums, swap(marker, bit), packed))
    deltas, grads = [], []
    for sums, received, packed in held:
        mine = call(deltas_kernel, packed, sums, received, cost=FAR_DELTAS_COST if deltas else 1)
        if deltas:
            mine = after(mine, deltas[1])
        pair = [mine, swap(mine, 1)]
        deltas += pair
        block = shape(capacity, width)
        if grads:
            to_pair = call(
                far_grad_kernel, shape(half * capacity, width), *pair, *turned[:2], grads[-1]
            )
        else:
            grads = call(near_grad_kernel, (block,) * (half + 1), *pair, *turned[:2])

    returned_pair = swap(to_pair, 1, "expert")
    sizes = (width, hidden_units, slot_count, (*near, far, *deltas))
    (gate_grad,) = weight_grads(("gate",), *sizes)
    returned_pair = after(returned_pair, gate_grad)
    returned = {}
    for place, j in enumerate(far_first[1:], 1):
        more = returned_pair[place * capacity:(place + 1) * capacity]
        returned[j] = swap(jnp.concatenate([grads[place], more], axis=0), 2 * j, "expert")
    up_grad, down_grad = weight_grads(("up", "down"), *sizes)
    token_grad = call(
        token_grad_kernel,
        shape(tok_rows, width),
        chosen,
        grads[0],
        returned_pair,
        *[returned[j] for j in far_first[1:]],
    )
    return (token_grad, gate_grad[None], up_grad[None], down_grad[None])


def body(tokens, cotangent, expert_ids, *rest):
    owners = lax.axis_size("expert")
    width_parts = lax.axis_size("dp")
    tok_rows, top_count = expert_ids.shape
    by_pairs = (
        top_count == 1
        and owners >= 8
        and owners & (owners - 1) == 0
        and width_parts >= 4
        and tok_rows % (16 * owners) == 0
    )
    chosen = body_by_pairs if by_pairs else body_by_all_to_all
    return chosen(tokens, cotangent, expert_ids, *rest)


def solution(mesh):
    return jax.shard_map(
        body,
        mesh=mesh,
        in_specs=(
            P("expert", "dp"),
            P("expert", "dp"),
            P("expert", None),
            P("expert", None),
            P("expert", "dp", None),
            P("expert", "dp", None),
            P("expert", None, "dp"),
        ),
        out_specs=(
            P("expert", "dp"),
            P("expert", "dp", None),
            P("expert", "dp", None),
            P("expert", None, "dp"),
        ),
        check_vma=False,
    )
```

```python
import functools

import jax
import jax.numpy as jnp
from jax import lax
from jax.experimental import pallas as pl
from jax.experimental.pallas import tpu as pltpu
from jax.sharding import PartitionSpec as P


def contract_rows(left, right):
    return lax.dot_general(
        left, right, (((0,), (0,)), ((), ())), preferred_element_type=jnp.float32
    )


def contract_cols(left, right):
    return lax.dot_general(
        left, right, (((1,), (1,)), ((), ())), preferred_element_type=jnp.float32
    )


def local_deltas(gate_pre, up_pre, hidden_grad):
    sigma = jax.nn.sigmoid(gate_pre)
    activated = gate_pre * sigma
    hidden = (activated * up_pre).astype(jnp.bfloat16)
    gate_delta = (hidden_grad * up_pre * sigma * (1.0 + gate_pre * (1.0 - sigma))).astype(
        jnp.bfloat16
    )
    up_delta = (hidden_grad * activated).astype(jnp.bfloat16)
    return (hidden, gate_delta, up_delta)


def swap(value, bit, axis="dp"):
    size = lax.axis_size(axis)
    return lax.ppermute(value, axis, [(i, i ^ bit) for i in range(size)])


FAR_PRODUCTS_COST = 3 * 10**8
FAR_DELTAS_COST = 8 * 10**8
OWN_DELTAS_COST = 3 * 10**9


def after(values, marker):
    return lax.optimization_barrier((values, marker))[0]


def call(kernel, outs, *args, cost=1, far=(), scratch=()):
    spaces = [pltpu.HBM if place in far else pltpu.VMEM for place in range(len(args))]
    args = [
        pltpu.with_memory_space_constraint(arg, pltpu.HBM) if place in far else arg
        for place, arg in enumerate(args)
    ]
    return pl.pallas_call(
        kernel,
        out_shape=outs,
        in_specs=[pl.BlockSpec(memory_space=space) for space in spaces],
        scratch_shapes=scratch,
        compiler_params=pltpu.CompilerParams(vmem_limit_bytes=24 * 1024 * 1024),
        cost_estimate=pl.CostEstimate(flops=cost, bytes_accessed=cost, transcendentals=0),
    )(*args)


def shape(rows, cols, dtype=jnp.bfloat16):
    return jax.ShapeDtypeStruct((rows, cols), dtype)


def dispatch_kernel(owners, capacity, ids_hbm, weights_hbm, tokens_hbm, cotangent_hbm, *refs):
    chosen_ref, *out_refs, ids_ref, weights_ref, tokens_ref, cotangent_ref, sems = refs
    copies = [
        pltpu.make_async_copy(source, target, sems.at[place])
        for place, (source, target) in enumerate(
            (
                (ids_hbm, ids_ref),
                (weights_hbm, weights_ref),
                (tokens_hbm, tokens_ref),
                (cotangent_hbm, cotangent_ref),
            )
        )
    ]
    for copy in copies:
        copy.start()
    copies[0].wait()
    pairs = ids_ref.shape[1]
    width = tokens_ref.shape[1]
    slot_count = owners * capacity
    me = lax.axis_index("expert")
    ids = ids_ref[...]
    named = ids == lax.broadcasted_iota(jnp.int32, (owners, pairs), 0)
    before = lax.broadcasted_iota(jnp.int32, (pairs, pairs), 0) < lax.broadcasted_iota(
        jnp.int32, (pairs, pairs), 1
    )
    named = named.astype(jnp.float32)
    counts = jnp.dot(
        named.astype(jnp.bfloat16),
        before.astype(jnp.float32).astype(jnp.bfloat16),
        preferred_element_type=jnp.float32,
    )
    rank = jnp.sum(named * counts, axis=0, keepdims=True).astype(jnp.int32)
    slots = lax.broadcasted_iota(jnp.int32, (slot_count, pairs), 0)
    chosen = (slots == (ids ^ me) * capacity + rank).astype(jnp.float32)
    select = chosen.astype(jnp.bfloat16)
    chosen_ref[...] = select
    for copy in copies[1:]:
        copy.wait()
    scale = jnp.sum(chosen * weights_ref[...], axis=1, keepdims=True)
    feats = jnp.dot(select, tokens_ref[...], preferred_element_type=jnp.float32)
    cots = jnp.dot(select, cotangent_ref[...], preferred_element_type=jnp.float32) * scale
    at = 0
    for out_ref in out_refs:
        rows = slice(at, at + out_ref.shape[0])
        out_ref[:, :width] = feats[rows].astype(jnp.bfloat16)
        out_ref[:, width:] = cots[rows].astype(jnp.bfloat16)
        at += out_ref.shape[0]


def load_kernel(gate_hbm, up_hbm, down_hbm, marker_hbm, gate_ref, up_ref, down_ref, sems):
    copies = [
        pltpu.make_async_copy(source, target, sems.at[place])
        for place, (source, target) in enumerate(
            ((gate_hbm, gate_ref), (up_hbm, up_ref), (down_hbm, down_ref))
        )
    ]
    for copy in copies:
        copy.start()
    for copy in copies:
        copy.wait()


def turn_kernel(*refs):
    for source, target in zip(refs[:3], refs[3:]):
        target[...] = source[...].T


def near_rows(from_pair_ref, *group_refs):
    halves = [ref[:ref.shape[0] // 2] for ref in group_refs]
    return jnp.concatenate(halves + [from_pair_ref[...]], axis=0)


def with_own_rows(own, rows):
    part, half = own.shape[0] // 2, rows.shape[0] // 2
    return jnp.concatenate([own[:part], rows[:half], own[part:], rows[half:]], axis=0)


def products_kernel(turned, *refs):
    *row_refs, gate_ref, up_ref, down_ref, mine_ref, other_ref = refs
    rows = row_refs[-1][...]
    if len(row_refs) > 1:
        rows = with_own_rows(rows, near_rows(*row_refs[:-1]))
    half = rows.shape[0] // 2
    width = rows.shape[1] // 2
    hidden_units = gate_ref.shape[1]
    core = lax.axis_index("dp") % 2
    feats, cots = rows[:, :width], rows[:, width:]
    for place, weight_ref in enumerate((gate_ref, up_ref, down_ref)):
        cols = slice(place * hidden_units, (place + 1) * hidden_units)
        rows = feats if place < 2 else cots
        if place < 2 or turned:
            out = jnp.dot(rows, weight_ref[...], preferred_element_type=jnp.float32)
        else:
            out = contract_cols(rows, weight_ref[...])
        low, high = out[:half], out[half:]
        mine_ref[:, cols] = jnp.where(core == 0, low, high)
        other_ref[:, cols] = jnp.where(core == 0, high, low).astype(jnp.bfloat16)


def sums_kernel(mine_ref, received_ref, *refs):
    sums = mine_ref[...] + received_ref[...].astype(jnp.float32)
    at = 0
    for sums_ref, packed_ref in zip(refs[::2], refs[1::2]):
        part = sums[at:at + sums_ref.shape[0]]
        sums_ref[...] = part
        packed_ref[...] = part.astype(jnp.bfloat16)
        at += part.shape[0]


def deltas_kernel(sums_ref, received_ref, out_ref):
    hidden_units = sums_ref.shape[1] // 3
    cols = [slice(i * hidden_units, (i + 1) * hidden_units) for i in range(3)]
    parts = [sums_ref[:, c] + received_ref[:, c].astype(jnp.float32) for c in cols]
    for c, part in zip(cols, local_deltas(*parts)):
        out_ref[:, c] = part


def in_order(core, mine, other):
    return jnp.concatenate(
        [jnp.where(core == 0, mine, other), jnp.where(core == 0, other, mine)], axis=0
    )


def slot_grad_rows(mine_ref, other_ref, gate_ref, up_ref):
    hidden_units = gate_ref.shape[0]
    rows = in_order(lax.axis_index("dp") % 2, mine_ref[...], other_ref[...])
    by_gate, by_up = rows[:, hidden_units:2 * hidden_units], rows[:, 2 * hidden_units:]
    return (
        jnp.dot(by_gate, gate_ref[...], preferred_element_type=jnp.float32)
        + jnp.dot(by_up, up_ref[...], preferred_element_type=jnp.float32)
    ).astype(jnp.bfloat16)


def slot_grad_kernel(mine_ref, other_ref, gate_ref, up_ref, *block_refs):
    out = slot_grad_rows(mine_ref, other_ref, gate_ref, up_ref)
    block = block_refs[0].shape[0]
    for place, ref in enumerate(block_refs):
        ref[...] = out[place * block:(place + 1) * block]


def far_grad_kernel(mine_ref, other_ref, gate_ref, up_ref, pair_ref, out_ref):
    block = pair_ref.shape[0]
    out_ref[:block] = pair_ref[...]
    out_ref[block:] = slot_grad_rows(mine_ref, other_ref, gate_ref, up_ref)


def weight_grads_kernel(names, tiles, *refs):
    outs = len(names)
    *in_refs, rows_ref, deltas_ref, sems = refs
    in_refs, out_refs, tile_refs = in_refs[:-2 * outs], in_refs[-2 * outs:-outs], in_refs[-outs:]
    row_refs, delta_refs = in_refs[:-6], in_refs[-6:]
    width = rows_ref.shape[1] // 2
    hidden_units = deltas_ref.shape[1] // 3
    core = lax.axis_index("dp") % 2
    at = 0
    for place, rows in enumerate((near_rows(*row_refs[:-2]), row_refs[-2][...], row_refs[-1][...])):
        span = slice(at, at + rows.shape[0])
        rows_ref[span] = rows
        mine, other = delta_refs[2 * place:2 * place + 2]
        deltas_ref[span] = in_order(core, mine[...], other[...])
        at = span.stop

    copies = []
    for name, tile, out_ref, tile_ref in zip(names, tiles, out_refs, tile_refs):
        for at in range(0, out_ref.shape[0], tile):
            rows = min(tile, out_ref.shape[0] - at)
            if name == "down":
                out = contract_rows(deltas_ref[:, at:at + rows], rows_ref[:, width:])
            else:
                start = hidden_units * (1 if name == "gate" else 2)
                out = contract_rows(
                    rows_ref[:, at:at + rows], deltas_ref[:, start:start + hidden_units]
                )
            tile_ref[at:at + rows] = out
            span = pl.ds(at, rows)
            copies.append(
                pltpu.make_async_copy(tile_ref.at[span], out_ref.at[span], sems.at[len(copies)])
            )
            copies[-1].start()
    for copy in copies:
        copy.wait()


def weight_grads(names, width, hidden_units, slot_count, inputs):
    sizes = {"gate": (width, hidden_units), "up": (width, hidden_units), "down": (hidden_units, width)}
    outs = [shape(*sizes[name], jnp.float32) for name in names]
    tiles = [384 if name == "down" else 128 for name in names]
    copies = sum(-(-out.shape[0] // tile) for out, tile in zip(outs, tiles))
    return pl.pallas_call(
        functools.partial(weight_grads_kernel, names, tiles),
        out_shape=outs,
        in_specs=[pl.BlockSpec(memory_space=pltpu.VMEM)] * len(inputs),
        out_specs=[pl.BlockSpec(memory_space=pltpu.HBM)] * len(outs),
        scratch_shapes=[pltpu.VMEM(out.shape, out.dtype) for out in outs]
        + [
            pltpu.VMEM((slot_count, 2 * width), jnp.bfloat16),
            pltpu.VMEM((slot_count, 3 * hidden_units), jnp.bfloat16),
            pltpu.SemaphoreType.DMA((copies,)),
        ],
        compiler_params=pltpu.CompilerParams(vmem_limit_bytes=24 * 1024 * 1024),
        cost_estimate=pl.CostEstimate(flops=10**7, bytes_accessed=10**7, transcendentals=0),
    )(*inputs)


def token_grad_kernel(chosen_ref, own_ref, from_pair_ref, *refs):
    *group_refs, out_ref = refs
    block = own_ref.shape[0]
    rows = [own_ref[...], from_pair_ref[:block]] + [ref[...] for ref in reversed(group_refs)]
    returned = jnp.concatenate(rows, axis=0)
    out_ref[...] = contract_rows(chosen_ref[...], returned).astype(jnp.bfloat16)


def body_by_all_to_all(tokens, cotangent, expert_ids, route_weights, gate_weight, up_weight, down_weight):
    owners = lax.axis_size("expert")
    width_parts = lax.axis_size("dp")
    tok_rows, top_count = expert_ids.shape
    width = tokens.shape[1]
    capacity = min(tok_rows, max(2, (tok_rows * top_count + owners - 1) // owners))
    slot_count = owners * capacity
    flat_ids = expert_ids.reshape(-1)
    position = jnp.arange(flat_ids.shape[0], dtype=jnp.int32)
    earlier = (flat_ids[:, None] == flat_ids[None, :]) & (position[None, :] < position[:, None])
    rank_pos = jnp.sum(earlier.astype(jnp.int32), axis=1)
    slot_pos = flat_ids * capacity + rank_pos
    pair_select = (slot_pos[:, None] == jnp.arange(slot_count, dtype=jnp.int32)[None, :]).astype(
        jnp.bfloat16
    )
    chosen = jnp.sum(
        pair_select.reshape(tok_rows, top_count, slot_count).astype(jnp.float32), axis=1
    ).astype(jnp.bfloat16)
    pair_tokens = jnp.repeat(tokens, top_count, axis=0)
    pair_scaled = (
        jnp.repeat(cotangent.astype(jnp.float32), top_count, axis=0) * route_weights
    ).astype(jnp.bfloat16)
    payload = jnp.concatenate([pair_tokens, pair_scaled], axis=1)
    send = contract_rows(pair_select, payload).astype(jnp.bfloat16)
    slots = lax.all_to_all(send, "expert", split_axis=0, concat_axis=0, tiled=True)

    core = lax.axis_index("dp") % 2
    half = slot_count // 2
    mine_slots = lax.dynamic_slice_in_dim(slots, core * half, half, 0)
    other_slots = lax.dynamic_slice_in_dim(slots, (1 - core) * half, half, 0)
    w_gate = gate_weight[0]
    w_up = up_weight[0]
    w_down = down_weight[0]

    def partial_sums(rows):
        feats, cots = rows[:, :width], rows[:, width:]
        return (
            jnp.dot(feats, w_gate, preferred_element_type=jnp.float32),
            jnp.dot(feats, w_up, preferred_element_type=jnp.float32),
            contract_cols(cots, w_down),
        )

    def pack(parts):
        return jnp.stack([part.astype(jnp.bfloat16) for part in parts])

    received = swap(pack(partial_sums(other_slots)), 1)
    sums = jnp.stack(partial_sums(mine_slots)) + received.astype(jnp.float32)
    bit = 2
    while bit < width_parts:
        sums = sums + swap(sums.astype(jnp.bfloat16), bit).astype(jnp.float32)
        bit *= 2
    mine = jnp.stack(local_deltas(sums[0], sums[1], sums[2]))
    other = swap(mine, 1)
    hidden, gate_delta, up_delta = jnp.concatenate([mine, other], axis=1)
    both = jnp.concatenate([mine_slots, other_slots], axis=0)
    slot_grad = (contract_cols(gate_delta, w_gate) + contract_cols(up_delta, w_up)).astype(
        jnp.bfloat16
    )
    slot_grad = jnp.where(
        core == 0, slot_grad, jnp.concatenate([slot_grad[half:], slot_grad[:half]], axis=0)
    )
    returned = lax.all_to_all(slot_grad, "expert", split_axis=0, concat_axis=0, tiled=True)
    feats, cots = both[:, :width], both[:, width:]
    gate_grad = contract_rows(feats, gate_delta)
    up_grad = contract_rows(feats, up_delta)
    down_grad = contract_rows(hidden, cots)
    token_grad = jnp.dot(chosen, returned, preferred_element_type=jnp.float32).astype(jnp.bfloat16)
    return (token_grad, gate_grad[None], up_grad[None], down_grad[None])


def body_by_pairs(tokens, cotangent, expert_ids, route_weights, gate_weight, up_weight, down_weight):
    owners = lax.axis_size("expert")
    width_parts = lax.axis_size("dp")
    tok_rows, _ = expert_ids.shape
    width = tokens.shape[1]
    hidden_units = gate_weight.shape[2]
    capacity = min(tok_rows, max(2, (tok_rows + owners - 1) // owners))
    slot_count = owners * capacity
    half = owners // 2

    far_first = [0] + list(reversed(range(1, half)))
    chosen, own, pair_block, *groups = call(
        functools.partial(dispatch_kernel, owners, capacity),
        (shape(slot_count, tok_rows),)
        + (shape(capacity, 2 * width),) * 2
        + (shape(2 * capacity, 2 * width),) * (half - 1),
        expert_ids.reshape(1, tok_rows),
        route_weights.reshape(1, tok_rows),
        tokens,
        cotangent,
        far=range(4),
        scratch=[
            pltpu.VMEM((1, tok_rows), jnp.int32),
            pltpu.VMEM((1, tok_rows), jnp.float32),
            pltpu.VMEM((tok_rows, width), jnp.bfloat16),
            pltpu.VMEM((tok_rows, width), jnp.bfloat16),
            pltpu.SemaphoreType.DMA((4,)),
        ],
    )
    weights = call(
        load_kernel,
        (shape(width, hidden_units), shape(width, hidden_units), shape(hidden_units, width)),
        gate_weight[0],
        up_weight[0],
        down_weight[0],
        chosen,
        far=range(3),
        scratch=[pltpu.SemaphoreType.DMA((3,))],
        cost=10**7,
    )
    groups = [swap(groups[j - 1], 2 * j, "expert") for j in far_first[1:]]
    from_pair = swap(pair_block, 1, "expert")
    groups = after(groups, from_pair)
    seconds = jnp.concatenate([group[capacity:] for group in groups], axis=0)
    by_pair = swap(after(seconds, weights[2]), 1, "expert")

    turned = call(
        turn_kernel,
        (shape(hidden_units, width), shape(hidden_units, width), shape(width, hidden_units)),
        *after(weights, groups[0]),
    )
    far = after(by_pair, turned[0])
    near = [from_pair] + groups

    def pieces(*parts):
        shapes = []
        for part in parts:
            shapes += [shape(part, 3 * hidden_units, jnp.float32), shape(part, 3 * hidden_units)]
        return shapes

    def sums_over_cores(rows, down, cost, *parts):
        mine, other = call(
            functools.partial(products_kernel, down is turned[2]),
            pieces(sum(parts)),
            *rows,
            *weights[:2],
            down,
            cost=cost,
        )
        out = call(sums_kernel, pieces(*parts), mine, swap(other, 1))
        return list(zip(out[::2], out[1::2]))

    def exchanged(sums, marker):
        bit = 2
        while 2 * bit < width_parts:
            sums, marker = call(sums_kernel, pieces(sums.shape[0]), sums, swap(marker, bit))
            bit *= 2
        return sums, swap(marker, bit)

    def deltas_of(sums, received, cost):
        return call(deltas_kernel, shape(*sums.shape), sums, received, cost=cost)

    own_half = capacity // 2
    own_sums, near_sums = sums_over_cores(
        near + [own], weights[2], 1, own_half, half * capacity // 2
    )
    (far_sums,) = sums_over_cores([far], turned[2], FAR_PRODUCTS_COST, (half - 1) * capacity // 2)
    near_sums, far_sums = exchanged(*near_sums), exchanged(*far_sums)
    own_sums = exchanged(*own_sums)

    near_mine = deltas_of(*near_sums, 1)
    near_deltas = near_mine, swap(near_mine, 1)
    far_mine = after(deltas_of(*far_sums, FAR_DELTAS_COST), near_deltas[1])
    far_deltas = far_mine, swap(far_mine, 1)
    own_mine = deltas_of(*own_sums, OWN_DELTAS_COST)
    own_deltas = own_mine, swap(own_mine, 1)
    block = shape(capacity, width)
    grads = call(slot_grad_kernel, (block,) * half, *near_deltas, *turned[:2])
    (own_grad,) = call(slot_grad_kernel, (block,), *own_deltas, *turned[:2])
    to_pair = call(
        far_grad_kernel,
        shape(half * capacity, width),
        *after(far_deltas, own_mine),
        *turned[:2],
        grads[-1],
    )
    deltas = near_deltas + own_deltas + far_deltas

    returned_pair = swap(to_pair, 1, "expert")
    sizes = (width, hidden_units, slot_count, (*near, own, far, *deltas))
    (gate_grad,) = weight_grads(("gate",), *sizes)
    returned_pair = after(returned_pair, (gate_grad, own_grad))
    returned = {}
    for place, j in enumerate(far_first[1:], 1):
        more = returned_pair[place * capacity:(place + 1) * capacity]
        returned[j] = swap(jnp.concatenate([grads[place - 1], more], axis=0), 2 * j, "expert")
    up_grad, down_grad = weight_grads(("up", "down"), *sizes)
    token_grad = call(
        token_grad_kernel,
        shape(tok_rows, width),
        chosen,
        own_grad,
        returned_pair,
        *[returned[j] for j in far_first[1:]],
    )
    return (token_grad, gate_grad[None], up_grad[None], down_grad[None])


def body(tokens, cotangent, expert_ids, *rest):
    owners = lax.axis_size("expert")
    width_parts = lax.axis_size("dp")
    tok_rows, top_count = expert_ids.shape
    by_pairs = (
        top_count == 1
        and owners >= 8
        and owners & (owners - 1) == 0
        and width_parts >= 4
        and tok_rows % (16 * owners) == 0
    )
    chosen = body_by_pairs if by_pairs else body_by_all_to_all
    return chosen(tokens, cotangent, expert_ids, *rest)


def solution(mesh):
    return jax.shard_map(
        body,
        mesh=mesh,
        in_specs=(
            P("expert", "dp"),
            P("expert", "dp"),
            P("expert", None),
            P("expert", None),
            P("expert", "dp", None),
            P("expert", "dp", None),
            P("expert", None, "dp"),
        ),
        out_specs=(
            P("expert", "dp"),
            P("expert", "dp", None),
            P("expert", "dp", None),
            P("expert", None, "dp"),
        ),
        check_vma=False,
    )
```

```python
import functools

import jax
import jax.numpy as jnp
from jax import lax
from jax.experimental import pallas as pl
from jax.experimental.pallas import tpu as pltpu
from jax.sharding import PartitionSpec as P


def contract_rows(left, right):
    return lax.dot_general(
        left, right, (((0,), (0,)), ((), ())), preferred_element_type=jnp.float32
    )


def contract_cols(left, right):
    return lax.dot_general(
        left, right, (((1,), (1,)), ((), ())), preferred_element_type=jnp.float32
    )


def local_deltas(gate_pre, up_pre, hidden_grad):
    sigma = jax.nn.sigmoid(gate_pre)
    activated = gate_pre * sigma
    hidden = (activated * up_pre).astype(jnp.bfloat16)
    gate_delta = (hidden_grad * up_pre * sigma * (1.0 + gate_pre * (1.0 - sigma))).astype(
        jnp.bfloat16
    )
    up_delta = (hidden_grad * activated).astype(jnp.bfloat16)
    return (hidden, gate_delta, up_delta)


def swap(value, bit, axis="dp"):
    size = lax.axis_size(axis)
    return lax.ppermute(value, axis, [(i, i ^ bit) for i in range(size)])


FAR_PRODUCTS_COST = 3 * 10**8
FAR_DELTAS_COST = 8 * 10**8
OWN_DELTAS_COST = 3 * 10**9


def after(values, marker):
    return lax.optimization_barrier((values, marker))[0]


def call(kernel, outs, *args, cost=1, far=(), scratch=()):
    spaces = [pltpu.HBM if place in far else pltpu.VMEM for place in range(len(args))]
    args = [
        pltpu.with_memory_space_constraint(arg, pltpu.HBM) if place in far else arg
        for place, arg in enumerate(args)
    ]
    return pl.pallas_call(
        kernel,
        out_shape=outs,
        in_specs=[pl.BlockSpec(memory_space=space) for space in spaces],
        scratch_shapes=scratch,
        compiler_params=pltpu.CompilerParams(vmem_limit_bytes=24 * 1024 * 1024),
        cost_estimate=pl.CostEstimate(flops=cost, bytes_accessed=cost, transcendentals=0),
    )(*args)


def shape(rows, cols, dtype=jnp.bfloat16):
    return jax.ShapeDtypeStruct((rows, cols), dtype)


def dispatch_kernel(owners, capacity, ids_hbm, weights_hbm, tokens_hbm, cotangent_hbm, *refs):
    chosen_ref, *out_refs, ids_ref, weights_ref, tokens_ref, cotangent_ref, sems = refs
    copies = [
        pltpu.make_async_copy(source, target, sems.at[place])
        for place, (source, target) in enumerate(
            (
                (ids_hbm, ids_ref),
                (weights_hbm, weights_ref),
                (tokens_hbm, tokens_ref),
                (cotangent_hbm, cotangent_ref),
            )
        )
    ]
    for copy in copies:
        copy.start()
    copies[0].wait()
    pairs = ids_ref.shape[1]
    width = tokens_ref.shape[1]
    slot_count = owners * capacity
    me = lax.axis_index("expert")
    ids = ids_ref[...]
    named = ids == lax.broadcasted_iota(jnp.int32, (owners, pairs), 0)
    before = lax.broadcasted_iota(jnp.int32, (pairs, pairs), 0) < lax.broadcasted_iota(
        jnp.int32, (pairs, pairs), 1
    )
    named = named.astype(jnp.float32)
    counts = jnp.dot(
        named.astype(jnp.bfloat16),
        before.astype(jnp.float32).astype(jnp.bfloat16),
        preferred_element_type=jnp.float32,
    )
    rank = jnp.sum(named * counts, axis=0, keepdims=True).astype(jnp.int32)
    slots = lax.broadcasted_iota(jnp.int32, (slot_count, pairs), 0)
    chosen = (slots == (ids ^ me) * capacity + rank).astype(jnp.float32)
    select = chosen.astype(jnp.bfloat16)
    chosen_ref[...] = select
    for copy in copies[1:]:
        copy.wait()
    scale = jnp.sum(chosen * weights_ref[...], axis=1, keepdims=True)
    feats = jnp.dot(select, tokens_ref[...], preferred_element_type=jnp.float32)
    cots = jnp.dot(select, cotangent_ref[...], preferred_element_type=jnp.float32) * scale
    at = 0
    for out_ref in out_refs:
        rows = slice(at, at + out_ref.shape[0])
        out_ref[:, :width] = feats[rows].astype(jnp.bfloat16)
        out_ref[:, width:] = cots[rows].astype(jnp.bfloat16)
        at += out_ref.shape[0]


def load_kernel(down_hbm, gate_hbm, up_hbm, marker_hbm, turned_ref, gate_ref, up_ref, down_ref, sems):
    copies = [
        pltpu.make_async_copy(source, target, sems.at[place])
        for place, (source, target) in enumerate(
            ((down_hbm, down_ref), (gate_hbm, gate_ref), (up_hbm, up_ref))
        )
    ]
    for copy in copies:
        copy.start()
    copies[0].wait()
    turned_ref[...] = down_ref[...].T
    for copy in copies[1:]:
        copy.wait()


def turn_kernel(*refs):
    for source, target in zip(refs[:2], refs[2:]):
        target[...] = source[...].T


def near_rows(from_pair_ref, *group_refs, cols=slice(None)):
    halves = [ref[:ref.shape[0] // 2, cols] for ref in group_refs]
    return jnp.concatenate(halves + [from_pair_ref[:, cols]], axis=0)


def with_own_rows(own, rows):
    part, half = own.shape[0] // 2, rows.shape[0] // 2
    return jnp.concatenate([own[:part], rows[:half], own[part:], rows[half:]], axis=0)


def products_kernel(*refs):
    *row_refs, gate_ref, up_ref, down_ref, mine_ref, other_ref = refs
    rows = row_refs[-1][...]
    if len(row_refs) > 1:
        rows = with_own_rows(rows, near_rows(*row_refs[:-1]))
    half = rows.shape[0] // 2
    width = rows.shape[1] // 2
    hidden_units = gate_ref.shape[1]
    core = lax.axis_index("dp") % 2
    feats, cots = rows[:, :width], rows[:, width:]
    for place, weight_ref in enumerate((gate_ref, up_ref, down_ref)):
        cols = slice(place * hidden_units, (place + 1) * hidden_units)
        rows = feats if place < 2 else cots
        out = jnp.dot(rows, weight_ref[...], preferred_element_type=jnp.float32)
        low, high = out[:half], out[half:]
        mine_ref[:, cols] = jnp.where(core == 0, low, high)
        other_ref[:, cols] = jnp.where(core == 0, high, low).astype(jnp.bfloat16)


def sums_kernel(mine_ref, received_ref, *refs):
    sums = mine_ref[...] + received_ref[...].astype(jnp.float32)
    at = 0
    for sums_ref, packed_ref in zip(refs[::2], refs[1::2]):
        part = sums[at:at + sums_ref.shape[0]]
        sums_ref[...] = part
        packed_ref[...] = part.astype(jnp.bfloat16)
        at += part.shape[0]


def deltas_kernel(sums_ref, received_ref, out_ref):
    hidden_units = sums_ref.shape[1] // 3
    cols = [slice(i * hidden_units, (i + 1) * hidden_units) for i in range(3)]
    parts = [sums_ref[:, c] + received_ref[:, c].astype(jnp.float32) for c in cols]
    for c, part in zip(cols, local_deltas(*parts)):
        out_ref[:, c] = part


def in_order(core, mine, other):
    return jnp.concatenate(
        [jnp.where(core == 0, mine, other), jnp.where(core == 0, other, mine)], axis=0
    )


def slot_grad_rows(mine_ref, other_ref, gate_ref, up_ref):
    hidden_units = gate_ref.shape[0]
    rows = in_order(lax.axis_index("dp") % 2, mine_ref[...], other_ref[...])
    by_gate, by_up = rows[:, hidden_units:2 * hidden_units], rows[:, 2 * hidden_units:]
    return (
        jnp.dot(by_gate, gate_ref[...], preferred_element_type=jnp.float32)
        + jnp.dot(by_up, up_ref[...], preferred_element_type=jnp.float32)
    ).astype(jnp.bfloat16)


def slot_grad_kernel(mine_ref, other_ref, gate_ref, up_ref, *block_refs):
    out = slot_grad_rows(mine_ref, other_ref, gate_ref, up_ref)
    block = block_refs[0].shape[0]
    for place, ref in enumerate(block_refs):
        ref[...] = out[place * block:(place + 1) * block]


def far_grad_kernel(mine_ref, other_ref, gate_ref, up_ref, pair_ref, out_ref):
    block = pair_ref.shape[0]
    out_ref[:block] = pair_ref[...]
    out_ref[block:] = slot_grad_rows(mine_ref, other_ref, gate_ref, up_ref)


def weight_grads_kernel(names, tiles, *refs):
    outs = len(names)
    *in_refs, rows_ref, deltas_ref, sems = refs
    in_refs, out_refs, tile_refs = in_refs[:-2 * outs], in_refs[-2 * outs:-outs], in_refs[-outs:]
    row_refs, delta_refs = in_refs[:-6], in_refs[-6:]
    width = rows_ref.shape[1] // 2
    hidden_units = deltas_ref.shape[1] // 3
    core = lax.axis_index("dp") % 2

    def gather_rows(cols):
        *near_refs, own_ref, far_ref = row_refs
        near = near_rows(*near_refs, cols=cols)
        rows_ref[:, cols] = jnp.concatenate([near, own_ref[:, cols], far_ref[:, cols]], axis=0)

    def gather_deltas(cols):
        at = 0
        for mine, other in zip(delta_refs[::2], delta_refs[1::2]):
            both = in_order(core, mine[:, cols], other[:, cols])
            deltas_ref[at:at + both.shape[0], cols] = both
            at += both.shape[0]

    copies = []
    for name, tile, out_ref, tile_ref in zip(names, tiles, out_refs, tile_refs):
        place = ("down", "gate", "up").index(name)
        of_name = slice(place * hidden_units, (place + 1) * hidden_units)
        gather_deltas(of_name)
        if name == "down":
            gather_rows(slice(width, 2 * width))
        elif name == names[0]:
            gather_rows(slice(0, width))
        for at in range(0, out_ref.shape[0], tile):
            rows = min(tile, out_ref.shape[0] - at)
            if name == "down":
                out = contract_rows(deltas_ref[:, at:at + rows], rows_ref[:, width:])
            else:
                out = contract_rows(rows_ref[:, at:at + rows], deltas_ref[:, of_name])
            tile_ref[at:at + rows] = out
            span = pl.ds(at, rows)
            copies.append(
                pltpu.make_async_copy(tile_ref.at[span], out_ref.at[span], sems.at[len(copies)])
            )
            copies[-1].start()
    for copy in copies:
        copy.wait()


def weight_grads(names, width, hidden_units, slot_count, inputs):
    sizes = {"gate": (width, hidden_units), "up": (width, hidden_units), "down": (hidden_units, width)}
    outs = [shape(*sizes[name], jnp.float32) for name in names]
    tiles = [384 if name == "down" else 128 for name in names]
    copies = sum(-(-out.shape[0] // tile) for out, tile in zip(outs, tiles))
    return pl.pallas_call(
        functools.partial(weight_grads_kernel, names, tiles),
        out_shape=outs,
        in_specs=[pl.BlockSpec(memory_space=pltpu.VMEM)] * len(inputs),
        out_specs=[pl.BlockSpec(memory_space=pltpu.HBM)] * len(outs),
        scratch_shapes=[pltpu.VMEM(out.shape, out.dtype) for out in outs]
        + [
            pltpu.VMEM((slot_count, 2 * width), jnp.bfloat16),
            pltpu.VMEM((slot_count, 3 * hidden_units), jnp.bfloat16),
            pltpu.SemaphoreType.DMA((copies,)),
        ],
        compiler_params=pltpu.CompilerParams(vmem_limit_bytes=24 * 1024 * 1024),
        cost_estimate=pl.CostEstimate(flops=10**7, bytes_accessed=10**7, transcendentals=0),
    )(*inputs)


def token_grad_kernel(chosen_ref, own_ref, from_pair_ref, *refs):
    *group_refs, out_ref = refs
    block = own_ref.shape[0]
    rows = [own_ref[...], from_pair_ref[:block]] + [ref[...] for ref in reversed(group_refs)]
    returned = jnp.concatenate(rows, axis=0)
    out_ref[...] = contract_rows(chosen_ref[...], returned).astype(jnp.bfloat16)


def body_by_all_to_all(tokens, cotangent, expert_ids, route_weights, gate_weight, up_weight, down_weight):
    owners = lax.axis_size("expert")
    width_parts = lax.axis_size("dp")
    tok_rows, top_count = expert_ids.shape
    width = tokens.shape[1]
    capacity = min(tok_rows, max(2, (tok_rows * top_count + owners - 1) // owners))
    slot_count = owners * capacity
    flat_ids = expert_ids.reshape(-1)
    position = jnp.arange(flat_ids.shape[0], dtype=jnp.int32)
    earlier = (flat_ids[:, None] == flat_ids[None, :]) & (position[None, :] < position[:, None])
    rank_pos = jnp.sum(earlier.astype(jnp.int32), axis=1)
    slot_pos = flat_ids * capacity + rank_pos
    pair_select = (slot_pos[:, None] == jnp.arange(slot_count, dtype=jnp.int32)[None, :]).astype(
        jnp.bfloat16
    )
    chosen = jnp.sum(
        pair_select.reshape(tok_rows, top_count, slot_count).astype(jnp.float32), axis=1
    ).astype(jnp.bfloat16)
    pair_tokens = jnp.repeat(tokens, top_count, axis=0)
    pair_scaled = (
        jnp.repeat(cotangent.astype(jnp.float32), top_count, axis=0) * route_weights
    ).astype(jnp.bfloat16)
    payload = jnp.concatenate([pair_tokens, pair_scaled], axis=1)
    send = contract_rows(pair_select, payload).astype(jnp.bfloat16)
    slots = lax.all_to_all(send, "expert", split_axis=0, concat_axis=0, tiled=True)

    core = lax.axis_index("dp") % 2
    half = slot_count // 2
    mine_slots = lax.dynamic_slice_in_dim(slots, core * half, half, 0)
    other_slots = lax.dynamic_slice_in_dim(slots, (1 - core) * half, half, 0)
    w_gate = gate_weight[0]
    w_up = up_weight[0]
    w_down = down_weight[0]

    def partial_sums(rows):
        feats, cots = rows[:, :width], rows[:, width:]
        return (
            jnp.dot(feats, w_gate, preferred_element_type=jnp.float32),
            jnp.dot(feats, w_up, preferred_element_type=jnp.float32),
            contract_cols(cots, w_down),
        )

    def pack(parts):
        return jnp.stack([part.astype(jnp.bfloat16) for part in parts])

    received = swap(pack(partial_sums(other_slots)), 1)
    sums = jnp.stack(partial_sums(mine_slots)) + received.astype(jnp.float32)
    bit = 2
    while bit < width_parts:
        sums = sums + swap(sums.astype(jnp.bfloat16), bit).astype(jnp.float32)
        bit *= 2
    mine = jnp.stack(local_deltas(sums[0], sums[1], sums[2]))
    other = swap(mine, 1)
    hidden, gate_delta, up_delta = jnp.concatenate([mine, other], axis=1)
    both = jnp.concatenate([mine_slots, other_slots], axis=0)
    slot_grad = (contract_cols(gate_delta, w_gate) + contract_cols(up_delta, w_up)).astype(
        jnp.bfloat16
    )
    slot_grad = jnp.where(
        core == 0, slot_grad, jnp.concatenate([slot_grad[half:], slot_grad[:half]], axis=0)
    )
    returned = lax.all_to_all(slot_grad, "expert", split_axis=0, concat_axis=0, tiled=True)
    feats, cots = both[:, :width], both[:, width:]
    gate_grad = contract_rows(feats, gate_delta)
    up_grad = contract_rows(feats, up_delta)
    down_grad = contract_rows(hidden, cots)
    token_grad = jnp.dot(chosen, returned, preferred_element_type=jnp.float32).astype(jnp.bfloat16)
    return (token_grad, gate_grad[None], up_grad[None], down_grad[None])


def body_by_pairs(tokens, cotangent, expert_ids, route_weights, gate_weight, up_weight, down_weight):
    owners = lax.axis_size("expert")
    width_parts = lax.axis_size("dp")
    tok_rows, _ = expert_ids.shape
    width = tokens.shape[1]
    hidden_units = gate_weight.shape[2]
    capacity = min(tok_rows, max(2, (tok_rows + owners - 1) // owners))
    slot_count = owners * capacity
    half = owners // 2

    far_first = [0] + list(reversed(range(1, half)))
    chosen, own, pair_block, *groups = call(
        functools.partial(dispatch_kernel, owners, capacity),
        (shape(slot_count, tok_rows),)
        + (shape(capacity, 2 * width),) * 2
        + (shape(2 * capacity, 2 * width),) * (half - 1),
        expert_ids.reshape(1, tok_rows),
        route_weights.reshape(1, tok_rows),
        tokens,
        cotangent,
        far=range(4),
        scratch=[
            pltpu.VMEM((1, tok_rows), jnp.int32),
            pltpu.VMEM((1, tok_rows), jnp.float32),
            pltpu.VMEM((tok_rows, width), jnp.bfloat16),
            pltpu.VMEM((tok_rows, width), jnp.bfloat16),
            pltpu.SemaphoreType.DMA((4,)),
        ],
    )
    down, gate, up = call(
        load_kernel,
        (shape(width, hidden_units),) * 3,
        down_weight[0],
        gate_weight[0],
        up_weight[0],
        chosen,
        far=range(3),
        scratch=[
            pltpu.VMEM((hidden_units, width), jnp.bfloat16),
            pltpu.SemaphoreType.DMA((3,)),
        ],
        cost=10**7,
    )
    groups = [swap(groups[j - 1], 2 * j, "expert") for j in far_first[1:]]
    from_pair = swap(pair_block, 1, "expert")
    groups = after(groups, from_pair)
    seconds = jnp.concatenate([group[capacity:] for group in groups], axis=0)
    by_pair = swap(after(seconds, up), 1, "expert")

    turned = call(turn_kernel, (shape(hidden_units, width),) * 2, *after((gate, up), groups[0]))
    far = after(by_pair, turned[0])
    near = [from_pair] + groups

    def pieces(*parts):
        shapes = []
        for part in parts:
            shapes += [shape(part, 3 * hidden_units, jnp.float32), shape(part, 3 * hidden_units)]
        return shapes

    def sums_over_cores(rows, cost, *parts):
        mine, other = call(
            products_kernel, pieces(sum(parts)), *rows, gate, up, down, cost=cost
        )
        out = call(sums_kernel, pieces(*parts), mine, swap(other, 1))
        return list(zip(out[::2], out[1::2]))

    def exchanged(sums, marker):
        bit = 2
        while 2 * bit < width_parts:
            sums, marker = call(sums_kernel, pieces(sums.shape[0]), sums, swap(marker, bit))
            bit *= 2
        return sums, swap(marker, bit)

    def deltas_of(sums, received, cost):
        return call(deltas_kernel, shape(*sums.shape), sums, received, cost=cost)

    own_half = capacity // 2
    own_sums, near_sums = sums_over_cores(
        near + [own], 1, own_half, half * capacity // 2
    )
    (far_sums,) = sums_over_cores([far], FAR_PRODUCTS_COST, (half - 1) * capacity // 2)
    near_sums, far_sums = exchanged(*near_sums), exchanged(*far_sums)
    own_sums = exchanged(*own_sums)

    near_mine = deltas_of(*near_sums, 1)
    near_deltas = near_mine, swap(near_mine, 1)
    far_mine = after(deltas_of(*far_sums, FAR_DELTAS_COST), near_deltas[1])
    far_deltas = far_mine, swap(far_mine, 1)
    own_mine = deltas_of(*own_sums, OWN_DELTAS_COST)
    own_deltas = own_mine, swap(own_mine, 1)
    block = shape(capacity, width)
    grads = call(slot_grad_kernel, (block,) * half, *near_deltas, *turned)
    (own_grad,) = call(slot_grad_kernel, (block,), *own_deltas, *turned)
    to_pair = call(
        far_grad_kernel,
        shape(half * capacity, width),
        *after(far_deltas, own_mine),
        *turned,
        grads[-1],
    )
    deltas = near_deltas + own_deltas + far_deltas

    returned_pair = swap(to_pair, 1, "expert")
    sizes = (width, hidden_units, slot_count, (*near, own, far, *deltas))
    (gate_grad,) = weight_grads(("gate",), *sizes)
    returned_pair = after(returned_pair, (gate_grad, own_grad))
    returned = {}
    for place, j in enumerate(far_first[1:], 1):
        more = returned_pair[place * capacity:(place + 1) * capacity]
        returned[j] = swap(jnp.concatenate([grads[place - 1], more], axis=0), 2 * j, "expert")
    up_grad, down_grad = weight_grads(("up", "down"), *sizes)
    token_grad = call(
        token_grad_kernel,
        shape(tok_rows, width),
        chosen,
        own_grad,
        returned_pair,
        *[returned[j] for j in far_first[1:]],
    )
    return (token_grad, gate_grad[None], up_grad[None], down_grad[None])


def body(tokens, cotangent, expert_ids, *rest):
    owners = lax.axis_size("expert")
    width_parts = lax.axis_size("dp")
    tok_rows, top_count = expert_ids.shape
    by_pairs = (
        top_count == 1
        and owners >= 8
        and owners & (owners - 1) == 0
        and width_parts >= 4
        and tok_rows % (16 * owners) == 0
    )
    chosen = body_by_pairs if by_pairs else body_by_all_to_all
    return chosen(tokens, cotangent, expert_ids, *rest)


def solution(mesh):
    return jax.shard_map(
        body,
        mesh=mesh,
        in_specs=(
            P("expert", "dp"),
            P("expert", "dp"),
            P("expert", None),
            P("expert", None),
            P("expert", "dp", None),
            P("expert", "dp", None),
            P("expert", None, "dp"),
        ),
        out_specs=(
            P("expert", "dp"),
            P("expert", "dp", None),
            P("expert", "dp", None),
            P("expert", None, "dp"),
        ),
        check_vma=False,
    )
```

```python
import functools

import jax
import jax.numpy as jnp
from jax import lax
from jax.experimental import pallas as pl
from jax.experimental.pallas import tpu as pltpu
from jax.sharding import PartitionSpec as P


def contract_rows(left, right):
    return lax.dot_general(
        left, right, (((0,), (0,)), ((), ())), preferred_element_type=jnp.float32
    )


def contract_cols(left, right):
    return lax.dot_general(
        left, right, (((1,), (1,)), ((), ())), preferred_element_type=jnp.float32
    )


def local_deltas(gate_pre, up_pre, hidden_grad):
    sigma = jax.nn.sigmoid(gate_pre)
    activated = gate_pre * sigma
    hidden = (activated * up_pre).astype(jnp.bfloat16)
    gate_delta = (hidden_grad * up_pre * sigma * (1.0 + gate_pre * (1.0 - sigma))).astype(
        jnp.bfloat16
    )
    up_delta = (hidden_grad * activated).astype(jnp.bfloat16)
    return (hidden, gate_delta, up_delta)


def swap(value, bit, axis="dp"):
    size = lax.axis_size(axis)
    return lax.ppermute(value, axis, [(i, i ^ bit) for i in range(size)])


FAR_PRODUCTS_COST = 3 * 10**8
FAR_DELTAS_COST = 8 * 10**8
OWN_DELTAS_COST = 18 * 10**8


def after(values, marker):
    return lax.optimization_barrier((values, marker))[0]


def call(kernel, outs, *args, cost=1, far=(), scratch=()):
    spaces = [pltpu.HBM if place in far else pltpu.VMEM for place in range(len(args))]
    args = [
        pltpu.with_memory_space_constraint(arg, pltpu.HBM) if place in far else arg
        for place, arg in enumerate(args)
    ]
    return pl.pallas_call(
        kernel,
        out_shape=outs,
        in_specs=[pl.BlockSpec(memory_space=space) for space in spaces],
        scratch_shapes=scratch,
        compiler_params=pltpu.CompilerParams(vmem_limit_bytes=24 * 1024 * 1024),
        cost_estimate=pl.CostEstimate(flops=cost, bytes_accessed=cost, transcendentals=0),
    )(*args)


def shape(rows, cols, dtype=jnp.bfloat16):
    return jax.ShapeDtypeStruct((rows, cols), dtype)


def dispatch_kernel(owners, capacity, ids_hbm, weights_hbm, tokens_hbm, cotangent_hbm, *refs):
    chosen_ref, *out_refs, ids_ref, weights_ref, tokens_ref, cotangent_ref, sems = refs
    copies = [
        pltpu.make_async_copy(source, target, sems.at[place])
        for place, (source, target) in enumerate(
            (
                (ids_hbm, ids_ref),
                (weights_hbm, weights_ref),
                (tokens_hbm, tokens_ref),
                (cotangent_hbm, cotangent_ref),
            )
        )
    ]
    for copy in copies:
        copy.start()
    copies[0].wait()
    pairs = ids_ref.shape[1]
    width = tokens_ref.shape[1]
    slot_count = owners * capacity
    me = lax.axis_index("expert")
    ids = ids_ref[...]
    named = ids == lax.broadcasted_iota(jnp.int32, (owners, pairs), 0)
    before = lax.broadcasted_iota(jnp.int32, (pairs, pairs), 0) < lax.broadcasted_iota(
        jnp.int32, (pairs, pairs), 1
    )
    named = named.astype(jnp.float32)
    counts = jnp.dot(
        named.astype(jnp.bfloat16),
        before.astype(jnp.float32).astype(jnp.bfloat16),
        preferred_element_type=jnp.float32,
    )
    rank = jnp.sum(named * counts, axis=0, keepdims=True).astype(jnp.int32)
    slots = lax.broadcasted_iota(jnp.int32, (slot_count, pairs), 0)
    chosen = (slots == (ids ^ me) * capacity + rank).astype(jnp.float32)
    select = chosen.astype(jnp.bfloat16)
    chosen_ref[...] = select
    for copy in copies[1:]:
        copy.wait()
    scale = jnp.sum(chosen * weights_ref[...], axis=1, keepdims=True)
    feats = jnp.dot(select, tokens_ref[...], preferred_element_type=jnp.float32)
    cots = jnp.dot(select, cotangent_ref[...], preferred_element_type=jnp.float32) * scale
    at = 0
    for out_ref in out_refs:
        rows = slice(at, at + out_ref.shape[0])
        out_ref[:, :width] = feats[rows].astype(jnp.bfloat16)
        out_ref[:, width:] = cots[rows].astype(jnp.bfloat16)
        at += out_ref.shape[0]


def load_kernel(down_hbm, gate_hbm, up_hbm, marker_hbm, turned_ref, gate_ref, up_ref, down_ref, sems):
    copies = [
        pltpu.make_async_copy(source, target, sems.at[place])
        for place, (source, target) in enumerate(
            ((down_hbm, down_ref), (gate_hbm, gate_ref), (up_hbm, up_ref))
        )
    ]
    for copy in copies:
        copy.start()
    copies[0].wait()
    turned_ref[...] = down_ref[...].T
    for copy in copies[1:]:
        copy.wait()


def turn_kernel(*refs):
    for source, target in zip(refs[:2], refs[2:]):
        target[...] = source[...].T


def near_rows(from_pair_ref, *group_refs, cols=slice(None)):
    halves = [ref[:ref.shape[0] // 2, cols] for ref in group_refs]
    return jnp.concatenate(halves + [from_pair_ref[:, cols]], axis=0)


def with_own_rows(own, rows):
    part, half = own.shape[0] // 2, rows.shape[0] // 2
    return jnp.concatenate([own[:part], rows[:half], own[part:], rows[half:]], axis=0)


def products_kernel(*refs):
    *row_refs, gate_ref, up_ref, down_ref, mine_ref, other_ref = refs
    rows = row_refs[-1][...]
    if len(row_refs) > 1:
        rows = with_own_rows(rows, near_rows(*row_refs[:-1]))
    half = rows.shape[0] // 2
    width = rows.shape[1] // 2
    hidden_units = gate_ref.shape[1]
    core = lax.axis_index("dp") % 2
    feats, cots = rows[:, :width], rows[:, width:]
    for place, weight_ref in enumerate((gate_ref, up_ref, down_ref)):
        cols = slice(place * hidden_units, (place + 1) * hidden_units)
        rows = feats if place < 2 else cots
        out = jnp.dot(rows, weight_ref[...], preferred_element_type=jnp.float32)
        low, high = out[:half], out[half:]
        mine_ref[:, cols] = jnp.where(core == 0, low, high)
        other_ref[:, cols] = jnp.where(core == 0, high, low).astype(jnp.bfloat16)


def sums_kernel(mine_ref, received_ref, *refs):
    sums = mine_ref[...] + received_ref[...].astype(jnp.float32)
    at = 0
    for sums_ref, packed_ref in zip(refs[::2], refs[1::2]):
        part = sums[at:at + sums_ref.shape[0]]
        sums_ref[...] = part
        packed_ref[...] = part.astype(jnp.bfloat16)
        at += part.shape[0]


def deltas_kernel(sums_ref, received_ref, out_ref):
    hidden_units = sums_ref.shape[1] // 3
    cols = [slice(i * hidden_units, (i + 1) * hidden_units) for i in range(3)]
    parts = [sums_ref[:, c] + received_ref[:, c].astype(jnp.float32) for c in cols]
    for c, part in zip(cols, local_deltas(*parts)):
        out_ref[:, c] = part


def in_order(core, mine, other):
    return jnp.concatenate(
        [jnp.where(core == 0, mine, other), jnp.where(core == 0, other, mine)], axis=0
    )


def slot_grad_rows(mine_ref, other_ref, gate_ref, up_ref):
    hidden_units = gate_ref.shape[0]
    rows = in_order(lax.axis_index("dp") % 2, mine_ref[...], other_ref[...])
    by_gate, by_up = rows[:, hidden_units:2 * hidden_units], rows[:, 2 * hidden_units:]
    return (
        jnp.dot(by_gate, gate_ref[...], preferred_element_type=jnp.float32)
        + jnp.dot(by_up, up_ref[...], preferred_element_type=jnp.float32)
    ).astype(jnp.bfloat16)


def slot_grad_kernel(mine_ref, other_ref, gate_ref, up_ref, *block_refs):
    out = slot_grad_rows(mine_ref, other_ref, gate_ref, up_ref)
    block = block_refs[0].shape[0]
    for place, ref in enumerate(block_refs):
        ref[...] = out[place * block:(place + 1) * block]


def far_grad_kernel(mine_ref, other_ref, gate_ref, up_ref, pair_ref, out_ref):
    block = pair_ref.shape[0]
    out_ref[:block] = pair_ref[...]
    out_ref[block:] = slot_grad_rows(mine_ref, other_ref, gate_ref, up_ref)


def weight_grads_kernel(names, tiles, *refs):
    outs = len(names)
    *in_refs, rows_ref, deltas_ref, sems = refs
    in_refs, out_refs, tile_refs = in_refs[:-2 * outs], in_refs[-2 * outs:-outs], in_refs[-outs:]
    row_refs, delta_refs = in_refs[:-6], in_refs[-6:]
    width = rows_ref.shape[1] // 2
    hidden_units = deltas_ref.shape[1] // 3
    core = lax.axis_index("dp") % 2

    def gather_rows(cols):
        *near_refs, own_ref, far_ref = row_refs
        near = near_rows(*near_refs, cols=cols)
        rows_ref[:, cols] = jnp.concatenate([near, own_ref[:, cols], far_ref[:, cols]], axis=0)

    def gather_deltas(cols):
        at = 0
        for mine, other in zip(delta_refs[::2], delta_refs[1::2]):
            both = in_order(core, mine[:, cols], other[:, cols])
            deltas_ref[at:at + both.shape[0], cols] = both
            at += both.shape[0]

    copies = []
    for name, tile, out_ref, tile_ref in zip(names, tiles, out_refs, tile_refs):
        place = ("down", "gate", "up").index(name)
        of_name = slice(place * hidden_units, (place + 1) * hidden_units)
        gather_deltas(of_name)
        if name == "down":
            gather_rows(slice(width, 2 * width))
        elif name == names[0]:
            gather_rows(slice(0, width))
        for at in range(0, out_ref.shape[0], tile):
            rows = min(tile, out_ref.shape[0] - at)
            if name == "down":
                out = contract_rows(deltas_ref[:, at:at + rows], rows_ref[:, width:])
            else:
                out = contract_rows(rows_ref[:, at:at + rows], deltas_ref[:, of_name])
            tile_ref[at:at + rows] = out
            span = pl.ds(at, rows)
            copies.append(
                pltpu.make_async_copy(tile_ref.at[span], out_ref.at[span], sems.at[len(copies)])
            )
            copies[-1].start()
    for copy in copies:
        copy.wait()


def weight_grads(names, width, hidden_units, slot_count, inputs):
    sizes = {"gate": (width, hidden_units), "up": (width, hidden_units), "down": (hidden_units, width)}
    outs = [shape(*sizes[name], jnp.float32) for name in names]
    tiles = [384 if name == "down" else 128 for name in names]
    copies = sum(-(-out.shape[0] // tile) for out, tile in zip(outs, tiles))
    return pl.pallas_call(
        functools.partial(weight_grads_kernel, names, tiles),
        out_shape=outs,
        in_specs=[pl.BlockSpec(memory_space=pltpu.VMEM)] * len(inputs),
        out_specs=[pl.BlockSpec(memory_space=pltpu.HBM)] * len(outs),
        scratch_shapes=[pltpu.VMEM(out.shape, out.dtype) for out in outs]
        + [
            pltpu.VMEM((slot_count, 2 * width), jnp.bfloat16),
            pltpu.VMEM((slot_count, 3 * hidden_units), jnp.bfloat16),
            pltpu.SemaphoreType.DMA((copies,)),
        ],
        compiler_params=pltpu.CompilerParams(vmem_limit_bytes=24 * 1024 * 1024),
        cost_estimate=pl.CostEstimate(flops=10**7, bytes_accessed=10**7, transcendentals=0),
    )(*inputs)


def token_grad_kernel(chosen_ref, own_ref, from_pair_ref, *refs):
    *group_refs, out_ref = refs
    block = own_ref.shape[0]
    rows = [own_ref[...], from_pair_ref[:block]] + [ref[...] for ref in reversed(group_refs)]
    returned = jnp.concatenate(rows, axis=0)
    out_ref[...] = contract_rows(chosen_ref[...], returned).astype(jnp.bfloat16)


def body_by_all_to_all(tokens, cotangent, expert_ids, route_weights, gate_weight, up_weight, down_weight):
    owners = lax.axis_size("expert")
    width_parts = lax.axis_size("dp")
    tok_rows, top_count = expert_ids.shape
    width = tokens.shape[1]
    capacity = min(tok_rows, max(2, (tok_rows * top_count + owners - 1) // owners))
    slot_count = owners * capacity
    flat_ids = expert_ids.reshape(-1)
    position = jnp.arange(flat_ids.shape[0], dtype=jnp.int32)
    earlier = (flat_ids[:, None] == flat_ids[None, :]) & (position[None, :] < position[:, None])
    rank_pos = jnp.sum(earlier.astype(jnp.int32), axis=1)
    slot_pos = flat_ids * capacity + rank_pos
    pair_select = (slot_pos[:, None] == jnp.arange(slot_count, dtype=jnp.int32)[None, :]).astype(
        jnp.bfloat16
    )
    chosen = jnp.sum(
        pair_select.reshape(tok_rows, top_count, slot_count).astype(jnp.float32), axis=1
    ).astype(jnp.bfloat16)
    pair_tokens = jnp.repeat(tokens, top_count, axis=0)
    pair_scaled = (
        jnp.repeat(cotangent.astype(jnp.float32), top_count, axis=0) * route_weights
    ).astype(jnp.bfloat16)
    payload = jnp.concatenate([pair_tokens, pair_scaled], axis=1)
    send = contract_rows(pair_select, payload).astype(jnp.bfloat16)
    slots = lax.all_to_all(send, "expert", split_axis=0, concat_axis=0, tiled=True)

    core = lax.axis_index("dp") % 2
    half = slot_count // 2
    mine_slots = lax.dynamic_slice_in_dim(slots, core * half, half, 0)
    other_slots = lax.dynamic_slice_in_dim(slots, (1 - core) * half, half, 0)
    w_gate = gate_weight[0]
    w_up = up_weight[0]
    w_down = down_weight[0]

    def partial_sums(rows):
        feats, cots = rows[:, :width], rows[:, width:]
        return (
            jnp.dot(feats, w_gate, preferred_element_type=jnp.float32),
            jnp.dot(feats, w_up, preferred_element_type=jnp.float32),
            contract_cols(cots, w_down),
        )

    def pack(parts):
        return jnp.stack([part.astype(jnp.bfloat16) for part in parts])

    received = swap(pack(partial_sums(other_slots)), 1)
    sums = jnp.stack(partial_sums(mine_slots)) + received.astype(jnp.float32)
    bit = 2
    while bit < width_parts:
        sums = sums + swap(sums.astype(jnp.bfloat16), bit).astype(jnp.float32)
        bit *= 2
    mine = jnp.stack(local_deltas(sums[0], sums[1], sums[2]))
    other = swap(mine, 1)
    hidden, gate_delta, up_delta = jnp.concatenate([mine, other], axis=1)
    both = jnp.concatenate([mine_slots, other_slots], axis=0)
    slot_grad = (contract_cols(gate_delta, w_gate) + contract_cols(up_delta, w_up)).astype(
        jnp.bfloat16
    )
    slot_grad = jnp.where(
        core == 0, slot_grad, jnp.concatenate([slot_grad[half:], slot_grad[:half]], axis=0)
    )
    returned = lax.all_to_all(slot_grad, "expert", split_axis=0, concat_axis=0, tiled=True)
    feats, cots = both[:, :width], both[:, width:]
    gate_grad = contract_rows(feats, gate_delta)
    up_grad = contract_rows(feats, up_delta)
    down_grad = contract_rows(hidden, cots)
    token_grad = jnp.dot(chosen, returned, preferred_element_type=jnp.float32).astype(jnp.bfloat16)
    return (token_grad, gate_grad[None], up_grad[None], down_grad[None])


def body_by_pairs(tokens, cotangent, expert_ids, route_weights, gate_weight, up_weight, down_weight):
    owners = lax.axis_size("expert")
    width_parts = lax.axis_size("dp")
    tok_rows, _ = expert_ids.shape
    width = tokens.shape[1]
    hidden_units = gate_weight.shape[2]
    capacity = min(tok_rows, max(2, (tok_rows + owners - 1) // owners))
    slot_count = owners * capacity
    half = owners // 2

    far_first = [0] + list(reversed(range(1, half)))
    chosen, own, pair_block, *groups = call(
        functools.partial(dispatch_kernel, owners, capacity),
        (shape(slot_count, tok_rows),)
        + (shape(capacity, 2 * width),) * 2
        + (shape(2 * capacity, 2 * width),) * (half - 1),
        expert_ids.reshape(1, tok_rows),
        route_weights.reshape(1, tok_rows),
        tokens,
        cotangent,
        far=range(4),
        scratch=[
            pltpu.VMEM((1, tok_rows), jnp.int32),
            pltpu.VMEM((1, tok_rows), jnp.float32),
            pltpu.VMEM((tok_rows, width), jnp.bfloat16),
            pltpu.VMEM((tok_rows, width), jnp.bfloat16),
            pltpu.SemaphoreType.DMA((4,)),
        ],
    )
    down, gate, up = call(
        load_kernel,
        (shape(width, hidden_units),) * 3,
        down_weight[0],
        gate_weight[0],
        up_weight[0],
        chosen,
        far=range(3),
        scratch=[
            pltpu.VMEM((hidden_units, width), jnp.bfloat16),
            pltpu.SemaphoreType.DMA((3,)),
        ],
        cost=10**7,
    )
    groups = [swap(groups[j - 1], 2 * j, "expert") for j in far_first[1:]]
    from_pair = swap(pair_block, 1, "expert")
    groups = after(groups, from_pair)
    seconds = jnp.concatenate([group[capacity:] for group in groups], axis=0)
    by_pair = swap(after(seconds, up), 1, "expert")

    near = [from_pair] + groups

    def pieces(*parts):
        shapes = []
        for part in parts:
            shapes += [shape(part, 3 * hidden_units, jnp.float32), shape(part, 3 * hidden_units)]
        return shapes

    def sums_over_cores(rows, cost, *parts):
        mine, other = call(
            products_kernel, pieces(sum(parts)), *rows, gate, up, down, cost=cost
        )
        out = call(sums_kernel, pieces(*parts), mine, swap(other, 1))
        return list(zip(out[::2], out[1::2]))

    def exchanged(sums, marker):
        bit = 2
        while 2 * bit < width_parts:
            sums, marker = call(sums_kernel, pieces(sums.shape[0]), sums, swap(marker, bit))
            bit *= 2
        return sums, swap(marker, bit)

    def deltas_of(sums, received, cost):
        return call(deltas_kernel, shape(*sums.shape), sums, received, cost=cost)

    own_half = capacity // 2
    own_sums, near_sums = sums_over_cores(
        near + [own], 1, own_half, half * capacity // 2
    )
    (far_sums,) = sums_over_cores([by_pair], FAR_PRODUCTS_COST, (half - 1) * capacity // 2)
    near_sums, far_sums = exchanged(*near_sums), exchanged(*far_sums)

    near_mine = deltas_of(*near_sums, 1)
    turned = call(turn_kernel, (shape(hidden_units, width),) * 2, *after((gate, up), near_mine))
    own_sums = exchanged(own_sums[0], after(own_sums[1], turned[0]))
    near_deltas = near_mine, swap(near_mine, 1)
    far_mine = after(deltas_of(*far_sums, FAR_DELTAS_COST), near_deltas[1])
    far_deltas = far_mine, swap(far_mine, 1)
    block = shape(capacity, width)
    grads = call(slot_grad_kernel, (block,) * half, *near_deltas, *turned)
    own_mine = deltas_of(after(own_sums[0], grads[0]), own_sums[1], OWN_DELTAS_COST)
    own_deltas = own_mine, swap(own_mine, 1)
    (own_grad,) = call(slot_grad_kernel, (block,), *own_deltas, *turned)
    to_pair = call(
        far_grad_kernel,
        shape(half * capacity, width),
        *after(far_deltas, own_mine),
        *turned,
        grads[-1],
    )
    deltas = near_deltas + own_deltas + far_deltas

    returned_pair = swap(to_pair, 1, "expert")
    sizes = (width, hidden_units, slot_count, (*near, own, by_pair, *deltas))
    (gate_grad,) = weight_grads(("gate",), *sizes)
    returned_pair = after(returned_pair, (gate_grad, own_grad))
    returned = {}
    for place, j in enumerate(far_first[1:], 1):
        more = returned_pair[place * capacity:(place + 1) * capacity]
        returned[j] = swap(jnp.concatenate([grads[place - 1], more], axis=0), 2 * j, "expert")
    up_grad, down_grad = weight_grads(("up", "down"), *sizes)
    token_grad = call(
        token_grad_kernel,
        shape(tok_rows, width),
        chosen,
        own_grad,
        returned_pair,
        *[returned[j] for j in far_first[1:]],
    )
    return (token_grad, gate_grad[None], up_grad[None], down_grad[None])


def body(tokens, cotangent, expert_ids, *rest):
    owners = lax.axis_size("expert")
    width_parts = lax.axis_size("dp")
    tok_rows, top_count = expert_ids.shape
    by_pairs = (
        top_count == 1
        and owners >= 8
        and owners & (owners - 1) == 0
        and width_parts >= 4
        and tok_rows % (16 * owners) == 0
    )
    chosen = body_by_pairs if by_pairs else body_by_all_to_all
    return chosen(tokens, cotangent, expert_ids, *rest)


def solution(mesh):
    return jax.shard_map(
        body,
        mesh=mesh,
        in_specs=(
            P("expert", "dp"),
            P("expert", "dp"),
            P("expert", None),
            P("expert", None),
            P("expert", "dp", None),
            P("expert", "dp", None),
            P("expert", None, "dp"),
        ),
        out_specs=(
            P("expert", "dp"),
            P("expert", "dp", None),
            P("expert", "dp", None),
            P("expert", None, "dp"),
        ),
        check_vma=False,
    )
```

```python
import functools

import jax
import jax.numpy as jnp
from jax import lax
from jax.experimental import pallas as pl
from jax.experimental.pallas import tpu as pltpu
from jax.sharding import PartitionSpec as P


def contract_rows(left, right):
    return lax.dot_general(
        left, right, (((0,), (0,)), ((), ())), preferred_element_type=jnp.float32
    )


def contract_cols(left, right):
    return lax.dot_general(
        left, right, (((1,), (1,)), ((), ())), preferred_element_type=jnp.float32
    )


def local_deltas(gate_pre, up_pre, hidden_grad):
    sigma = jax.nn.sigmoid(gate_pre)
    activated = gate_pre * sigma
    hidden = (activated * up_pre).astype(jnp.bfloat16)
    gate_delta = (hidden_grad * up_pre * sigma * (1.0 + gate_pre * (1.0 - sigma))).astype(
        jnp.bfloat16
    )
    up_delta = (hidden_grad * activated).astype(jnp.bfloat16)
    return (hidden, gate_delta, up_delta)


def swap(value, bit, axis="dp"):
    size = lax.axis_size(axis)
    return lax.ppermute(value, axis, [(i, i ^ bit) for i in range(size)])


FAR_PRODUCTS_COST = 3 * 10**8
FAR_DELTAS_COST = 8 * 10**8
OWN_DELTAS_COST = 11 * 10**8


def after(values, marker):
    return lax.optimization_barrier((values, marker))[0]


def call(kernel, outs, *args, cost=1, far=(), scratch=()):
    spaces = [pltpu.HBM if place in far else pltpu.VMEM for place in range(len(args))]
    args = [
        pltpu.with_memory_space_constraint(arg, pltpu.HBM) if place in far else arg
        for place, arg in enumerate(args)
    ]
    return pl.pallas_call(
        kernel,
        out_shape=outs,
        in_specs=[pl.BlockSpec(memory_space=space) for space in spaces],
        scratch_shapes=scratch,
        compiler_params=pltpu.CompilerParams(vmem_limit_bytes=24 * 1024 * 1024),
        cost_estimate=pl.CostEstimate(flops=cost, bytes_accessed=cost, transcendentals=0),
    )(*args)


def shape(rows, cols, dtype=jnp.bfloat16):
    return jax.ShapeDtypeStruct((rows, cols), dtype)


def dispatch_kernel(owners, capacity, ids_hbm, weights_hbm, tokens_hbm, cotangent_hbm, *refs):
    chosen_ref, *out_refs, ids_ref, weights_ref, tokens_ref, cotangent_ref, sems = refs
    copies = [
        pltpu.make_async_copy(source, target, sems.at[place])
        for place, (source, target) in enumerate(
            (
                (ids_hbm, ids_ref),
                (weights_hbm, weights_ref),
                (tokens_hbm, tokens_ref),
                (cotangent_hbm, cotangent_ref),
            )
        )
    ]
    for copy in copies:
        copy.start()
    pairs = ids_ref.shape[1]
    width = tokens_ref.shape[1]
    slot_count = owners * capacity
    me = lax.axis_index("expert")
    before = lax.broadcasted_iota(jnp.int32, (pairs, pairs), 0) < lax.broadcasted_iota(
        jnp.int32, (pairs, pairs), 1
    )
    before = before.astype(jnp.float32).astype(jnp.bfloat16)
    experts = lax.broadcasted_iota(jnp.int32, (owners, pairs), 0)
    slots = lax.broadcasted_iota(jnp.int32, (slot_count, pairs), 0)
    copies[0].wait()
    ids = ids_ref[...]
    named = (ids == experts).astype(jnp.float32)
    counts = jnp.dot(named.astype(jnp.bfloat16), before, preferred_element_type=jnp.float32)
    rank = jnp.sum(named * counts, axis=0, keepdims=True).astype(jnp.int32)
    chosen = (slots == (ids ^ me) * capacity + rank).astype(jnp.float32)
    select = chosen.astype(jnp.bfloat16)
    chosen_ref[...] = select
    for copy in copies[1:]:
        copy.wait()
    scale = jnp.sum(chosen * weights_ref[...], axis=1, keepdims=True)
    feats = jnp.dot(select, tokens_ref[...], preferred_element_type=jnp.float32)
    cots = jnp.dot(select, cotangent_ref[...], preferred_element_type=jnp.float32) * scale
    at = 0
    for out_ref in out_refs:
        rows = slice(at, at + out_ref.shape[0])
        out_ref[:, :width] = feats[rows].astype(jnp.bfloat16)
        out_ref[:, width:] = cots[rows].astype(jnp.bfloat16)
        at += out_ref.shape[0]


def load_kernel(down_hbm, gate_hbm, up_hbm, marker_hbm, turned_ref, gate_ref, up_ref, down_ref, sems):
    copies = [
        pltpu.make_async_copy(source, target, sems.at[place])
        for place, (source, target) in enumerate(
            ((down_hbm, down_ref), (gate_hbm, gate_ref), (up_hbm, up_ref))
        )
    ]
    for copy in copies:
        copy.start()
    copies[0].wait()
    turned_ref[...] = down_ref[...].T
    for copy in copies[1:]:
        copy.wait()


def turn_kernel(*refs):
    half = len(refs) // 2
    for source, target in zip(refs[:half], refs[half:]):
        target[...] = source[...].T


def near_rows(from_pair_ref, *group_refs, cols=slice(None)):
    halves = [ref[:ref.shape[0] // 2, cols] for ref in group_refs]
    return jnp.concatenate(halves + [from_pair_ref[:, cols]], axis=0)


def with_own_rows(own, rows):
    part, half = own.shape[0] // 2, rows.shape[0] // 2
    return jnp.concatenate([own[:part], rows[:half], own[part:], rows[half:]], axis=0)


def products_kernel(*refs):
    *row_refs, gate_ref, up_ref, down_ref, mine_ref, other_ref = refs
    rows = row_refs[-1][...]
    if len(row_refs) > 1:
        rows = with_own_rows(rows, near_rows(*row_refs[:-1]))
    half = rows.shape[0] // 2
    width = rows.shape[1] // 2
    hidden_units = gate_ref.shape[1]
    core = lax.axis_index("dp") % 2
    feats, cots = rows[:, :width], rows[:, width:]
    for place, weight_ref in enumerate((gate_ref, up_ref, down_ref)):
        cols = slice(place * hidden_units, (place + 1) * hidden_units)
        rows = feats if place < 2 else cots
        out = jnp.dot(rows, weight_ref[...], preferred_element_type=jnp.float32)
        low, high = out[:half], out[half:]
        mine_ref[:, cols] = jnp.where(core == 0, low, high)
        other_ref[:, cols] = jnp.where(core == 0, high, low).astype(jnp.bfloat16)


def sums_kernel(mine_ref, received_ref, *refs):
    sums = mine_ref[...] + received_ref[...].astype(jnp.float32)
    at = 0
    for sums_ref, packed_ref in zip(refs[::2], refs[1::2]):
        part = sums[at:at + sums_ref.shape[0]]
        sums_ref[...] = part
        packed_ref[...] = part.astype(jnp.bfloat16)
        at += part.shape[0]


def deltas_kernel(sums_ref, received_ref, *out_refs):
    hidden_units = sums_ref.shape[1] // 3
    cols = [slice(i * hidden_units, (i + 1) * hidden_units) for i in range(3)]
    parts = [sums_ref[:, c] + received_ref[:, c].astype(jnp.float32) for c in cols]
    hidden, gate_delta, up_delta = local_deltas(*parts)
    if len(out_refs) == 1:
        values = [hidden, gate_delta, up_delta]
    else:
        out_refs[0][...] = hidden
        values = [gate_delta, up_delta]
    for c, value in zip(cols, values):
        out_refs[-1][:, c] = value


def in_order(core, mine, other):
    return jnp.concatenate(
        [jnp.where(core == 0, mine, other), jnp.where(core == 0, other, mine)], axis=0
    )


def slot_grad_rows(mine_ref, other_ref, gate_ref, up_ref):
    hidden_units = gate_ref.shape[0]
    rows = in_order(lax.axis_index("dp") % 2, mine_ref[...], other_ref[...])
    by_gate, by_up = rows[:, -2 * hidden_units:-hidden_units], rows[:, -hidden_units:]
    return (
        jnp.dot(by_gate, gate_ref[...], preferred_element_type=jnp.float32)
        + jnp.dot(by_up, up_ref[...], preferred_element_type=jnp.float32)
    ).astype(jnp.bfloat16)


def slot_grad_kernel(mine_ref, other_ref, gate_ref, up_ref, *block_refs):
    out = slot_grad_rows(mine_ref, other_ref, gate_ref, up_ref)
    block = block_refs[0].shape[0]
    for place, ref in enumerate(block_refs):
        ref[...] = out[place * block:(place + 1) * block]


def far_grad_kernel(mine_ref, other_ref, gate_ref, up_ref, pair_ref, out_ref):
    block = pair_ref.shape[0]
    out_ref[:block] = pair_ref[...]
    out_ref[block:] = slot_grad_rows(mine_ref, other_ref, gate_ref, up_ref)


def weight_grads_kernel(names, tiles, *refs):
    outs = len(names)
    *in_refs, rows_ref, deltas_ref, sems = refs
    in_refs, out_refs, tile_refs = in_refs[:-2 * outs], in_refs[-2 * outs:-outs], in_refs[-outs:]
    row_refs, delta_refs = in_refs[:-8], in_refs[-8:]
    width = rows_ref.shape[1] // 2
    hidden_units = deltas_ref.shape[1] // 3
    core = lax.axis_index("dp") % 2

    def gather_rows(cols):
        *near_refs, own_ref, far_ref = row_refs
        near = near_rows(*near_refs, cols=cols)
        rows_ref[:, cols] = jnp.concatenate([near, own_ref[:, cols], far_ref[:, cols]], axis=0)

    def gather_deltas(cols):
        at = 0
        for place in range(3):
            mine, other, of = *delta_refs[2 * place:2 * place + 2], cols
            if place == 2 and cols.start:
                mine, other = delta_refs[6:]
                of = slice(cols.start - hidden_units, cols.stop - hidden_units)
            both = in_order(core, mine[:, of], other[:, of])
            deltas_ref[at:at + both.shape[0], cols] = both
            at += both.shape[0]

    copies = []
    for name, tile, out_ref, tile_ref in zip(names, tiles, out_refs, tile_refs):
        place = ("down", "gate", "up").index(name)
        of_name = slice(place * hidden_units, (place + 1) * hidden_units)
        gather_deltas(of_name)
        if name == "down":
            gather_rows(slice(width, 2 * width))
        elif name == names[0]:
            gather_rows(slice(0, width))
        for at in range(0, out_ref.shape[0], tile):
            rows = min(tile, out_ref.shape[0] - at)
            if name == "down":
                out = contract_rows(deltas_ref[:, at:at + rows], rows_ref[:, width:])
            else:
                out = contract_rows(rows_ref[:, at:at + rows], deltas_ref[:, of_name])
            tile_ref[at:at + rows] = out
            span = pl.ds(at, rows)
            copies.append(
                pltpu.make_async_copy(tile_ref.at[span], out_ref.at[span], sems.at[len(copies)])
            )
            copies[-1].start()
    for copy in copies:
        copy.wait()


def weight_grads(names, width, hidden_units, slot_count, inputs):
    sizes = {"gate": (width, hidden_units), "up": (width, hidden_units), "down": (hidden_units, width)}
    outs = [shape(*sizes[name], jnp.float32) for name in names]
    tiles = [384 if name == "down" else 128 for name in names]
    copies = sum(-(-out.shape[0] // tile) for out, tile in zip(outs, tiles))
    return pl.pallas_call(
        functools.partial(weight_grads_kernel, names, tiles),
        out_shape=outs,
        in_specs=[pl.BlockSpec(memory_space=pltpu.VMEM)] * len(inputs),
        out_specs=[pl.BlockSpec(memory_space=pltpu.HBM)] * len(outs),
        scratch_shapes=[pltpu.VMEM(out.shape, out.dtype) for out in outs]
        + [
            pltpu.VMEM((slot_count, 2 * width), jnp.bfloat16),
            pltpu.VMEM((slot_count, 3 * hidden_units), jnp.bfloat16),
            pltpu.SemaphoreType.DMA((copies,)),
        ],
        compiler_params=pltpu.CompilerParams(vmem_limit_bytes=24 * 1024 * 1024),
        cost_estimate=pl.CostEstimate(flops=10**7, bytes_accessed=10**7, transcendentals=0),
    )(*inputs)


def token_grad_kernel(chosen_ref, own_ref, from_pair_ref, *refs):
    *group_refs, out_ref = refs
    block = own_ref.shape[0]
    rows = [own_ref[...], from_pair_ref[:block]] + [ref[...] for ref in reversed(group_refs)]
    returned = jnp.concatenate(rows, axis=0)
    out = jnp.dot(chosen_ref[...], returned, preferred_element_type=jnp.float32)
    out_ref[...] = out.astype(jnp.bfloat16)


def body_by_all_to_all(tokens, cotangent, expert_ids, route_weights, gate_weight, up_weight, down_weight):
    owners = lax.axis_size("expert")
    width_parts = lax.axis_size("dp")
    tok_rows, top_count = expert_ids.shape
    width = tokens.shape[1]
    capacity = min(tok_rows, max(2, (tok_rows * top_count + owners - 1) // owners))
    slot_count = owners * capacity
    flat_ids = expert_ids.reshape(-1)
    position = jnp.arange(flat_ids.shape[0], dtype=jnp.int32)
    earlier = (flat_ids[:, None] == flat_ids[None, :]) & (position[None, :] < position[:, None])
    rank_pos = jnp.sum(earlier.astype(jnp.int32), axis=1)
    slot_pos = flat_ids * capacity + rank_pos
    pair_select = (slot_pos[:, None] == jnp.arange(slot_count, dtype=jnp.int32)[None, :]).astype(
        jnp.bfloat16
    )
    chosen = jnp.sum(
        pair_select.reshape(tok_rows, top_count, slot_count).astype(jnp.float32), axis=1
    ).astype(jnp.bfloat16)
    pair_tokens = jnp.repeat(tokens, top_count, axis=0)
    pair_scaled = (
        jnp.repeat(cotangent.astype(jnp.float32), top_count, axis=0) * route_weights
    ).astype(jnp.bfloat16)
    payload = jnp.concatenate([pair_tokens, pair_scaled], axis=1)
    send = contract_rows(pair_select, payload).astype(jnp.bfloat16)
    slots = lax.all_to_all(send, "expert", split_axis=0, concat_axis=0, tiled=True)

    core = lax.axis_index("dp") % 2
    half = slot_count // 2
    mine_slots = lax.dynamic_slice_in_dim(slots, core * half, half, 0)
    other_slots = lax.dynamic_slice_in_dim(slots, (1 - core) * half, half, 0)
    w_gate = gate_weight[0]
    w_up = up_weight[0]
    w_down = down_weight[0]

    def partial_sums(rows):
        feats, cots = rows[:, :width], rows[:, width:]
        return (
            jnp.dot(feats, w_gate, preferred_element_type=jnp.float32),
            jnp.dot(feats, w_up, preferred_element_type=jnp.float32),
            contract_cols(cots, w_down),
        )

    def pack(parts):
        return jnp.stack([part.astype(jnp.bfloat16) for part in parts])

    received = swap(pack(partial_sums(other_slots)), 1)
    sums = jnp.stack(partial_sums(mine_slots)) + received.astype(jnp.float32)
    bit = 2
    while bit < width_parts:
        sums = sums + swap(sums.astype(jnp.bfloat16), bit).astype(jnp.float32)
        bit *= 2
    mine = jnp.stack(local_deltas(sums[0], sums[1], sums[2]))
    other = swap(mine, 1)
    hidden, gate_delta, up_delta = jnp.concatenate([mine, other], axis=1)
    both = jnp.concatenate([mine_slots, other_slots], axis=0)
    slot_grad = (contract_cols(gate_delta, w_gate) + contract_cols(up_delta, w_up)).astype(
        jnp.bfloat16
    )
    slot_grad = jnp.where(
        core == 0, slot_grad, jnp.concatenate([slot_grad[half:], slot_grad[:half]], axis=0)
    )
    returned = lax.all_to_all(slot_grad, "expert", split_axis=0, concat_axis=0, tiled=True)
    feats, cots = both[:, :width], both[:, width:]
    gate_grad = contract_rows(feats, gate_delta)
    up_grad = contract_rows(feats, up_delta)
    down_grad = contract_rows(hidden, cots)
    token_grad = jnp.dot(chosen, returned, preferred_element_type=jnp.float32).astype(jnp.bfloat16)
    return (token_grad, gate_grad[None], up_grad[None], down_grad[None])


def body_by_pairs(tokens, cotangent, expert_ids, route_weights, gate_weight, up_weight, down_weight):
    owners = lax.axis_size("expert")
    width_parts = lax.axis_size("dp")
    tok_rows, _ = expert_ids.shape
    width = tokens.shape[1]
    hidden_units = gate_weight.shape[2]
    capacity = min(tok_rows, max(2, (tok_rows + owners - 1) // owners))
    slot_count = owners * capacity
    half = owners // 2

    far_first = [0] + list(reversed(range(1, half)))
    chosen, own, pair_block, *groups = call(
        functools.partial(dispatch_kernel, owners, capacity),
        (shape(slot_count, tok_rows),)
        + (shape(capacity, 2 * width),) * 2
        + (shape(2 * capacity, 2 * width),) * (half - 1),
        expert_ids.reshape(1, tok_rows),
        route_weights.reshape(1, tok_rows),
        tokens,
        cotangent,
        far=range(4),
        scratch=[
            pltpu.VMEM((1, tok_rows), jnp.int32),
            pltpu.VMEM((1, tok_rows), jnp.float32),
            pltpu.VMEM((tok_rows, width), jnp.bfloat16),
            pltpu.VMEM((tok_rows, width), jnp.bfloat16),
            pltpu.SemaphoreType.DMA((4,)),
        ],
    )
    down, gate, up = call(
        load_kernel,
        (shape(width, hidden_units),) * 3,
        down_weight[0],
        gate_weight[0],
        up_weight[0],
        chosen,
        far=range(3),
        scratch=[
            pltpu.VMEM((hidden_units, width), jnp.bfloat16),
            pltpu.SemaphoreType.DMA((3,)),
        ],
        cost=10**7,
    )
    groups = [swap(groups[j - 1], 2 * j, "expert") for j in far_first[1:]]
    from_pair = swap(pair_block, 1, "expert")
    groups = after(groups, from_pair)
    seconds = jnp.concatenate([group[capacity:] for group in groups], axis=0)
    by_pair = swap(after(seconds, up), 1, "expert")

    near = [from_pair] + groups

    def pieces(*parts):
        shapes = []
        for part in parts:
            shapes += [shape(part, 3 * hidden_units, jnp.float32), shape(part, 3 * hidden_units)]
        return shapes

    def sums_over_cores(rows, cost, *parts):
        mine, other = call(
            products_kernel, pieces(sum(parts)), *rows, gate, up, down, cost=cost
        )
        out = call(sums_kernel, pieces(*parts), mine, swap(other, 1))
        return list(zip(out[::2], out[1::2]))

    def exchanged(sums, marker):
        bit = 2
        while 2 * bit < width_parts:
            sums, marker = call(sums_kernel, pieces(sums.shape[0]), sums, swap(marker, bit))
            bit *= 2
        return sums, swap(marker, bit)

    def deltas_of(sums, received, cost):
        return call(deltas_kernel, shape(*sums.shape), sums, received, cost=cost)

    own_half = capacity // 2
    own_sums, near_sums = sums_over_cores(
        near + [own], 1, own_half, half * capacity // 2
    )
    (far_sums,) = sums_over_cores([by_pair], FAR_PRODUCTS_COST, (half - 1) * capacity // 2)
    near_sums, far_sums = exchanged(*near_sums), exchanged(*far_sums)

    near_mine = deltas_of(*near_sums, 1)
    *turned, chosen = call(
        turn_kernel,
        (shape(hidden_units, width),) * 2 + (shape(tok_rows, slot_count),),
        *after((gate, up, chosen), near_mine),
    )
    own_sums = exchanged(own_sums[0], after(own_sums[1], turned[0]))
    near_deltas = near_mine, swap(near_mine, 1)
    part = far_sums[0].shape[0]
    far_hidden, far_mine = after(
        call(
            deltas_kernel,
            (shape(part, hidden_units), shape(part, 2 * hidden_units)),
            *far_sums,
            cost=FAR_DELTAS_COST,
        ),
        near_deltas[1],
    )
    far_deltas = far_mine, swap(far_mine, 1)
    hidden_pair = far_hidden, swap(far_hidden, 1)
    block = shape(capacity, width)
    grads = call(slot_grad_kernel, (block,) * half, *near_deltas, *turned)
    own_mine = deltas_of(after(own_sums[0], grads[0]), own_sums[1], OWN_DELTAS_COST)
    own_deltas = own_mine, swap(own_mine, 1)
    (own_grad,) = call(slot_grad_kernel, (block,), *own_deltas, *turned)
    to_pair = call(
        far_grad_kernel,
        shape(half * capacity, width),
        *after(far_deltas, own_mine),
        *turned,
        grads[-1],
    )
    without_hidden = near_deltas + own_deltas + far_deltas + far_deltas
    deltas = near_deltas + own_deltas + hidden_pair + far_deltas

    returned_pair = swap(to_pair, 1, "expert")
    rows = (*near, own, by_pair)
    sizes = (width, hidden_units, slot_count)
    (gate_grad,) = weight_grads(("gate",), *sizes, (*rows, *without_hidden))
    returned_pair = after(returned_pair, (gate_grad, own_grad))
    returned = {}
    for place, j in enumerate(far_first[1:], 1):
        more = returned_pair[place * capacity:(place + 1) * capacity]
        returned[j] = swap(jnp.concatenate([grads[place - 1], more], axis=0), 2 * j, "expert")
    up_grad, down_grad = weight_grads(("up", "down"), *sizes, (*rows, *deltas))
    token_grad = call(
        token_grad_kernel,
        shape(tok_rows, width),
        chosen,
        own_grad,
        returned_pair,
        *[returned[j] for j in far_first[1:]],
    )
    return (token_grad, gate_grad[None], up_grad[None], down_grad[None])


def body(tokens, cotangent, expert_ids, *rest):
    owners = lax.axis_size("expert")
    width_parts = lax.axis_size("dp")
    tok_rows, top_count = expert_ids.shape
    by_pairs = (
        top_count == 1
        and owners >= 8
        and owners & (owners - 1) == 0
        and width_parts >= 4
        and tok_rows % (16 * owners) == 0
    )
    chosen = body_by_pairs if by_pairs else body_by_all_to_all
    return chosen(tokens, cotangent, expert_ids, *rest)


def solution(mesh):
    return jax.shard_map(
        body,
        mesh=mesh,
        in_specs=(
            P("expert", "dp"),
            P("expert", "dp"),
            P("expert", None),
            P("expert", None),
            P("expert", "dp", None),
            P("expert", "dp", None),
            P("expert", None, "dp"),
        ),
        out_specs=(
            P("expert", "dp"),
            P("expert", "dp", None),
            P("expert", "dp", None),
            P("expert", None, "dp"),
        ),
        check_vma=False,
    )
```

```python
import functools

import jax
import jax.numpy as jnp
from jax import lax
from jax.experimental import pallas as pl
from jax.experimental.pallas import tpu as pltpu
from jax.sharding import PartitionSpec as P


def contract_rows(left, right):
    return lax.dot_general(
        left, right, (((0,), (0,)), ((), ())), preferred_element_type=jnp.float32
    )


def contract_cols(left, right):
    return lax.dot_general(
        left, right, (((1,), (1,)), ((), ())), preferred_element_type=jnp.float32
    )


def local_deltas(gate_pre, up_pre, hidden_grad):
    sigma = jax.nn.sigmoid(gate_pre)
    activated = gate_pre * sigma
    hidden = (activated * up_pre).astype(jnp.bfloat16)
    gate_delta = (hidden_grad * up_pre * sigma * (1.0 + gate_pre * (1.0 - sigma))).astype(
        jnp.bfloat16
    )
    up_delta = (hidden_grad * activated).astype(jnp.bfloat16)
    return (hidden, gate_delta, up_delta)


def swap(value, bit, axis="dp"):
    size = lax.axis_size(axis)
    return lax.ppermute(value, axis, [(i, i ^ bit) for i in range(size)])


FAR_PRODUCTS_COST = 3 * 10**8
FAR_DELTAS_COST = 8 * 10**8
OWN_DELTAS_COST = 11 * 10**8


def after(values, marker):
    return lax.optimization_barrier((values, marker))[0]


def call(kernel, outs, *args, cost=1, far=(), scratch=()):
    spaces = [pltpu.HBM if place in far else pltpu.VMEM for place in range(len(args))]
    args = [
        pltpu.with_memory_space_constraint(arg, pltpu.HBM) if place in far else arg
        for place, arg in enumerate(args)
    ]
    return pl.pallas_call(
        kernel,
        out_shape=outs,
        in_specs=[pl.BlockSpec(memory_space=space) for space in spaces],
        scratch_shapes=scratch,
        compiler_params=pltpu.CompilerParams(vmem_limit_bytes=24 * 1024 * 1024),
        cost_estimate=pl.CostEstimate(flops=cost, bytes_accessed=cost, transcendentals=0),
    )(*args)


def shape(rows, cols, dtype=jnp.bfloat16):
    return jax.ShapeDtypeStruct((rows, cols), dtype)


def dispatch_kernel(owners, capacity, ids_hbm, weights_hbm, tokens_hbm, cotangent_hbm, *refs):
    chosen_ref, *out_refs, ids_ref, weights_ref, tokens_ref, cotangent_ref, sems = refs
    copies = [
        pltpu.make_async_copy(source, target, sems.at[place])
        for place, (source, target) in enumerate(
            (
                (ids_hbm, ids_ref),
                (weights_hbm, weights_ref),
                (tokens_hbm, tokens_ref),
                (cotangent_hbm, cotangent_ref),
            )
        )
    ]
    for copy in copies:
        copy.start()
    pairs = ids_ref.shape[1]
    width = tokens_ref.shape[1]
    slot_count = owners * capacity
    me = lax.axis_index("expert")
    before = lax.broadcasted_iota(jnp.int32, (pairs, pairs), 0) < lax.broadcasted_iota(
        jnp.int32, (pairs, pairs), 1
    )
    before = before.astype(jnp.float32).astype(jnp.bfloat16)
    experts = lax.broadcasted_iota(jnp.int32, (owners, pairs), 0)
    slots = lax.broadcasted_iota(jnp.int32, (slot_count, pairs), 0)
    copies[0].wait()
    ids = ids_ref[...]
    named = (ids == experts).astype(jnp.float32)
    counts = jnp.dot(named.astype(jnp.bfloat16), before, preferred_element_type=jnp.float32)
    rank = jnp.sum(named * counts, axis=0, keepdims=True).astype(jnp.int32)
    chosen = (slots == (ids ^ me) * capacity + rank).astype(jnp.float32)
    select = chosen.astype(jnp.bfloat16)
    chosen_ref[...] = select
    for copy in copies[1:]:
        copy.wait()
    scale = jnp.sum(chosen * weights_ref[...], axis=1, keepdims=True)
    feats = jnp.dot(select, tokens_ref[...], preferred_element_type=jnp.float32)
    cots = jnp.dot(select, cotangent_ref[...], preferred_element_type=jnp.float32) * scale
    at = 0
    for out_ref in out_refs:
        rows = slice(at, at + out_ref.shape[0])
        out_ref[:, :width] = feats[rows].astype(jnp.bfloat16)
        out_ref[:, width:] = cots[rows].astype(jnp.bfloat16)
        at += out_ref.shape[0]


def load_kernel(down_hbm, gate_hbm, up_hbm, marker_hbm, turned_ref, gate_ref, up_ref, down_ref, sems):
    copies = [
        pltpu.make_async_copy(source, target, sems.at[place])
        for place, (source, target) in enumerate(
            ((down_hbm, down_ref), (gate_hbm, gate_ref), (up_hbm, up_ref))
        )
    ]
    for copy in copies:
        copy.start()
    copies[0].wait()
    turned_ref[...] = down_ref[...].T
    for copy in copies[1:]:
        copy.wait()


def turn_kernel(*refs):
    half = len(refs) // 2
    for source, target in zip(refs[:half], refs[half:]):
        target[...] = source[...].T


def near_rows(from_pair_ref, *group_refs, cols=slice(None)):
    halves = [ref[:ref.shape[0] // 2, cols] for ref in group_refs]
    return jnp.concatenate(halves + [from_pair_ref[:, cols]], axis=0)


def with_own_rows(own, rows):
    part, half = own.shape[0] // 2, rows.shape[0] // 2
    return jnp.concatenate([own[:part], rows[:half], own[part:], rows[half:]], axis=0)


def products_kernel(*refs):
    *row_refs, gate_ref, up_ref, down_ref, mine_ref, other_ref = refs
    rows = row_refs[-1][...]
    if len(row_refs) > 1:
        rows = with_own_rows(rows, near_rows(*row_refs[:-1]))
    half = rows.shape[0] // 2
    width = rows.shape[1] // 2
    hidden_units = gate_ref.shape[1]
    core = lax.axis_index("dp") % 2
    feats, cots = rows[:, :width], rows[:, width:]
    for place, weight_ref in enumerate((gate_ref, up_ref, down_ref)):
        cols = slice(place * hidden_units, (place + 1) * hidden_units)
        rows = feats if place < 2 else cots
        out = jnp.dot(rows, weight_ref[...], preferred_element_type=jnp.float32)
        low, high = out[:half], out[half:]
        mine_ref[:, cols] = jnp.where(core == 0, low, high)
        other_ref[:, cols] = jnp.where(core == 0, high, low).astype(jnp.bfloat16)


def sums_kernel(mine_ref, received_ref, *refs):
    sums = mine_ref[...] + received_ref[...].astype(jnp.float32)
    at = 0
    for sums_ref, packed_ref in zip(refs[::2], refs[1::2]):
        part = sums[at:at + sums_ref.shape[0]]
        sums_ref[...] = part
        packed_ref[...] = part.astype(jnp.bfloat16)
        at += part.shape[0]


def deltas_kernel(sums_ref, received_ref, *out_refs):
    hidden_units = sums_ref.shape[1] // 3
    cols = [slice(i * hidden_units, (i + 1) * hidden_units) for i in range(3)]
    parts = [sums_ref[:, c] + received_ref[:, c].astype(jnp.float32) for c in cols]
    hidden, gate_delta, up_delta = local_deltas(*parts)
    if len(out_refs) == 1:
        values = [hidden, gate_delta, up_delta]
    else:
        out_refs[0][...] = hidden
        values = [gate_delta, up_delta]
    for c, value in zip(cols, values):
        out_refs[-1][:, c] = value


def in_order(core, mine, other):
    return jnp.concatenate(
        [jnp.where(core == 0, mine, other), jnp.where(core == 0, other, mine)], axis=0
    )


def slot_grad_rows(mine_ref, other_ref, gate_ref, up_ref):
    hidden_units = gate_ref.shape[0]
    rows = in_order(lax.axis_index("dp") % 2, mine_ref[...], other_ref[...])
    by_gate, by_up = rows[:, -2 * hidden_units:-hidden_units], rows[:, -hidden_units:]
    return (
        jnp.dot(by_gate, gate_ref[...], preferred_element_type=jnp.float32)
        + jnp.dot(by_up, up_ref[...], preferred_element_type=jnp.float32)
    ).astype(jnp.bfloat16)


def slot_grad_kernel(mine_ref, other_ref, gate_ref, up_ref, *block_refs):
    out = slot_grad_rows(mine_ref, other_ref, gate_ref, up_ref)
    block = block_refs[0].shape[0]
    for place, ref in enumerate(block_refs):
        ref[...] = out[place * block:(place + 1) * block]


def far_grad_kernel(mine_ref, other_ref, gate_ref, up_ref, pair_ref, out_ref):
    block = pair_ref.shape[0]
    out_ref[:block] = pair_ref[...]
    out_ref[block:] = slot_grad_rows(mine_ref, other_ref, gate_ref, up_ref)


def gather_deltas(target_ref, delta_refs, cols):
    core = lax.axis_index("dp") % 2
    at = 0
    for mine, other, of in zip(delta_refs[::2], delta_refs[1::2], cols):
        both = in_order(core, mine[:, of], other[:, of])
        target_ref[at:at + both.shape[0]] = both
        at += both.shape[0]


def send_tiles(left, right, tile, tile_ref, out_ref, sems, copies, start=0, stop=None):
    stop = stop or out_ref.shape[0]
    for at in range(start, stop, tile):
        rows = min(tile, stop - at)
        tile_ref[at:at + rows] = contract_rows(left[:, at:at + rows], right)
        span = pl.ds(at, rows)
        copies.append(
            pltpu.make_async_copy(tile_ref.at[span], out_ref.at[span], sems.at[len(copies)])
        )
        copies[-1].start()


def gate_grad_kernel(*refs):
    *in_refs, gate_ref, up_grad_ref, rows_ref, up_ref, tile_ref, up_tile_ref, deltas_ref, sems = refs
    row_refs, delta_refs = in_refs[:-6], in_refs[-6:]
    *near_refs, own_ref, far_ref = row_refs
    width = rows_ref.shape[1] // 2
    hidden_units = up_ref.shape[1]

    def gather_rows(cols):
        near = near_rows(*near_refs, cols=cols)
        rows_ref[:, cols] = jnp.concatenate([near, own_ref[:, cols], far_ref[:, cols]], axis=0)

    def columns(place):
        whole = slice(place * hidden_units, (place + 1) * hidden_units)
        return whole, whole, slice(whole.start - hidden_units, whole.stop - hidden_units)

    gather_deltas(deltas_ref, delta_refs, columns(1))
    gather_rows(slice(0, width))
    copies = []
    send_tiles(rows_ref[:, :width], deltas_ref[...], 128, tile_ref, gate_ref, sems, copies)
    gather_deltas(up_ref, delta_refs, columns(2))
    send_tiles(
        rows_ref[:, :width], up_ref[...], 128, up_tile_ref, up_grad_ref, sems, copies, stop=128
    )
    gather_rows(slice(width, 2 * width))
    for copy in copies:
        copy.wait()


def up_down_grad_kernel(started_ref, rows_ref, deltas_ref, *refs):
    *hidden_refs, up_ref, down_ref, up_tile_ref, down_tile_ref, hidden_ref, sems = refs
    width = rows_ref.shape[1] // 2
    hidden_units = hidden_ref.shape[1]
    copies = []
    send_tiles(
        rows_ref[:, :width], deltas_ref[...], 128, up_tile_ref, up_ref, sems, copies, start=128
    )
    gather_deltas(hidden_ref, hidden_refs, (slice(0, hidden_units),) * 3)
    send_tiles(hidden_ref[...], rows_ref[:, width:], 384, down_tile_ref, down_ref, sems, copies)
    for copy in copies:
        copy.wait()


def grads_call(kernel, grads, extra, delta_shape, *args, started=False):
    spaces = [pltpu.HBM] * len(grads) + [pltpu.VMEM] * len(extra)
    copies = sum(-(-grad.shape[0] // 128) for grad in grads)
    in_spaces = [pltpu.HBM if started and place == 0 else pltpu.VMEM for place in range(len(args))]
    return pl.pallas_call(
        kernel,
        out_shape=(*grads, *extra),
        input_output_aliases={0: 0} if started else {},
        in_specs=[pl.BlockSpec(memory_space=space) for space in in_spaces],
        out_specs=tuple(pl.BlockSpec(memory_space=space) for space in spaces),
        scratch_shapes=[pltpu.VMEM(grad.shape, grad.dtype) for grad in grads]
        + [pltpu.VMEM(delta_shape.shape, delta_shape.dtype), pltpu.SemaphoreType.DMA((copies,))],
        compiler_params=pltpu.CompilerParams(vmem_limit_bytes=24 * 1024 * 1024),
        cost_estimate=pl.CostEstimate(flops=10**7, bytes_accessed=10**7, transcendentals=0),
    )(*args)


def token_grad_kernel(chosen_ref, own_ref, from_pair_ref, *refs):
    *group_refs, out_ref = refs
    block = own_ref.shape[0]
    rows = [own_ref[...], from_pair_ref[:block]] + [ref[...] for ref in reversed(group_refs)]
    returned = jnp.concatenate(rows, axis=0)
    out = jnp.dot(chosen_ref[...], returned, preferred_element_type=jnp.float32)
    out_ref[...] = out.astype(jnp.bfloat16)


def body_by_all_to_all(tokens, cotangent, expert_ids, route_weights, gate_weight, up_weight, down_weight):
    owners = lax.axis_size("expert")
    width_parts = lax.axis_size("dp")
    tok_rows, top_count = expert_ids.shape
    width = tokens.shape[1]
    capacity = min(tok_rows, max(2, (tok_rows * top_count + owners - 1) // owners))
    slot_count = owners * capacity
    flat_ids = expert_ids.reshape(-1)
    position = jnp.arange(flat_ids.shape[0], dtype=jnp.int32)
    earlier = (flat_ids[:, None] == flat_ids[None, :]) & (position[None, :] < position[:, None])
    rank_pos = jnp.sum(earlier.astype(jnp.int32), axis=1)
    slot_pos = flat_ids * capacity + rank_pos
    pair_select = (slot_pos[:, None] == jnp.arange(slot_count, dtype=jnp.int32)[None, :]).astype(
        jnp.bfloat16
    )
    chosen = jnp.sum(
        pair_select.reshape(tok_rows, top_count, slot_count).astype(jnp.float32), axis=1
    ).astype(jnp.bfloat16)
    pair_tokens = jnp.repeat(tokens, top_count, axis=0)
    pair_scaled = (
        jnp.repeat(cotangent.astype(jnp.float32), top_count, axis=0) * route_weights
    ).astype(jnp.bfloat16)
    payload = jnp.concatenate([pair_tokens, pair_scaled], axis=1)
    send = contract_rows(pair_select, payload).astype(jnp.bfloat16)
    slots = lax.all_to_all(send, "expert", split_axis=0, concat_axis=0, tiled=True)

    core = lax.axis_index("dp") % 2
    half = slot_count // 2
    mine_slots = lax.dynamic_slice_in_dim(slots, core * half, half, 0)
    other_slots = lax.dynamic_slice_in_dim(slots, (1 - core) * half, half, 0)
    w_gate = gate_weight[0]
    w_up = up_weight[0]
    w_down = down_weight[0]

    def partial_sums(rows):
        feats, cots = rows[:, :width], rows[:, width:]
        return (
            jnp.dot(feats, w_gate, preferred_element_type=jnp.float32),
            jnp.dot(feats, w_up, preferred_element_type=jnp.float32),
            contract_cols(cots, w_down),
        )

    def pack(parts):
        return jnp.stack([part.astype(jnp.bfloat16) for part in parts])

    received = swap(pack(partial_sums(other_slots)), 1)
    sums = jnp.stack(partial_sums(mine_slots)) + received.astype(jnp.float32)
    bit = 2
    while bit < width_parts:
        sums = sums + swap(sums.astype(jnp.bfloat16), bit).astype(jnp.float32)
        bit *= 2
    mine = jnp.stack(local_deltas(sums[0], sums[1], sums[2]))
    other = swap(mine, 1)
    hidden, gate_delta, up_delta = jnp.concatenate([mine, other], axis=1)
    both = jnp.concatenate([mine_slots, other_slots], axis=0)
    slot_grad = (contract_cols(gate_delta, w_gate) + contract_cols(up_delta, w_up)).astype(
        jnp.bfloat16
    )
    slot_grad = jnp.where(
        core == 0, slot_grad, jnp.concatenate([slot_grad[half:], slot_grad[:half]], axis=0)
    )
    returned = lax.all_to_all(slot_grad, "expert", split_axis=0, concat_axis=0, tiled=True)
    feats, cots = both[:, :width], both[:, width:]
    gate_grad = contract_rows(feats, gate_delta)
    up_grad = contract_rows(feats, up_delta)
    down_grad = contract_rows(hidden, cots)
    token_grad = jnp.dot(chosen, returned, preferred_element_type=jnp.float32).astype(jnp.bfloat16)
    return (token_grad, gate_grad[None], up_grad[None], down_grad[None])


def body_by_pairs(tokens, cotangent, expert_ids, route_weights, gate_weight, up_weight, down_weight):
    owners = lax.axis_size("expert")
    width_parts = lax.axis_size("dp")
    tok_rows, _ = expert_ids.shape
    width = tokens.shape[1]
    hidden_units = gate_weight.shape[2]
    capacity = min(tok_rows, max(2, (tok_rows + owners - 1) // owners))
    slot_count = owners * capacity
    half = owners // 2

    far_first = [0] + list(reversed(range(1, half)))
    chosen, own, pair_block, *groups = call(
        functools.partial(dispatch_kernel, owners, capacity),
        (shape(slot_count, tok_rows),)
        + (shape(capacity, 2 * width),) * 2
        + (shape(2 * capacity, 2 * width),) * (half - 1),
        expert_ids.reshape(1, tok_rows),
        route_weights.reshape(1, tok_rows),
        tokens,
        cotangent,
        far=range(4),
        scratch=[
            pltpu.VMEM((1, tok_rows), jnp.int32),
            pltpu.VMEM((1, tok_rows), jnp.float32),
            pltpu.VMEM((tok_rows, width), jnp.bfloat16),
            pltpu.VMEM((tok_rows, width), jnp.bfloat16),
            pltpu.SemaphoreType.DMA((4,)),
        ],
    )
    down, gate, up = call(
        load_kernel,
        (shape(width, hidden_units),) * 3,
        down_weight[0],
        gate_weight[0],
        up_weight[0],
        chosen,
        far=range(3),
        scratch=[
            pltpu.VMEM((hidden_units, width), jnp.bfloat16),
            pltpu.SemaphoreType.DMA((3,)),
        ],
        cost=10**7,
    )
    groups = [swap(groups[j - 1], 2 * j, "expert") for j in far_first[1:]]
    from_pair = swap(pair_block, 1, "expert")
    groups = after(groups, from_pair)
    seconds = jnp.concatenate([group[capacity:] for group in groups], axis=0)
    by_pair = swap(after(seconds, up), 1, "expert")

    near = [from_pair] + groups

    def pieces(*parts):
        shapes = []
        for part in parts:
            shapes += [shape(part, 3 * hidden_units, jnp.float32), shape(part, 3 * hidden_units)]
        return shapes

    def sums_over_cores(rows, cost, *parts):
        mine, other = call(
            products_kernel, pieces(sum(parts)), *rows, gate, up, down, cost=cost
        )
        out = call(sums_kernel, pieces(*parts), mine, swap(other, 1))
        return list(zip(out[::2], out[1::2]))

    def exchanged(sums, marker):
        bit = 2
        while 2 * bit < width_parts:
            sums, marker = call(sums_kernel, pieces(sums.shape[0]), sums, swap(marker, bit))
            bit *= 2
        return sums, swap(marker, bit)

    def deltas_of(sums, received, cost):
        return call(deltas_kernel, shape(*sums.shape), sums, received, cost=cost)

    own_half = capacity // 2
    own_sums, near_sums = sums_over_cores(
        near + [own], 1, own_half, half * capacity // 2
    )
    (far_sums,) = sums_over_cores([by_pair], FAR_PRODUCTS_COST, (half - 1) * capacity // 2)
    near_sums, far_sums = exchanged(*near_sums), exchanged(*far_sums)

    near_mine = deltas_of(*near_sums, 1)
    *turned, chosen = call(
        turn_kernel,
        (shape(hidden_units, width),) * 2 + (shape(tok_rows, slot_count),),
        *after((gate, up, chosen), near_mine),
    )
    own_sums = exchanged(own_sums[0], after(own_sums[1], turned[0]))
    near_deltas = near_mine, swap(near_mine, 1)
    part = far_sums[0].shape[0]
    far_hidden, far_mine = after(
        call(
            deltas_kernel,
            (shape(part, hidden_units), shape(part, 2 * hidden_units)),
            *far_sums,
            cost=FAR_DELTAS_COST,
        ),
        near_deltas[1],
    )
    far_deltas = far_mine, swap(far_mine, 1)
    hidden_pair = far_hidden, swap(far_hidden, 1)
    block = shape(capacity, width)
    grads = call(slot_grad_kernel, (block,) * half, *near_deltas, *turned)
    own_mine = deltas_of(after(own_sums[0], grads[0]), own_sums[1], OWN_DELTAS_COST)
    own_deltas = own_mine, swap(own_mine, 1)
    (own_grad,) = call(slot_grad_kernel, (block,), *own_deltas, *turned)
    to_pair = call(
        far_grad_kernel,
        shape(half * capacity, width),
        *after(far_deltas, own_mine),
        *turned,
        grads[-1],
    )
    returned_pair = swap(to_pair, 1, "expert")
    wide = shape(width, hidden_units, jnp.float32)
    one_delta = shape(slot_count, hidden_units)
    gate_grad, up_started, all_rows, up_deltas = grads_call(
        gate_grad_kernel,
        (wide, wide),
        (shape(slot_count, 2 * width), one_delta),
        one_delta,
        *near,
        own,
        by_pair,
        *near_deltas,
        *own_deltas,
        *far_deltas,
    )
    returned_pair = after(returned_pair, (gate_grad, own_grad))
    returned = {}
    for place, j in enumerate(far_first[1:], 1):
        more = returned_pair[place * capacity:(place + 1) * capacity]
        returned[j] = swap(jnp.concatenate([grads[place - 1], more], axis=0), 2 * j, "expert")
    up_grad, down_grad = grads_call(
        up_down_grad_kernel,
        (wide, shape(hidden_units, width, jnp.float32)),
        (),
        one_delta,
        up_started,
        all_rows,
        up_deltas,
        *near_deltas,
        *own_deltas,
        *hidden_pair,
        started=True,
    )
    token_grad = call(
        token_grad_kernel,
        shape(tok_rows, width),
        chosen,
        own_grad,
        returned_pair,
        *[returned[j] for j in far_first[1:]],
    )
    return (token_grad, gate_grad[None], up_grad[None], down_grad[None])


def body(tokens, cotangent, expert_ids, *rest):
    owners = lax.axis_size("expert")
    width_parts = lax.axis_size("dp")
    tok_rows, top_count = expert_ids.shape
    by_pairs = (
        top_count == 1
        and owners >= 8
        and owners & (owners - 1) == 0
        and width_parts >= 4
        and tok_rows % (16 * owners) == 0
    )
    chosen = body_by_pairs if by_pairs else body_by_all_to_all
    return chosen(tokens, cotangent, expert_ids, *rest)


def solution(mesh):
    return jax.shard_map(
        body,
        mesh=mesh,
        in_specs=(
            P("expert", "dp"),
            P("expert", "dp"),
            P("expert", None),
            P("expert", None),
            P("expert", "dp", None),
            P("expert", "dp", None),
            P("expert", None, "dp"),
        ),
        out_specs=(
            P("expert", "dp"),
            P("expert", "dp", None),
            P("expert", "dp", None),
            P("expert", None, "dp"),
        ),
        check_vma=False,
    )
```

```python
import functools

import jax
import jax.numpy as jnp
from jax import lax
from jax.experimental import pallas as pl
from jax.experimental.pallas import tpu as pltpu
from jax.sharding import PartitionSpec as P


def contract_rows(left, right):
    return lax.dot_general(
        left, right, (((0,), (0,)), ((), ())), preferred_element_type=jnp.float32
    )


def contract_cols(left, right):
    return lax.dot_general(
        left, right, (((1,), (1,)), ((), ())), preferred_element_type=jnp.float32
    )


def local_deltas(gate_pre, up_pre, hidden_grad):
    sigma = jax.nn.sigmoid(gate_pre)
    activated = gate_pre * sigma
    hidden = (activated * up_pre).astype(jnp.bfloat16)
    gate_delta = (hidden_grad * up_pre * sigma * (1.0 + gate_pre * (1.0 - sigma))).astype(
        jnp.bfloat16
    )
    up_delta = (hidden_grad * activated).astype(jnp.bfloat16)
    return (hidden, gate_delta, up_delta)


def swap(value, bit, axis="dp"):
    size = lax.axis_size(axis)
    return lax.ppermute(value, axis, [(i, i ^ bit) for i in range(size)])


FAR_PRODUCTS_COST = 3 * 10**8
FAR_DELTAS_COST = 8 * 10**8
OWN_DELTAS_COST = 11 * 10**8


def after(values, marker):
    return lax.optimization_barrier((values, marker))[0]


def call(kernel, outs, *args, cost=1, far=(), scratch=()):
    spaces = [pltpu.HBM if place in far else pltpu.VMEM for place in range(len(args))]
    args = [
        pltpu.with_memory_space_constraint(arg, pltpu.HBM) if place in far else arg
        for place, arg in enumerate(args)
    ]
    return pl.pallas_call(
        kernel,
        out_shape=outs,
        in_specs=[pl.BlockSpec(memory_space=space) for space in spaces],
        scratch_shapes=scratch,
        compiler_params=pltpu.CompilerParams(vmem_limit_bytes=24 * 1024 * 1024),
        cost_estimate=pl.CostEstimate(flops=cost, bytes_accessed=cost, transcendentals=0),
    )(*args)


def shape(rows, cols, dtype=jnp.bfloat16):
    return jax.ShapeDtypeStruct((rows, cols), dtype)


def dispatch_kernel(owners, capacity, ids_hbm, weights_hbm, tokens_hbm, cotangent_hbm, *refs):
    chosen_ref, *out_refs, ids_ref, weights_ref, tokens_ref, cotangent_ref, sems = refs
    copies = [
        pltpu.make_async_copy(source, target, sems.at[place])
        for place, (source, target) in enumerate(
            (
                (ids_hbm, ids_ref),
                (weights_hbm, weights_ref),
                (tokens_hbm, tokens_ref),
                (cotangent_hbm, cotangent_ref),
            )
        )
    ]
    for copy in copies:
        copy.start()
    pairs = ids_ref.shape[1]
    width = tokens_ref.shape[1]
    slot_count = owners * capacity
    me = lax.axis_index("expert")
    before = lax.broadcasted_iota(jnp.int32, (pairs, pairs), 0) < lax.broadcasted_iota(
        jnp.int32, (pairs, pairs), 1
    )
    before = before.astype(jnp.float32).astype(jnp.bfloat16)
    experts = lax.broadcasted_iota(jnp.int32, (owners, pairs), 0)
    slots = lax.broadcasted_iota(jnp.int32, (slot_count, pairs), 0)
    copies[0].wait()
    ids = ids_ref[...]
    named = (ids == experts).astype(jnp.float32)
    counts = jnp.dot(named.astype(jnp.bfloat16), before, preferred_element_type=jnp.float32)
    rank = jnp.sum(named * counts, axis=0, keepdims=True).astype(jnp.int32)
    chosen = (slots == (ids ^ me) * capacity + rank).astype(jnp.float32)
    select = chosen.astype(jnp.bfloat16)
    chosen_ref[...] = select
    for copy in copies[1:]:
        copy.wait()
    scale = jnp.sum(chosen * weights_ref[...], axis=1, keepdims=True)
    feats = jnp.dot(select, tokens_ref[...], preferred_element_type=jnp.float32)
    cots = jnp.dot(select, cotangent_ref[...], preferred_element_type=jnp.float32) * scale
    at = 0
    for out_ref in out_refs:
        rows = slice(at, at + out_ref.shape[0])
        out_ref[:, :width] = feats[rows].astype(jnp.bfloat16)
        out_ref[:, width:] = cots[rows].astype(jnp.bfloat16)
        at += out_ref.shape[0]


def load_kernel(down_hbm, gate_hbm, up_hbm, marker_hbm, turned_ref, gate_ref, up_ref, down_ref, sems):
    copies = [
        pltpu.make_async_copy(source, target, sems.at[place])
        for place, (source, target) in enumerate(
            ((down_hbm, down_ref), (gate_hbm, gate_ref), (up_hbm, up_ref))
        )
    ]
    for copy in copies:
        copy.start()
    copies[0].wait()
    turned_ref[...] = down_ref[...].T
    for copy in copies[1:]:
        copy.wait()


def turn_kernel(*refs):
    half = len(refs) // 2
    for source, target in zip(refs[:half], refs[half:]):
        target[...] = source[...].T


def near_rows(from_pair_ref, *group_refs, cols=slice(None)):
    halves = [ref[:ref.shape[0] // 2, cols] for ref in group_refs]
    return jnp.concatenate(halves + [from_pair_ref[:, cols]], axis=0)


def with_own_rows(own, rows):
    part, half = own.shape[0] // 2, rows.shape[0] // 2
    return jnp.concatenate([own[:part], rows[:half], own[part:], rows[half:]], axis=0)


def products_kernel(*refs):
    *row_refs, gate_ref, up_ref, down_ref, mine_ref, other_ref = refs
    rows = row_refs[-1][...]
    if len(row_refs) > 1:
        rows = with_own_rows(rows, near_rows(*row_refs[:-1]))
    half = rows.shape[0] // 2
    width = rows.shape[1] // 2
    hidden_units = gate_ref.shape[1]
    core = lax.axis_index("dp") % 2
    feats, cots = rows[:, :width], rows[:, width:]
    for place, weight_ref in enumerate((gate_ref, up_ref, down_ref)):
        cols = slice(place * hidden_units, (place + 1) * hidden_units)
        rows = feats if place < 2 else cots
        out = jnp.dot(rows, weight_ref[...], preferred_element_type=jnp.float32)
        low, high = out[:half], out[half:]
        mine_ref[:, cols] = jnp.where(core == 0, low, high)
        other_ref[:, cols] = jnp.where(core == 0, high, low).astype(jnp.bfloat16)


def sums_kernel(mine_ref, received_ref, *refs):
    sums = mine_ref[...] + received_ref[...].astype(jnp.float32)
    at = 0
    for sums_ref, packed_ref in zip(refs[::2], refs[1::2]):
        part = sums[at:at + sums_ref.shape[0]]
        sums_ref[...] = part
        packed_ref[...] = part.astype(jnp.bfloat16)
        at += part.shape[0]


def deltas_kernel(sums_ref, received_ref, *out_refs):
    hidden_units = sums_ref.shape[1] // 3
    cols = [slice(i * hidden_units, (i + 1) * hidden_units) for i in range(3)]
    parts = [sums_ref[:, c] + received_ref[:, c].astype(jnp.float32) for c in cols]
    hidden, gate_delta, up_delta = local_deltas(*parts)
    if len(out_refs) == 1:
        values = [hidden, gate_delta, up_delta]
    else:
        out_refs[0][...] = hidden
        values = [gate_delta, up_delta]
    for c, value in zip(cols, values):
        out_refs[-1][:, c] = value


def in_order(core, mine, other):
    return jnp.concatenate(
        [jnp.where(core == 0, mine, other), jnp.where(core == 0, other, mine)], axis=0
    )


def slot_grad_rows(mine_ref, other_ref, gate_ref, up_ref):
    hidden_units = gate_ref.shape[0]
    rows = in_order(lax.axis_index("dp") % 2, mine_ref[...], other_ref[...])
    by_gate, by_up = rows[:, -2 * hidden_units:-hidden_units], rows[:, -hidden_units:]
    return (
        jnp.dot(by_gate, gate_ref[...], preferred_element_type=jnp.float32)
        + jnp.dot(by_up, up_ref[...], preferred_element_type=jnp.float32)
    ).astype(jnp.bfloat16)


def slot_grad_kernel(mine_ref, other_ref, gate_ref, up_ref, *block_refs):
    out = slot_grad_rows(mine_ref, other_ref, gate_ref, up_ref)
    block = block_refs[0].shape[0]
    for place, ref in enumerate(block_refs):
        ref[...] = out[place * block:(place + 1) * block]


def far_grad_kernel(mine_ref, other_ref, gate_ref, up_ref, pair_ref, out_ref):
    block = pair_ref.shape[0]
    out_ref[:block] = pair_ref[...]
    out_ref[block:] = slot_grad_rows(mine_ref, other_ref, gate_ref, up_ref)


def gather_deltas(target_ref, delta_refs, cols):
    core = lax.axis_index("dp") % 2
    at = 0
    for mine, other, of in zip(delta_refs[::2], delta_refs[1::2], cols):
        both = in_order(core, mine[:, of], other[:, of])
        target_ref[at:at + both.shape[0]] = both
        at += both.shape[0]


def send_tiles(left, right, tile, tile_ref, out_ref, sems, copies, start=0, stop=None):
    stop = stop or out_ref.shape[0]
    for at in range(start, stop, tile):
        rows = min(tile, stop - at)
        tile_ref[at:at + rows] = contract_rows(left[:, at:at + rows], right)
        span = pl.ds(at, rows)
        copies.append(
            pltpu.make_async_copy(tile_ref.at[span], out_ref.at[span], sems.at[len(copies)])
        )
        copies[-1].start()


def gate_grad_kernel(*refs):
    *in_refs, gate_ref, up_grad_ref, rows_ref, up_ref, tile_ref, up_tile_ref, deltas_ref, sems = refs
    row_refs, delta_refs = in_refs[:-6], in_refs[-6:]
    *near_refs, own_ref, far_ref = row_refs
    width = rows_ref.shape[1] // 2
    hidden_units = up_ref.shape[1]

    def gather_rows(cols):
        near = near_rows(*near_refs, cols=cols)
        rows_ref[:, cols] = jnp.concatenate([near, own_ref[:, cols], far_ref[:, cols]], axis=0)

    def columns(place):
        whole = slice(place * hidden_units, (place + 1) * hidden_units)
        return whole, whole, slice(whole.start - hidden_units, whole.stop - hidden_units)

    gather_deltas(deltas_ref, delta_refs, columns(1))
    gather_rows(slice(0, width))
    copies = []
    send_tiles(rows_ref[:, :width], deltas_ref[...], 128, tile_ref, gate_ref, sems, copies)
    gather_deltas(up_ref, delta_refs, columns(2))
    send_tiles(
        rows_ref[:, :width], up_ref[...], 128, up_tile_ref, up_grad_ref, sems, copies, stop=256
    )
    gather_rows(slice(width, 2 * width))
    for copy in copies:
        copy.wait()


def up_down_grad_kernel(started_ref, rows_ref, deltas_ref, *refs):
    *hidden_refs, up_ref, down_ref, up_tile_ref, down_tile_ref, hidden_ref, sems = refs
    width = rows_ref.shape[1] // 2
    hidden_units = hidden_ref.shape[1]
    copies = []
    send_tiles(
        rows_ref[:, :width], deltas_ref[...], 128, up_tile_ref, up_ref, sems, copies, start=256
    )
    gather_deltas(hidden_ref, hidden_refs, (slice(0, hidden_units),) * 3)
    send_tiles(hidden_ref[...], rows_ref[:, width:], 384, down_tile_ref, down_ref, sems, copies)
    for copy in copies:
        copy.wait()


def grads_call(kernel, grads, extra, delta_shape, *args, started=False):
    spaces = [pltpu.HBM] * len(grads) + [pltpu.VMEM] * len(extra)
    copies = sum(-(-grad.shape[0] // 128) for grad in grads)
    in_spaces = [pltpu.HBM if started and place == 0 else pltpu.VMEM for place in range(len(args))]
    return pl.pallas_call(
        kernel,
        out_shape=(*grads, *extra),
        input_output_aliases={0: 0} if started else {},
        in_specs=[pl.BlockSpec(memory_space=space) for space in in_spaces],
        out_specs=tuple(pl.BlockSpec(memory_space=space) for space in spaces),
        scratch_shapes=[pltpu.VMEM(grad.shape, grad.dtype) for grad in grads]
        + [pltpu.VMEM(delta_shape.shape, delta_shape.dtype), pltpu.SemaphoreType.DMA((copies,))],
        compiler_params=pltpu.CompilerParams(vmem_limit_bytes=24 * 1024 * 1024),
        cost_estimate=pl.CostEstimate(flops=10**7, bytes_accessed=10**7, transcendentals=0),
    )(*args)


def token_grad_kernel(chosen_ref, own_ref, from_pair_ref, *refs):
    *group_refs, out_ref = refs
    block = own_ref.shape[0]
    rows = [own_ref[...], from_pair_ref[:block]] + [ref[...] for ref in reversed(group_refs)]
    returned = jnp.concatenate(rows, axis=0)
    out = jnp.dot(chosen_ref[...], returned, preferred_element_type=jnp.float32)
    out_ref[...] = out.astype(jnp.bfloat16)


def body_by_all_to_all(tokens, cotangent, expert_ids, route_weights, gate_weight, up_weight, down_weight):
    owners = lax.axis_size("expert")
    width_parts = lax.axis_size("dp")
    tok_rows, top_count = expert_ids.shape
    width = tokens.shape[1]
    capacity = min(tok_rows, max(2, (tok_rows * top_count + owners - 1) // owners))
    slot_count = owners * capacity
    flat_ids = expert_ids.reshape(-1)
    position = jnp.arange(flat_ids.shape[0], dtype=jnp.int32)
    earlier = (flat_ids[:, None] == flat_ids[None, :]) & (position[None, :] < position[:, None])
    rank_pos = jnp.sum(earlier.astype(jnp.int32), axis=1)
    slot_pos = flat_ids * capacity + rank_pos
    pair_select = (slot_pos[:, None] == jnp.arange(slot_count, dtype=jnp.int32)[None, :]).astype(
        jnp.bfloat16
    )
    chosen = jnp.sum(
        pair_select.reshape(tok_rows, top_count, slot_count).astype(jnp.float32), axis=1
    ).astype(jnp.bfloat16)
    pair_tokens = jnp.repeat(tokens, top_count, axis=0)
    pair_scaled = (
        jnp.repeat(cotangent.astype(jnp.float32), top_count, axis=0) * route_weights
    ).astype(jnp.bfloat16)
    payload = jnp.concatenate([pair_tokens, pair_scaled], axis=1)
    send = contract_rows(pair_select, payload).astype(jnp.bfloat16)
    slots = lax.all_to_all(send, "expert", split_axis=0, concat_axis=0, tiled=True)

    core = lax.axis_index("dp") % 2
    half = slot_count // 2
    mine_slots = lax.dynamic_slice_in_dim(slots, core * half, half, 0)
    other_slots = lax.dynamic_slice_in_dim(slots, (1 - core) * half, half, 0)
    w_gate = gate_weight[0]
    w_up = up_weight[0]
    w_down = down_weight[0]

    def partial_sums(rows):
        feats, cots = rows[:, :width], rows[:, width:]
        return (
            jnp.dot(feats, w_gate, preferred_element_type=jnp.float32),
            jnp.dot(feats, w_up, preferred_element_type=jnp.float32),
            contract_cols(cots, w_down),
        )

    def pack(parts):
        return jnp.stack([part.astype(jnp.bfloat16) for part in parts])

    received = swap(pack(partial_sums(other_slots)), 1)
    sums = jnp.stack(partial_sums(mine_slots)) + received.astype(jnp.float32)
    bit = 2
    while bit < width_parts:
        sums = sums + swap(sums.astype(jnp.bfloat16), bit).astype(jnp.float32)
        bit *= 2
    mine = jnp.stack(local_deltas(sums[0], sums[1], sums[2]))
    other = swap(mine, 1)
    hidden, gate_delta, up_delta = jnp.concatenate([mine, other], axis=1)
    both = jnp.concatenate([mine_slots, other_slots], axis=0)
    slot_grad = (contract_cols(gate_delta, w_gate) + contract_cols(up_delta, w_up)).astype(
        jnp.bfloat16
    )
    slot_grad = jnp.where(
        core == 0, slot_grad, jnp.concatenate([slot_grad[half:], slot_grad[:half]], axis=0)
    )
    returned = lax.all_to_all(slot_grad, "expert", split_axis=0, concat_axis=0, tiled=True)
    feats, cots = both[:, :width], both[:, width:]
    gate_grad = contract_rows(feats, gate_delta)
    up_grad = contract_rows(feats, up_delta)
    down_grad = contract_rows(hidden, cots)
    token_grad = jnp.dot(chosen, returned, preferred_element_type=jnp.float32).astype(jnp.bfloat16)
    return (token_grad, gate_grad[None], up_grad[None], down_grad[None])


def body_by_pairs(tokens, cotangent, expert_ids, route_weights, gate_weight, up_weight, down_weight):
    owners = lax.axis_size("expert")
    width_parts = lax.axis_size("dp")
    tok_rows, _ = expert_ids.shape
    width = tokens.shape[1]
    hidden_units = gate_weight.shape[2]
    capacity = min(tok_rows, max(2, (tok_rows + owners - 1) // owners))
    slot_count = owners * capacity
    half = owners // 2

    far_first = [0] + list(reversed(range(1, half)))
    chosen, own, pair_block, *groups = call(
        functools.partial(dispatch_kernel, owners, capacity),
        (shape(slot_count, tok_rows),)
        + (shape(capacity, 2 * width),) * 2
        + (shape(2 * capacity, 2 * width),) * (half - 1),
        expert_ids.reshape(1, tok_rows),
        route_weights.reshape(1, tok_rows),
        tokens,
        cotangent,
        far=range(4),
        scratch=[
            pltpu.VMEM((1, tok_rows), jnp.int32),
            pltpu.VMEM((1, tok_rows), jnp.float32),
            pltpu.VMEM((tok_rows, width), jnp.bfloat16),
            pltpu.VMEM((tok_rows, width), jnp.bfloat16),
            pltpu.SemaphoreType.DMA((4,)),
        ],
    )
    down, gate, up = call(
        load_kernel,
        (shape(width, hidden_units),) * 3,
        down_weight[0],
        gate_weight[0],
        up_weight[0],
        chosen,
        far=range(3),
        scratch=[
            pltpu.VMEM((hidden_units, width), jnp.bfloat16),
            pltpu.SemaphoreType.DMA((3,)),
        ],
        cost=10**7,
    )
    groups = [swap(groups[j - 1], 2 * j, "expert") for j in far_first[1:]]
    from_pair = swap(pair_block, 1, "expert")
    groups = after(groups, from_pair)
    seconds = jnp.concatenate([group[capacity:] for group in groups], axis=0)
    by_pair = swap(after(seconds, up), 1, "expert")

    near = [from_pair] + groups

    def pieces(*parts):
        shapes = []
        for part in parts:
            shapes += [shape(part, 3 * hidden_units, jnp.float32), shape(part, 3 * hidden_units)]
        return shapes

    def sums_over_cores(rows, cost, *parts):
        mine, other = call(
            products_kernel, pieces(sum(parts)), *rows, gate, up, down, cost=cost
        )
        out = call(sums_kernel, pieces(*parts), mine, swap(other, 1))
        return list(zip(out[::2], out[1::2]))

    def exchanged(sums, marker):
        bit = 2
        while 2 * bit < width_parts:
            sums, marker = call(sums_kernel, pieces(sums.shape[0]), sums, swap(marker, bit))
            bit *= 2
        return sums, swap(marker, bit)

    def deltas_of(sums, received, cost):
        return call(deltas_kernel, shape(*sums.shape), sums, received, cost=cost)

    own_half = capacity // 2
    own_sums, near_sums = sums_over_cores(
        near + [own], 1, own_half, half * capacity // 2
    )
    (far_sums,) = sums_over_cores([by_pair], FAR_PRODUCTS_COST, (half - 1) * capacity // 2)
    near_sums, far_sums = exchanged(*near_sums), exchanged(*far_sums)

    near_mine = deltas_of(*near_sums, 1)
    *turned, chosen = call(
        turn_kernel,
        (shape(hidden_units, width),) * 2 + (shape(tok_rows, slot_count),),
        *after((gate, up, chosen), near_mine),
    )
    own_sums = exchanged(own_sums[0], after(own_sums[1], turned[0]))
    near_deltas = near_mine, swap(near_mine, 1)
    part = far_sums[0].shape[0]
    far_hidden, far_mine = after(
        call(
            deltas_kernel,
            (shape(part, hidden_units), shape(part, 2 * hidden_units)),
            *far_sums,
            cost=FAR_DELTAS_COST,
        ),
        near_deltas[1],
    )
    far_deltas = far_mine, swap(far_mine, 1)
    hidden_pair = far_hidden, swap(far_hidden, 1)
    block = shape(capacity, width)
    grads = call(slot_grad_kernel, (block,) * half, *near_deltas, *turned)
    own_mine = deltas_of(after(own_sums[0], grads[0]), own_sums[1], OWN_DELTAS_COST)
    own_deltas = own_mine, swap(own_mine, 1)
    (own_grad,) = call(slot_grad_kernel, (block,), *own_deltas, *turned)
    to_pair = call(
        far_grad_kernel,
        shape(half * capacity, width),
        *after(far_deltas, own_mine),
        *turned,
        grads[-1],
    )
    returned_pair = swap(to_pair, 1, "expert")
    wide = shape(width, hidden_units, jnp.float32)
    one_delta = shape(slot_count, hidden_units)
    gate_grad, up_started, all_rows, up_deltas = grads_call(
        gate_grad_kernel,
        (wide, wide),
        (shape(slot_count, 2 * width), one_delta),
        one_delta,
        *near,
        own,
        by_pair,
        *near_deltas,
        *own_deltas,
        *far_deltas,
    )
    returned_pair = after(returned_pair, gate_grad)
    returned = {}
    for place, j in enumerate(far_first[1:], 1):
        more = returned_pair[place * capacity:(place + 1) * capacity]
        returned[j] = swap(jnp.concatenate([grads[place - 1], more], axis=0), 2 * j, "expert")
    up_grad, down_grad = grads_call(
        up_down_grad_kernel,
        (wide, shape(hidden_units, width, jnp.float32)),
        (),
        one_delta,
        up_started,
        all_rows,
        up_deltas,
        *near_deltas,
        *own_deltas,
        *hidden_pair,
        started=True,
    )
    token_grad = call(
        token_grad_kernel,
        shape(tok_rows, width),
        chosen,
        own_grad,
        returned_pair,
        *[returned[j] for j in far_first[1:]],
    )
    return (token_grad, gate_grad[None], up_grad[None], down_grad[None])


def body(tokens, cotangent, expert_ids, *rest):
    owners = lax.axis_size("expert")
    width_parts = lax.axis_size("dp")
    tok_rows, top_count = expert_ids.shape
    by_pairs = (
        top_count == 1
        and owners >= 8
        and owners & (owners - 1) == 0
        and width_parts >= 4
        and tok_rows % (16 * owners) == 0
    )
    chosen = body_by_pairs if by_pairs else body_by_all_to_all
    return chosen(tokens, cotangent, expert_ids, *rest)


def solution(mesh):
    return jax.shard_map(
        body,
        mesh=mesh,
        in_specs=(
            P("expert", "dp"),
            P("expert", "dp"),
            P("expert", None),
            P("expert", None),
            P("expert", "dp", None),
            P("expert", "dp", None),
            P("expert", None, "dp"),
        ),
        out_specs=(
            P("expert", "dp"),
            P("expert", "dp", None),
            P("expert", "dp", None),
            P("expert", None, "dp"),
        ),
        check_vma=False,
    )
```

```python
import functools

import jax
import jax.numpy as jnp
from jax import lax
from jax.experimental import pallas as pl
from jax.experimental.pallas import tpu as pltpu
from jax.sharding import PartitionSpec as P


def contract_rows(left, right):
    return lax.dot_general(
        left, right, (((0,), (0,)), ((), ())), preferred_element_type=jnp.float32
    )


def contract_cols(left, right):
    return lax.dot_general(
        left, right, (((1,), (1,)), ((), ())), preferred_element_type=jnp.float32
    )


def local_deltas(gate_pre, up_pre, hidden_grad):
    sigma = jax.nn.sigmoid(gate_pre)
    activated = gate_pre * sigma
    hidden = (activated * up_pre).astype(jnp.bfloat16)
    gate_delta = (hidden_grad * up_pre * sigma * (1.0 + gate_pre * (1.0 - sigma))).astype(
        jnp.bfloat16
    )
    up_delta = (hidden_grad * activated).astype(jnp.bfloat16)
    return (hidden, gate_delta, up_delta)


def swap(value, bit, axis="dp"):
    size = lax.axis_size(axis)
    return lax.ppermute(value, axis, [(i, i ^ bit) for i in range(size)])


FAR_PRODUCTS_COST = 3 * 10**8
FAR_DELTAS_COST = 8 * 10**8
OWN_DELTAS_COST = 11 * 10**8


def after(values, marker):
    return lax.optimization_barrier((values, marker))[0]


def call(kernel, outs, *args, cost=1, far=(), scratch=()):
    spaces = [pltpu.HBM if place in far else pltpu.VMEM for place in range(len(args))]
    args = [
        pltpu.with_memory_space_constraint(arg, pltpu.HBM) if place in far else arg
        for place, arg in enumerate(args)
    ]
    return pl.pallas_call(
        kernel,
        out_shape=outs,
        in_specs=[pl.BlockSpec(memory_space=space) for space in spaces],
        scratch_shapes=scratch,
        compiler_params=pltpu.CompilerParams(vmem_limit_bytes=24 * 1024 * 1024),
        cost_estimate=pl.CostEstimate(flops=cost, bytes_accessed=cost, transcendentals=0),
    )(*args)


def shape(rows, cols, dtype=jnp.bfloat16):
    return jax.ShapeDtypeStruct((rows, cols), dtype)


def dispatch_kernel(owners, capacity, ids_hbm, weights_hbm, tokens_hbm, cotangent_hbm, *refs):
    chosen_ref, *out_refs, ids_ref, weights_ref, tokens_ref, cotangent_ref, sems = refs
    copies = [
        pltpu.make_async_copy(source, target, sems.at[place])
        for place, (source, target) in enumerate(
            (
                (ids_hbm, ids_ref),
                (weights_hbm, weights_ref),
                (tokens_hbm, tokens_ref),
                (cotangent_hbm, cotangent_ref),
            )
        )
    ]
    for copy in copies:
        copy.start()
    pairs = ids_ref.shape[1]
    width = tokens_ref.shape[1]
    slot_count = owners * capacity
    me = lax.axis_index("expert")
    before = lax.broadcasted_iota(jnp.int32, (pairs, pairs), 0) < lax.broadcasted_iota(
        jnp.int32, (pairs, pairs), 1
    )
    before = before.astype(jnp.float32).astype(jnp.bfloat16)
    experts = lax.broadcasted_iota(jnp.int32, (owners, pairs), 0)
    slots = lax.broadcasted_iota(jnp.int32, (slot_count, pairs), 0)
    copies[0].wait()
    ids = ids_ref[...]
    named = (ids == experts).astype(jnp.float32)
    counts = jnp.dot(named.astype(jnp.bfloat16), before, preferred_element_type=jnp.float32)
    rank = jnp.sum(named * counts, axis=0, keepdims=True).astype(jnp.int32)
    chosen = (slots == (ids ^ me) * capacity + rank).astype(jnp.float32)
    select = chosen.astype(jnp.bfloat16)
    chosen_ref[...] = select
    for copy in copies[1:]:
        copy.wait()
    scale = jnp.sum(chosen * weights_ref[...], axis=1, keepdims=True)
    feats = jnp.dot(select, tokens_ref[...], preferred_element_type=jnp.float32)
    cots = jnp.dot(select, cotangent_ref[...], preferred_element_type=jnp.float32) * scale
    at = 0
    for out_ref in out_refs:
        rows = slice(at, at + out_ref.shape[0])
        out_ref[:, :width] = feats[rows].astype(jnp.bfloat16)
        out_ref[:, width:] = cots[rows].astype(jnp.bfloat16)
        at += out_ref.shape[0]


def load_kernel(down_hbm, gate_hbm, up_hbm, marker_hbm, turned_ref, gate_ref, up_ref, down_ref, sems):
    copies = [
        pltpu.make_async_copy(source, target, sems.at[place])
        for place, (source, target) in enumerate(
            ((down_hbm, down_ref), (gate_hbm, gate_ref), (up_hbm, up_ref))
        )
    ]
    for copy in copies:
        copy.start()
    copies[0].wait()
    turned_ref[...] = down_ref[...].T
    for copy in copies[1:]:
        copy.wait()


def turn_kernel(*refs):
    half = len(refs) // 2
    for source, target in zip(refs[:half], refs[half:]):
        target[...] = source[...].T


def near_rows(from_pair_ref, *group_refs, cols=slice(None)):
    halves = [ref[:ref.shape[0] // 2, cols] for ref in group_refs]
    return jnp.concatenate(halves + [from_pair_ref[:, cols]], axis=0)


def with_own_rows(own, rows):
    part, half = own.shape[0] // 2, rows.shape[0] // 2
    return jnp.concatenate([own[:part], rows[:half], own[part:], rows[half:]], axis=0)


def products_kernel(*refs):
    *row_refs, gate_ref, up_ref, down_ref, mine_ref, other_ref = refs
    rows = row_refs[-1][...]
    if len(row_refs) > 1:
        rows = with_own_rows(rows, near_rows(*row_refs[:-1]))
    half = rows.shape[0] // 2
    width = rows.shape[1] // 2
    hidden_units = gate_ref.shape[1]
    core = lax.axis_index("dp") % 2
    feats, cots = rows[:, :width], rows[:, width:]
    for place, weight_ref in enumerate((gate_ref, up_ref, down_ref)):
        cols = slice(place * hidden_units, (place + 1) * hidden_units)
        rows = feats if place < 2 else cots
        out = jnp.dot(rows, weight_ref[...], preferred_element_type=jnp.float32)
        low, high = out[:half], out[half:]
        mine_ref[:, cols] = jnp.where(core == 0, low, high)
        other_ref[:, cols] = jnp.where(core == 0, high, low).astype(jnp.bfloat16)


def sums_kernel(mine_ref, received_ref, *refs):
    sums = mine_ref[...] + received_ref[...].astype(jnp.float32)
    at = 0
    for sums_ref, packed_ref in zip(refs[::2], refs[1::2]):
        part = sums[at:at + sums_ref.shape[0]]
        sums_ref[...] = part
        packed_ref[...] = part.astype(jnp.bfloat16)
        at += part.shape[0]


def deltas_kernel(sums_ref, received_ref, *out_refs):
    hidden_units = sums_ref.shape[1] // 3
    cols = [slice(i * hidden_units, (i + 1) * hidden_units) for i in range(3)]
    parts = [sums_ref[:, c] + received_ref[:, c].astype(jnp.float32) for c in cols]
    hidden, gate_delta, up_delta = local_deltas(*parts)
    if len(out_refs) == 1:
        values = [hidden, gate_delta, up_delta]
    else:
        out_refs[0][...] = hidden
        values = [gate_delta, up_delta]
    for c, value in zip(cols, values):
        out_refs[-1][:, c] = value


def in_order(core, mine, other):
    return jnp.concatenate(
        [jnp.where(core == 0, mine, other), jnp.where(core == 0, other, mine)], axis=0
    )


def slot_grad_rows(mine_ref, other_ref, gate_ref, up_ref):
    hidden_units = gate_ref.shape[0]
    rows = in_order(lax.axis_index("dp") % 2, mine_ref[...], other_ref[...])
    by_gate, by_up = rows[:, -2 * hidden_units:-hidden_units], rows[:, -hidden_units:]
    return (
        jnp.dot(by_gate, gate_ref[...], preferred_element_type=jnp.float32)
        + jnp.dot(by_up, up_ref[...], preferred_element_type=jnp.float32)
    ).astype(jnp.bfloat16)


def slot_grad_kernel(mine_ref, other_ref, gate_ref, up_ref, *block_refs):
    out = slot_grad_rows(mine_ref, other_ref, gate_ref, up_ref)
    block = block_refs[0].shape[0]
    for place, ref in enumerate(block_refs):
        ref[...] = out[place * block:(place + 1) * block]


def far_grad_kernel(mine_ref, other_ref, gate_ref, up_ref, pair_ref, out_ref):
    block = pair_ref.shape[0]
    out_ref[:block] = pair_ref[...]
    out_ref[block:] = slot_grad_rows(mine_ref, other_ref, gate_ref, up_ref)


def gather_deltas(target_ref, delta_refs, cols):
    core = lax.axis_index("dp") % 2
    at = 0
    for mine, other, of in zip(delta_refs[::2], delta_refs[1::2], cols):
        both = in_order(core, mine[:, of], other[:, of])
        target_ref[at:at + both.shape[0]] = both
        at += both.shape[0]


def send_tiles(left, right, tile, tile_ref, out_ref, sems, copies, start=0, stop=None):
    stop = stop or out_ref.shape[0]
    for at in range(start, stop, tile):
        rows = min(tile, stop - at)
        tile_ref[at:at + rows] = contract_rows(left[:, at:at + rows], right)
        span = pl.ds(at, rows)
        copies.append(
            pltpu.make_async_copy(tile_ref.at[span], out_ref.at[span], sems.at[len(copies)])
        )
        copies[-1].start()


def gate_grad_kernel(*refs):
    *in_refs, gate_ref, up_grad_ref, rows_ref, up_ref, tile_ref, up_tile_ref, deltas_ref, sems = refs
    row_refs, delta_refs = in_refs[:-6], in_refs[-6:]
    *near_refs, own_ref, far_ref = row_refs
    width = rows_ref.shape[1] // 2
    hidden_units = up_ref.shape[1]

    def gather_rows(cols):
        near = near_rows(*near_refs, cols=cols)
        rows_ref[:, cols] = jnp.concatenate([near, own_ref[:, cols], far_ref[:, cols]], axis=0)

    def columns(place):
        whole = slice(place * hidden_units, (place + 1) * hidden_units)
        return whole, whole, slice(whole.start - hidden_units, whole.stop - hidden_units)

    gather_deltas(deltas_ref, delta_refs, columns(1))
    gather_rows(slice(0, width))
    copies = []
    send_tiles(rows_ref[:, :width], deltas_ref[...], 128, tile_ref, gate_ref, sems, copies)
    gather_deltas(up_ref, delta_refs, columns(2))
    send_tiles(
        rows_ref[:, :width], up_ref[...], 128, up_tile_ref, up_grad_ref, sems, copies, stop=128
    )
    gather_rows(slice(width, 2 * width))
    for copy in copies:
        copy.wait()


def up_down_grad_kernel(started_ref, rows_ref, deltas_ref, *refs):
    *hidden_refs, up_ref, down_ref, up_tile_ref, down_tile_ref, hidden_ref, sems = refs
    width = rows_ref.shape[1] // 2
    hidden_units = hidden_ref.shape[1]
    copies = []
    send_tiles(
        rows_ref[:, :width], deltas_ref[...], 128, up_tile_ref, up_ref, sems, copies, start=128
    )
    gather_deltas(hidden_ref, hidden_refs, (slice(0, hidden_units),) * 3)
    send_tiles(hidden_ref[...], rows_ref[:, width:], 256, down_tile_ref, down_ref, sems, copies)
    for copy in copies:
        copy.wait()


def grads_call(kernel, grads, extra, delta_shape, *args, started=False):
    spaces = [pltpu.HBM] * len(grads) + [pltpu.VMEM] * len(extra)
    copies = sum(-(-grad.shape[0] // 128) for grad in grads)
    in_spaces = [pltpu.HBM if started and place == 0 else pltpu.VMEM for place in range(len(args))]
    return pl.pallas_call(
        kernel,
        out_shape=(*grads, *extra),
        input_output_aliases={0: 0} if started else {},
        in_specs=[pl.BlockSpec(memory_space=space) for space in in_spaces],
        out_specs=tuple(pl.BlockSpec(memory_space=space) for space in spaces),
        scratch_shapes=[pltpu.VMEM(grad.shape, grad.dtype) for grad in grads]
        + [pltpu.VMEM(delta_shape.shape, delta_shape.dtype), pltpu.SemaphoreType.DMA((copies,))],
        compiler_params=pltpu.CompilerParams(vmem_limit_bytes=24 * 1024 * 1024),
        cost_estimate=pl.CostEstimate(flops=10**7, bytes_accessed=10**7, transcendentals=0),
    )(*args)


def token_grad_kernel(chosen_ref, own_ref, from_pair_ref, *refs):
    *group_refs, out_ref = refs
    block = own_ref.shape[0]
    rows = [own_ref[...], from_pair_ref[:block]] + [ref[...] for ref in reversed(group_refs)]
    returned = jnp.concatenate(rows, axis=0)
    out = jnp.dot(chosen_ref[...], returned, preferred_element_type=jnp.float32)
    out_ref[...] = out.astype(jnp.bfloat16)


def body_by_all_to_all(tokens, cotangent, expert_ids, route_weights, gate_weight, up_weight, down_weight):
    owners = lax.axis_size("expert")
    width_parts = lax.axis_size("dp")
    tok_rows, top_count = expert_ids.shape
    width = tokens.shape[1]
    capacity = min(tok_rows, max(2, (tok_rows * top_count + owners - 1) // owners))
    slot_count = owners * capacity
    flat_ids = expert_ids.reshape(-1)
    position = jnp.arange(flat_ids.shape[0], dtype=jnp.int32)
    earlier = (flat_ids[:, None] == flat_ids[None, :]) & (position[None, :] < position[:, None])
    rank_pos = jnp.sum(earlier.astype(jnp.int32), axis=1)
    slot_pos = flat_ids * capacity + rank_pos
    pair_select = (slot_pos[:, None] == jnp.arange(slot_count, dtype=jnp.int32)[None, :]).astype(
        jnp.bfloat16
    )
    chosen = jnp.sum(
        pair_select.reshape(tok_rows, top_count, slot_count).astype(jnp.float32), axis=1
    ).astype(jnp.bfloat16)
    pair_tokens = jnp.repeat(tokens, top_count, axis=0)
    pair_scaled = (
        jnp.repeat(cotangent.astype(jnp.float32), top_count, axis=0) * route_weights
    ).astype(jnp.bfloat16)
    payload = jnp.concatenate([pair_tokens, pair_scaled], axis=1)
    send = contract_rows(pair_select, payload).astype(jnp.bfloat16)
    slots = lax.all_to_all(send, "expert", split_axis=0, concat_axis=0, tiled=True)

    core = lax.axis_index("dp") % 2
    half = slot_count // 2
    mine_slots = lax.dynamic_slice_in_dim(slots, core * half, half, 0)
    other_slots = lax.dynamic_slice_in_dim(slots, (1 - core) * half, half, 0)
    w_gate = gate_weight[0]
    w_up = up_weight[0]
    w_down = down_weight[0]

    def partial_sums(rows):
        feats, cots = rows[:, :width], rows[:, width:]
        return (
            jnp.dot(feats, w_gate, preferred_element_type=jnp.float32),
            jnp.dot(feats, w_up, preferred_element_type=jnp.float32),
            contract_cols(cots, w_down),
        )

    def pack(parts):
        return jnp.stack([part.astype(jnp.bfloat16) for part in parts])

    received = swap(pack(partial_sums(other_slots)), 1)
    sums = jnp.stack(partial_sums(mine_slots)) + received.astype(jnp.float32)
    bit = 2
    while bit < width_parts:
        sums = sums + swap(sums.astype(jnp.bfloat16), bit).astype(jnp.float32)
        bit *= 2
    mine = jnp.stack(local_deltas(sums[0], sums[1], sums[2]))
    other = swap(mine, 1)
    hidden, gate_delta, up_delta = jnp.concatenate([mine, other], axis=1)
    both = jnp.concatenate([mine_slots, other_slots], axis=0)
    slot_grad = (contract_cols(gate_delta, w_gate) + contract_cols(up_delta, w_up)).astype(
        jnp.bfloat16
    )
    slot_grad = jnp.where(
        core == 0, slot_grad, jnp.concatenate([slot_grad[half:], slot_grad[:half]], axis=0)
    )
    returned = lax.all_to_all(slot_grad, "expert", split_axis=0, concat_axis=0, tiled=True)
    feats, cots = both[:, :width], both[:, width:]
    gate_grad = contract_rows(feats, gate_delta)
    up_grad = contract_rows(feats, up_delta)
    down_grad = contract_rows(hidden, cots)
    token_grad = jnp.dot(chosen, returned, preferred_element_type=jnp.float32).astype(jnp.bfloat16)
    return (token_grad, gate_grad[None], up_grad[None], down_grad[None])


def body_by_pairs(tokens, cotangent, expert_ids, route_weights, gate_weight, up_weight, down_weight):
    owners = lax.axis_size("expert")
    width_parts = lax.axis_size("dp")
    tok_rows, _ = expert_ids.shape
    width = tokens.shape[1]
    hidden_units = gate_weight.shape[2]
    capacity = min(tok_rows, max(2, (tok_rows + owners - 1) // owners))
    slot_count = owners * capacity
    half = owners // 2

    far_first = [0] + list(reversed(range(1, half)))
    chosen, own, pair_block, *groups = call(
        functools.partial(dispatch_kernel, owners, capacity),
        (shape(slot_count, tok_rows),)
        + (shape(capacity, 2 * width),) * 2
        + (shape(2 * capacity, 2 * width),) * (half - 1),
        expert_ids.reshape(1, tok_rows),
        route_weights.reshape(1, tok_rows),
        tokens,
        cotangent,
        far=range(4),
        scratch=[
            pltpu.VMEM((1, tok_rows), jnp.int32),
            pltpu.VMEM((1, tok_rows), jnp.float32),
            pltpu.VMEM((tok_rows, width), jnp.bfloat16),
            pltpu.VMEM((tok_rows, width), jnp.bfloat16),
            pltpu.SemaphoreType.DMA((4,)),
        ],
    )
    down, gate, up = call(
        load_kernel,
        (shape(width, hidden_units),) * 3,
        down_weight[0],
        gate_weight[0],
        up_weight[0],
        chosen,
        far=range(3),
        scratch=[
            pltpu.VMEM((hidden_units, width), jnp.bfloat16),
            pltpu.SemaphoreType.DMA((3,)),
        ],
        cost=10**7,
    )
    groups = [swap(groups[j - 1], 2 * j, "expert") for j in far_first[1:]]
    from_pair = swap(pair_block, 1, "expert")
    groups = after(groups, from_pair)
    seconds = jnp.concatenate([group[capacity:] for group in groups], axis=0)
    by_pair = swap(after(seconds, up), 1, "expert")

    near = [from_pair] + groups

    def pieces(*parts):
        shapes = []
        for part in parts:
            shapes += [shape(part, 3 * hidden_units, jnp.float32), shape(part, 3 * hidden_units)]
        return shapes

    def sums_over_cores(rows, cost, *parts):
        mine, other = call(
            products_kernel, pieces(sum(parts)), *rows, gate, up, down, cost=cost
        )
        out = call(sums_kernel, pieces(*parts), mine, swap(other, 1))
        return list(zip(out[::2], out[1::2]))

    def exchanged(sums, marker):
        bit = 2
        while 2 * bit < width_parts:
            sums, marker = call(sums_kernel, pieces(sums.shape[0]), sums, swap(marker, bit))
            bit *= 2
        return sums, swap(marker, bit)

    def deltas_of(sums, received, cost):
        return call(deltas_kernel, shape(*sums.shape), sums, received, cost=cost)

    own_half = capacity // 2
    own_sums, near_sums = sums_over_cores(
        near + [own], 1, own_half, half * capacity // 2
    )
    (far_sums,) = sums_over_cores([by_pair], FAR_PRODUCTS_COST, (half - 1) * capacity // 2)
    near_sums, far_sums = exchanged(*near_sums), exchanged(*far_sums)

    near_mine = deltas_of(*near_sums, 1)
    *turned, chosen = call(
        turn_kernel,
        (shape(hidden_units, width),) * 2 + (shape(tok_rows, slot_count),),
        *after((gate, up, chosen), near_mine),
    )
    own_sums = exchanged(own_sums[0], after(own_sums[1], turned[0]))
    near_deltas = near_mine, swap(near_mine, 1)
    part = far_sums[0].shape[0]
    far_hidden, far_mine = after(
        call(
            deltas_kernel,
            (shape(part, hidden_units), shape(part, 2 * hidden_units)),
            *far_sums,
            cost=FAR_DELTAS_COST,
        ),
        near_deltas[1],
    )
    far_deltas = far_mine, swap(far_mine, 1)
    hidden_pair = far_hidden, swap(far_hidden, 1)
    block = shape(capacity, width)
    grads = call(slot_grad_kernel, (block,) * half, *near_deltas, *turned)
    own_mine = deltas_of(after(own_sums[0], grads[0]), own_sums[1], OWN_DELTAS_COST)
    own_deltas = own_mine, swap(own_mine, 1)
    (own_grad,) = call(slot_grad_kernel, (block,), *own_deltas, *turned)
    to_pair = call(
        far_grad_kernel,
        shape(half * capacity, width),
        *after(far_deltas, own_mine),
        *turned,
        grads[-1],
    )
    returned_pair = swap(to_pair, 1, "expert")
    wide = shape(width, hidden_units, jnp.float32)
    one_delta = shape(slot_count, hidden_units)
    gate_grad, up_started, all_rows, up_deltas = grads_call(
        gate_grad_kernel,
        (wide, wide),
        (shape(slot_count, 2 * width), one_delta),
        one_delta,
        *near,
        own,
        by_pair,
        *near_deltas,
        *own_deltas,
        *far_deltas,
    )
    returned_pair = after(returned_pair, (gate_grad, own_grad))
    returned = {}
    for place, j in enumerate(far_first[1:], 1):
        more = returned_pair[place * capacity:(place + 1) * capacity]
        returned[j] = swap(jnp.concatenate([grads[place - 1], more], axis=0), 2 * j, "expert")
    up_grad, down_grad = grads_call(
        up_down_grad_kernel,
        (wide, shape(hidden_units, width, jnp.float32)),
        (),
        one_delta,
        up_started,
        all_rows,
        up_deltas,
        *near_deltas,
        *own_deltas,
        *hidden_pair,
        started=True,
    )
    token_grad = call(
        token_grad_kernel,
        shape(tok_rows, width),
        chosen,
        own_grad,
        returned_pair,
        *[returned[j] for j in far_first[1:]],
    )
    return (token_grad, gate_grad[None], up_grad[None], down_grad[None])


def body(tokens, cotangent, expert_ids, *rest):
    owners = lax.axis_size("expert")
    width_parts = lax.axis_size("dp")
    tok_rows, top_count = expert_ids.shape
    by_pairs = (
        top_count == 1
        and owners >= 8
        and owners & (owners - 1) == 0
        and width_parts >= 4
        and tok_rows % (16 * owners) == 0
    )
    chosen = body_by_pairs if by_pairs else body_by_all_to_all
    return chosen(tokens, cotangent, expert_ids, *rest)


def solution(mesh):
    return jax.shard_map(
        body,
        mesh=mesh,
        in_specs=(
            P("expert", "dp"),
            P("expert", "dp"),
            P("expert", None),
            P("expert", None),
            P("expert", "dp", None),
            P("expert", "dp", None),
            P("expert", None, "dp"),
        ),
        out_specs=(
            P("expert", "dp"),
            P("expert", "dp", None),
            P("expert", "dp", None),
            P("expert", None, "dp"),
        ),
        check_vma=False,
    )
```
